256 devices in a mesh: sec: 2 (over x_lo), gx: 64 (over y, z, core), gy: 2 (over x_hi).
Axes of the slice: x: 4 (x_hi: 2, x_lo: 2; x = x_hi * 2 + x_lo), y: 4, z: 8, core: 2. Of those that a mesh axis runs over, the one named last changes fastest.
Arguments:
- initial_unknowns: float32 [2, 2, 256, 128, 256], P('sec', None, 'gx', 'gy'), may hold values from -3.5 to 3.5, as said below
- section_coeffs: float32 [2, 4, 256, 128, 256], P('sec', None, 'gx', 'gy'), may hold values from 0.005 to 20, as said below
- rock_type: int32 [256, 128, 256], P('gx', 'gy'), may hold values from 0 to 7
- rock_table: float32 [8, 3], replicated, may hold values from 0.3 to 1
- opening_grid_location: int32 [32768], P(('gx', 'gy')), may hold values from 0 to 65535
- perf_well: int32 [32768], P(('gx', 'gy')), may hold values from -1 to 8191, as said below
- well_index: float32 [32768], P(('gx', 'gy')), may hold values from 0.5 to 5
- perf_pressure: float32 [32768], P(('gx', 'gy')), may hold values from -5 to 5
- well_owner: int32 [8192], replicated, may hold values from 0 to 127, as said below
- well_slot: int32 [8192], replicated, may hold values from 0 to 127, as said below
Outputs:
- closing_unknowns: float32 [2, 2, 256, 128, 256], P('sec', None, 'gx', 'gy')
- well_rates: float32 [2, 2, 16384], P('sec', None, ('gx', 'gy'))
The draws below stay inside these ranges and needn't reach their ends.
Inputs may be any that keep to these rules, and one draw needn't show every extreme that they name: `initial_unknowns`: section 0 holds pressure, then temperature within 0.5 to 1.5; section 1 holds water saturation within 0.1 to 0.5, then gas saturation within 0.05 to 0.3. `section_coeffs`: all positive: permeabilities within 0.005 to 20, accumulation coefficients within 0.3 to 3, conductivities within 0.2 to 2, pore volumes over the time step within 2 to 8, viscosities of water within 0.3 to 1, of oil within 1 to 10, of gas within 0.05 to 0.3. `perf_well`: -1 marks an empty slot; in each block of 256 slots the live ones come first and at least 64 are live; some block has all of them live. `well_owner`: owner blocks are numbered along gx+gy with gx slowest; no owner holds more than 128 wells and some owner holds exactly 128. `well_slot`: no two wells share both owner and slot.
All inputs are finite; a program needn't handle non-finite values.
Results may differ from the reference program's by a relative error of at most 0.00015.
Values sent between devices are 32-bit elements; how exact they have to be, the bound alone decides.
A program may use at most 64 MiB of HBM per device.

```python
import math
import jax
import jax.numpy as jnp

CX = 4
CY = 64
NZ = 256
PERF_DEV = 256
WSLOT = 128
SWEEPS = 2
NROCK = 8
NX = 256
NY = 128
OWNERS = 128
WELLS = 8192
CELLS_DEV = 65536
N_GY = 2


def log_uniform(key, mesh_extents, low_end, high_end):
    return jnp.exp(jax.random.uniform(key, mesh_extents, jnp.float32, math.log(low_end), math.log(high_end)))


def draw_initial_unknowns(key, part):
    key = jax.random.fold_in(key, 11)
    stochastic_seeds = jax.random.split(key, 4)
    mesh_extents = (NX, NY, NZ)
    fluid_head_array = jax.random.truncated_normal(stochastic_seeds[0], -3.5, 3.5, mesh_extents, jnp.float32)
    kelvin_level_array = jax.random.uniform(stochastic_seeds[1], mesh_extents, jnp.float32, 0.6, 1.4)
    aqueous_saturation = jax.random.uniform(stochastic_seeds[2], mesh_extents, jnp.float32, 0.15, 0.45)
    vapour_saturation = jax.random.uniform(stochastic_seeds[3], mesh_extents, jnp.float32, 0.08, 0.25)
    return jnp.stack([jnp.stack([fluid_head_array, kelvin_level_array]), jnp.stack([aqueous_saturation, vapour_saturation])]).astype(jnp.float32)


def draw_section_coeffs(key, part):
    key = jax.random.fold_in(key, 13)
    stochastic_seeds = jax.random.split(key, 8)
    mesh_extents = (NX, NY, NZ)
    lateral_darcy_flux = log_uniform(stochastic_seeds[0], mesh_extents, 0.1, 10.0)
    vertical = log_uniform(stochastic_seeds[1], mesh_extents, 0.01, 1.0)
    storage_summands = log_uniform(stochastic_seeds[2], mesh_extents, 0.3, 3.0)
    thermal_diffusion = log_uniform(stochastic_seeds[3], mesh_extents, 0.2, 2.0)
    pore_volume = log_uniform(stochastic_seeds[4], mesh_extents, 2.0, 8.0)
    visc_water = log_uniform(stochastic_seeds[5], mesh_extents, 0.3, 1.0)
    crude_dynamic_stickiness = log_uniform(stochastic_seeds[6], mesh_extents, 1.0, 10.0)
    vapour_viscosity = log_uniform(stochastic_seeds[7], mesh_extents, 0.05, 0.3)
    first_half = jnp.stack([lateral_darcy_flux, vertical, storage_summands, thermal_diffusion])
    second_half = jnp.stack([pore_volume, visc_water, crude_dynamic_stickiness, vapour_viscosity])
    return jnp.stack([first_half, second_half]).astype(jnp.float32)


def draw_perf_well(key, part):
    key = jax.random.fold_in(key, 23)
    count_key, full_key, ident_key = jax.random.split(key, 3)
    counts = jax.random.randint(count_key, (OWNERS, 1), PERF_DEV // 4, PERF_DEV + 1)
    full_block = jax.random.randint(full_key, (), 0, OWNERS)
    block_ids = jnp.arange(OWNERS, dtype=jnp.int32)[:, None]
    counts = jnp.where(block_ids == full_block, PERF_DEV, counts)
    position = jnp.arange(PERF_DEV, dtype=jnp.int32)[None, :]
    live_slot = position < counts
    idents = jax.random.randint(ident_key, (OWNERS, PERF_DEV), 0, WELLS)
    idents = jnp.where((block_ids == full_block) & (position == 0), WELLS - 1, idents)
    return jnp.where(live_slot, idents, -1).reshape(-1).astype(jnp.int32)


def well_layout(key):
    key = jax.random.fold_in(key, 41)
    full_key, pick_key, order_key = jax.random.split(key, 3)
    full_owner = jax.random.randint(full_key, (), 0, OWNERS)
    picked = jax.random.permutation(pick_key, (OWNERS - 1) * WSLOT)[:WELLS - WSLOT]
    other_owner = picked // WSLOT
    other_owner = other_owner + (other_owner >= full_owner).astype(jnp.int32)
    owners_all = jnp.concatenate([jnp.full((WSLOT,), full_owner, jnp.int32), other_owner.astype(jnp.int32)])
    slots_all = jnp.concatenate([jnp.arange(WSLOT, dtype=jnp.int32), (picked % WSLOT).astype(jnp.int32)])
    order = jax.random.permutation(order_key, WELLS)
    return (owners_all[order].astype(jnp.int32), slots_all[order].astype(jnp.int32))


def draw_well_owner(key, part):
    shared = well_layout(key)
    return shared[0]


def draw_well_slot(key, part):
    shared = well_layout(key)
    return shared[1]


def touch_ends(result, rng, smallest, largest):
    spot = [jax.random.randint(jax.random.fold_in(rng, axis), (), 0, length) for axis, length in enumerate(result.shape)]
    widest = result.shape.index(max(result.shape))
    beside = spot[:widest] + [(spot[widest] + 1) % result.shape[widest]] + spot[widest + 1:]
    return result.at[tuple(spot)].set(smallest).at[tuple(beside)].set(largest)


def shard_levels(stream_key, dims, shards, low, largest):
    loudness = 1.0
    for dim, shards_of in shards:
        heights = jax.random.uniform(jax.random.fold_in(jax.random.fold_in(stream_key, 6), dim), (shards_of,), jnp.float32, low / len(shards), largest / len(shards))
        loudness = loudness * jnp.repeat(jnp.exp(heights), dims[dim] // shards_of).reshape((-1,) + (1,) * (len(dims) - 1 - dim))
    return loudness


def scatter_about(stream_key, dims, deviation, limit, shards=(), held_as=jnp.bfloat16):
    entries = deviation * jax.random.normal(stream_key, dims, jnp.float32)
    if shards:
        entries = entries * shard_levels(stream_key, dims, shards, -0.22, 0.18)
    return jnp.clip(entries, -limit, limit).astype(held_as)


def setup_inputs(seed: int = 0) -> dict:
    key_of = jax.random.split(jax.random.key(seed), 11)
    initial_unknowns = draw_initial_unknowns(jax.random.fold_in(key_of[10], 71), 0)
    section_coeffs = draw_section_coeffs(jax.random.fold_in(key_of[10], 71), 0)
    rock_type = touch_ends(jax.random.randint(key_of[2], (NX, NY, NZ), 0, NROCK), jax.random.fold_in(key_of[2], 1), 0, NROCK - 1).astype(jnp.int32)
    rock_table = jnp.clip(jnp.exp(jax.random.uniform(key_of[3], (NROCK, 3), jnp.float32, math.log(0.3), math.log(1.0))), 0.3, 1.0)
    opening_grid_location = touch_ends(jax.random.randint(key_of[4], (OWNERS * PERF_DEV,), 0, CELLS_DEV), jax.random.fold_in(key_of[4], 1), 0, CELLS_DEV - 1).astype(jnp.int32)
    perf_well = draw_perf_well(jax.random.fold_in(key_of[10], 71), 0)
    well_index = jnp.clip(jnp.exp(math.log(5.0) - 2.3025851 * jax.random.uniform(key_of[6], (OWNERS * PERF_DEV,), jnp.float32) ** shard_levels(key_of[6], (OWNERS * PERF_DEV,), ((0, 128),), -0.2, 0.2)), 0.5, 5.0)
    perf_pressure = scatter_about(key_of[7], (OWNERS * PERF_DEV,), 1.5, 5.0, ((0, 128),), jnp.float32)
    well_owner = draw_well_owner(jax.random.fold_in(key_of[10], 71), 0)
    well_slot = draw_well_slot(jax.random.fold_in(key_of[10], 71), 0)
    return dict(initial_unknowns=initial_unknowns, section_coeffs=section_coeffs, rock_type=rock_type, rock_table=rock_table, opening_grid_location=opening_grid_location, perf_well=perf_well, well_index=well_index, perf_pressure=perf_pressure, well_owner=well_owner, well_slot=well_slot)


THERMAL_LINKED = 1.5


def harmonic(lower_value, upper_value):
    return 2.0 * lower_value * upper_value / (lower_value + upper_value)


def halo_layer_slab(grid_array):
    return jnp.pad(grid_array, ((1, 1), (1, 1), (0, 0)))


def relaxation_sweep_pass(current, lateral_darcy_flux, base, storage_summands, vertical, well_diag, well_rhs):
    east_face = harmonic(lateral_darcy_flux[1:, 1:-1], lateral_darcy_flux[:-1, 1:-1])
    north_face = harmonic(lateral_darcy_flux[1:-1, 1:], lateral_darcy_flux[1:-1, :-1])
    upper_face = harmonic(vertical[:, :, 1:], vertical[:, :, :-1])
    flat_zero = jnp.zeros_like(upper_face[:, :, :1])
    upward = jnp.concatenate([upper_face, flat_zero], axis=2)
    downward = jnp.concatenate([flat_zero, upper_face], axis=2)
    centre = current[1:-1, 1:-1]
    below_cell = jnp.concatenate([flat_zero, centre[:, :, :-1]], axis=2)
    above_cell = jnp.concatenate([centre[:, :, 1:], flat_zero], axis=2)
    neighbour_sum = (east_face[:-1] * current[:-2, 1:-1] + east_face[1:] * current[2:, 1:-1]
                     + north_face[:, :-1] * current[1:-1, :-2] + north_face[:, 1:] * current[1:-1, 2:]
                     + downward * below_cell + upward * above_cell)
    coupling = east_face[:-1] + east_face[1:] + north_face[:, :-1] + north_face[:, 1:] + downward + upward
    numerator = storage_summands * base + well_rhs + neighbour_sum
    denominator = storage_summands + well_diag + coupling
    return numerator / denominator


def face_fluxes(pressure_rim, horizontal_rim, vertical):
    east_face = harmonic(horizontal_rim[1:, 1:-1], horizontal_rim[:-1, 1:-1])
    flow_x = east_face * (pressure_rim[:-1, 1:-1] - pressure_rim[1:, 1:-1])
    north_face = harmonic(horizontal_rim[1:-1, 1:], horizontal_rim[1:-1, :-1])
    flow_y = north_face * (pressure_rim[1:-1, :-1] - pressure_rim[1:-1, 1:])
    upper_face = harmonic(vertical[:, :, 1:], vertical[:, :, :-1])
    centre = pressure_rim[1:-1, 1:-1]
    flow_z = upper_face * (centre[:, :, :-1] - centre[:, :, 1:])
    upward = jnp.concatenate([flow_z, jnp.zeros_like(flow_z[:, :, :1])], axis=2)
    return flow_x[:-1], flow_x[1:], flow_y[:, :-1], flow_y[:, 1:], upward


def upwind_net(share_rim, flows):
    west_flow, east_flow, south_flow, north_flow, upward = flows
    centre = share_rim[1:-1, 1:-1]
    flat_zero = jnp.zeros_like(centre[:, :, :1])
    below_cell = jnp.concatenate([flat_zero, centre[:, :, :-1]], axis=2)
    above_cell = jnp.concatenate([centre[:, :, 1:], flat_zero], axis=2)
    downward = jnp.concatenate([flat_zero, upward[:, :, :-1]], axis=2)
    in_west = jnp.maximum(west_flow, 0.0) * share_rim[:-2, 1:-1] + jnp.minimum(west_flow, 0.0) * centre
    out_east = jnp.maximum(east_flow, 0.0) * centre + jnp.minimum(east_flow, 0.0) * share_rim[2:, 1:-1]
    in_south = jnp.maximum(south_flow, 0.0) * share_rim[1:-1, :-2] + jnp.minimum(south_flow, 0.0) * centre
    out_north = jnp.maximum(north_flow, 0.0) * centre + jnp.minimum(north_flow, 0.0) * share_rim[1:-1, 2:]
    in_down = jnp.maximum(downward, 0.0) * below_cell + jnp.minimum(downward, 0.0) * centre
    out_up = jnp.maximum(upward, 0.0) * centre + jnp.minimum(upward, 0.0) * above_cell
    return in_west - out_east + in_south - out_north + in_down - out_up


def reference(initial_unknowns, section_coeffs, rock_type, rock_table, opening_grid_location, perf_well, well_index, perf_pressure, well_owner, well_slot):
    fluid_head_before = initial_unknowns[0, 0]
    kelvin_level_before = initial_unknowns[0, 1]
    aqueous_saturation = initial_unknowns[1, 0]
    vapour_saturation = initial_unknowns[1, 1]
    lateral_darcy_flux = section_coeffs[0, 0]
    vertical = section_coeffs[0, 1]
    storage_summands = section_coeffs[0, 2]
    thermal_diffusion = section_coeffs[0, 3]
    pore_volume = section_coeffs[1, 0]
    visc_water = section_coeffs[1, 1]
    crude_dynamic_stickiness = section_coeffs[1, 2]
    vapour_viscosity = section_coeffs[1, 3]

    live_slot = perf_well >= 0
    well_id = jnp.maximum(perf_well, 0).astype(jnp.int32)
    borehole_opening_partition = jnp.arange(OWNERS * PERF_DEV, dtype=jnp.int32) // PERF_DEV
    partition_line = borehole_opening_partition // N_GY
    block_col = borehole_opening_partition % N_GY
    local_row = opening_grid_location // (CY * NZ)
    local_col = (opening_grid_location // NZ) % CY
    local_depth = opening_grid_location % NZ
    domain_node_number = (((partition_line * CX + local_row) * NY + block_col * CY + local_col) * NZ + local_depth).astype(jnp.int32)
    total_cells = NX * NY * NZ

    live_index = jnp.where(live_slot, well_index, 0.0)
    well_diag = jnp.zeros((total_cells,), jnp.float32).at[domain_node_number].add(live_index).reshape(NX, NY, NZ)
    well_rhs = jnp.zeros((total_cells,), jnp.float32).at[domain_node_number].add(live_index * perf_pressure).reshape(NX, NY, NZ)

    present_pressure_height = fluid_head_before
    present_absolute_warmth = kelvin_level_before
    for sweep_index in range(SWEEPS):
        pressure_next = relaxation_sweep_pass(halo_layer_slab(present_pressure_height), halo_layer_slab(lateral_darcy_flux), fluid_head_before, storage_summands, vertical, well_diag, well_rhs)
        present_absolute_warmth = relaxation_sweep_pass(halo_layer_slab(present_absolute_warmth), halo_layer_slab(thermal_diffusion), kelvin_level_before, storage_summands, thermal_diffusion, 0.0, 0.0)
        present_pressure_height = pressure_next

    flows = face_fluxes(halo_layer_slab(present_pressure_height), halo_layer_slab(lateral_darcy_flux), vertical)

    rocktype_property_fetch = rock_table[rock_type]
    crude_saturation = 1.0 - aqueous_saturation - vapour_saturation
    water_mobility = rocktype_property_fetch[..., 0] * aqueous_saturation * aqueous_saturation / visc_water
    crude_relative_transport = rocktype_property_fetch[..., 1] * crude_saturation * crude_saturation * jnp.exp(THERMAL_LINKED * (present_absolute_warmth - 1.0)) / crude_dynamic_stickiness
    gas_mobility = rocktype_property_fetch[..., 2] * vapour_saturation * vapour_saturation / vapour_viscosity
    total_mobility = water_mobility + crude_relative_transport + gas_mobility
    water_share = water_mobility / total_mobility
    gas_share = gas_mobility / total_mobility

    at_cell = present_pressure_height.reshape(-1)[domain_node_number]
    opening_inflow_rate = jnp.where(live_slot, well_index * (perf_pressure - at_cell), 0.0)
    cell_rate = jnp.zeros((total_cells,), jnp.float32).at[domain_node_number].add(opening_inflow_rate).reshape(NX, NY, NZ)

    aqueous_saturation_new = aqueous_saturation + (upwind_net(halo_layer_slab(water_share), flows) + cell_rate * water_share) / pore_volume
    vapour_saturation_new = vapour_saturation + (upwind_net(halo_layer_slab(gas_share), flows) + cell_rate * gas_share) / pore_volume

    haloed_location = (well_owner[well_id] * WSLOT + well_slot[well_id]).astype(jnp.int32)
    element_number = OWNERS * WSLOT
    total_rate = jax.ops.segment_sum(opening_inflow_rate, haloed_location, num_segments=element_number)
    injected_heat_amount = jax.ops.segment_sum(opening_inflow_rate * present_absolute_warmth.reshape(-1)[domain_node_number], haloed_location, num_segments=element_number)
    water_rate = jax.ops.segment_sum(opening_inflow_rate * water_share.reshape(-1)[domain_node_number], haloed_location, num_segments=element_number)
    gas_rate = jax.ops.segment_sum(opening_inflow_rate * gas_share.reshape(-1)[domain_node_number], haloed_location, num_segments=element_number)

    closing_unknowns = jnp.stack([jnp.stack([present_pressure_height, present_absolute_warmth]), jnp.stack([aqueous_saturation_new, vapour_saturation_new])])
    well_rates = jnp.stack([jnp.stack([total_rate, injected_heat_amount]), jnp.stack([water_rate, gas_rate])])
    return (closing_unknowns, well_rates)
```

```python
import functools

import jax
import jax.numpy as jnp
from jax import lax
from jax.experimental import pallas as pl
from jax.experimental.pallas import tpu as pltpu
from jax.sharding import PartitionSpec as P

MESH = pl.DeviceIdType.MESH
F32 = jnp.float32
BF16 = jnp.bfloat16
CX, CY, NZ = 4, 64, 256
PERFS = 256
NROCK = 8
RING = 64
RUN = 16
PAIRS = 8
LINKED = 1.5

LO, HI = 8, 8 + CY
BODY = pl.ds(LO, CY)

X_UP, X_DOWN = 0, 3
Y_START = 6
KH_OVER, KV_OVER = 7, 8
X2_UP, X2_DOWN, Y_SECOND = 9, 10, 11
FIELD_OVER = 12
AT_OVER = 16
K_UP, K_DOWN, K_Y = 17, 18, 19
S_UP, S_DOWN, S_Y = 20, 21, 22
P_UP, P_DOWN = 23, 24
R_FIRST = 25
R_SECOND = 41
N_SEM = 49
N_LOCAL = 16


def reciprocal(x):
    r = pl.reciprocal(x, approx=True)
    return r * (2.0 - x * r)


def harmonic(a, b):
    return (2.0 * a) * (b * reciprocal(a + b))


def split(x):
    high = x.astype(BF16)
    rest = x - high.astype(F32)
    mid = rest.astype(BF16)
    low = (rest - mid.astype(F32)).astype(BF16)
    return high, mid, low


def dot_nt(a, b):
    return lax.dot_general(a, b, (((1,), (1,)), ((), ())), preferred_element_type=F32)


def dot_nn(a, b):
    return lax.dot_general(a, b, (((1,), (0,)), ((), ())), preferred_element_type=F32)


def hot(index, rows):
    return lax.broadcasted_iota(jnp.int32, (rows, PERFS), 0) == index


def as_bf16(mask):
    return jnp.where(mask, 1.0, 0.0).astype(BF16)


def spread(row_hot, col_mask, value):
    total = None
    for piece in split(value):
        term = dot_nt(row_hot, jnp.where(col_mask, piece.astype(F32), 0.0).astype(BF16))
        total = term if total is None else total + term
    return total


def pick(field, row_mask, col_hot):
    total = None
    for piece in split(field):
        term = dot_nn(piece, col_hot)
        total = term if total is None else total + term
    return jnp.sum(jnp.where(row_mask, total, 0.0), axis=0, keepdims=True)


def body(
    unk, coe, rock, table, loc, pw, wi, pp, own, slo,
    out, rates,
    F0, F1, F2, T0, SH, KVC, WG, VM, RK, TX, TY, TZ, INV, BASE, WD, MOB,
    s_loc, s_pw, s_wi, s_pp, s_own, s_slo,
    ys0, yr0, ys1, yr1, ys2, yr2, ys3, yr3, ats, atr,
    part, got1, part2, got2, rate_buf,
    send, recv, lsem,
):
    sec, gx, gy = (lax.axis_index(a) for a in ("sec", "gx", "gy"))
    up = (sec, lax.rem(gx + 1, RING), gy)
    down = (sec, lax.rem(gx + RING - 1, RING), gy)
    side = (sec, gx, 1 - gy)
    other = (1 - sec, gx, gy)
    zc, y = lax.rem(gx, RUN), gx // RUN
    pair = y * 2 + gy
    first = [(sec, y * RUN + lax.rem(zc + d, RUN), gy) for d in range(1, RUN)]
    second = []
    for d in range(1, PAIRS):
        q = lax.rem(pair + d, PAIRS)
        second.append((sec, (q // 2) * RUN + zc, lax.rem(q, 2)))

    barrier = pltpu.get_barrier_semaphore()
    partners = [up, down, side, other] + first + second
    for dev in partners:
        pl.semaphore_signal(barrier, inc=1, device_id=dev, device_id_type=MESH)

    def local(i, src, dst):
        return pltpu.make_async_copy(src, dst, lsem.at[i])

    def remote(i, src, dst, dev):
        return pltpu.make_async_remote_copy(
            src_ref=src,
            dst_ref=dst,
            send_sem=send.at[i],
            recv_sem=recv.at[i],
            device_id=dev,
            device_id_type=MESH,
        )

    small = [
        local(0, loc, s_loc),
        local(1, pw, s_pw),
        local(2, wi, s_wi),
        local(3, pp, s_pp),
        local(4, own, s_own),
        local(5, slo, s_slo),
    ]
    for c in small:
        c.start()
    loads0 = [
        local(6, unk.at[0], F0.at[:, pl.ds(1, CX), BODY, :]),
        local(7, coe.at[0, 0], T0.at[0, pl.ds(1, CX), BODY, :]),
        local(8, coe.at[0, 3], T0.at[1, pl.ds(1, CX), BODY, :]),
        local(9, coe.at[0, pl.ds(1, 2)], KVC),
    ]
    loads1 = [local(6, unk.at[0], WG), local(7, coe.at[0], VM), local(8, rock, RK)]

    def wells():
        for c in small:
            c.wait()
        place = s_loc[...]
        row, col = lax.shift_right_logical(place, 8), jnp.bitwise_and(place, 255)
        row_mask, col_mask = hot(row, PERFS), hot(col, PERFS)
        row_hot, col_hot = as_bf16(row_mask), as_bf16(col_mask)
        live = s_pw[...] >= 0
        index = jnp.where(live, s_wi[...], 0.0)
        WD[0] = spread(row_hot, col_mask, index)
        WD[1] = spread(row_hot, col_mask, index * s_pp[...])
        well = jnp.maximum(s_pw[...], 0)
        w_row = hot(lax.shift_right_logical(well, 7), 64)
        w_col = as_bf16(hot(jnp.bitwise_and(well, 127), 128))

        def look(ref):
            found = dot_nn(ref[...].astype(F32).astype(BF16), w_col)
            return jnp.sum(jnp.where(w_row, found, 0.0), axis=0, keepdims=True).astype(jnp.int32)

        owner, slot = look(s_own), look(s_slo)
        o_gx, o_gy = lax.shift_right_logical(owner, 1), jnp.bitwise_and(owner, 1)
        order = (
            jnp.bitwise_and(o_gx, RUN - 1) * PAIRS + lax.shift_right_logical(o_gx, 4) * 2 + o_gy
        )
        return row_mask, col_hot, index, order, slot

    def rates_first(values, order, slot):
        own_mask, slot_hot = hot(order, RUN * PAIRS), as_bf16(hot(slot, 128))
        for a, value in enumerate(values):
            total = None
            for piece in split(value):
                lhs = jnp.where(own_mask, piece.astype(F32), 0.0).astype(BF16)
                term = dot_nt(lhs, slot_hot)
                total = term if total is None else total + term
            part[:, a] = total.reshape(RUN, PAIRS, 128)
        copies = [
            remote(R_FIRST + d, part.at[lax.rem(zc + d, RUN)], got1.at[d], first[d - 1])
            for d in far_first(RUN)
        ]
        for c in copies:
            c.start()
        return copies

    def rates_second(copies):
        for c in copies:
            c.wait()
        total = part[zc]
        for d in range(1, RUN):
            total = total + got1[d]
        part2[...] = jnp.zeros_like(part2)
        for a in range(2):
            for q in range(PAIRS):
                part2[q, a : a + 1] = total[a, q : q + 1]
        copies = [
            remote(R_SECOND + d, part2.at[lax.rem(pair + d, PAIRS)], got2.at[d], second[d - 1])
            for d in range(1, PAIRS)
        ]
        for c in copies:
            c.start()
        return copies

    def rates_last(copies):
        for c in copies:
            c.wait()
        total = part2[pair]
        for d in range(1, PAIRS):
            total = total + got2[d]
        rate_buf[...] = total[0:2]
        c = local(10, rate_buf, rates.at[0])
        c.start()
        return c

    def edge(ref, f, i):
        return jnp.where(gy == 0, ref[f, i, HI - 1 : HI, :], ref[f, i, LO : LO + 1, :])

    def set_edges(ref, f, i, row, zero):
        if zero:
            ref[f, i, HI : HI + 1, :] = jnp.where(gy == 0, row, 0.0)
            ref[f, i, LO - 1 : LO, :] = jnp.where(gy == 1, row, 0.0)
        else:
            ref[f, i, HI : HI + 1, :] = row
            ref[f, i, LO - 1 : LO, :] = row

    def x_face(f, a):
        face = harmonic(T0[f, a, BODY, :], T0[f, a + 1, BODY, :])
        if a == 0:
            face = jnp.where(gx == 0, 0.0, face)
        if a == CX:
            face = jnp.where(gx == RING - 1, 0.0, face)
        TX[f, a] = face

    def y_faces(f, i):
        TY[f, i - 1, LO : HI - 1] = harmonic(T0[f, i, LO : HI - 1, :], T0[f, i, LO + 1 : HI, :])

    def y_ends(f, i):
        for r in (LO - 1, HI - 1):
            TY[f, i - 1, r : r + 1] = harmonic(T0[f, i, r : r + 1, :], T0[f, i, r + 1 : r + 2, :])

    def z_faces(f, i, value):
        lane = lax.broadcasted_iota(jnp.int32, (CY, NZ), 1)
        face = harmonic(value, pltpu.roll(value, NZ - 1, 1))
        TZ[f, i - 1] = jnp.where(lane == NZ - 1, 0.0, face)

    def system(f, i, start):
        c = KVC[1, i - 1]
        tz = TZ[f, i - 1]
        total = (
            c + TX[f, i - 1] + TX[f, i] + TY[f, i - 1, LO - 1 : HI - 1] + TY[f, i - 1, LO:HI]
            + tz + pltpu.roll(tz, 1, 1)
        )
        base = c * start[f, i, BODY, :]
        if f == 0:
            rows = slice((i - 1) * CY, i * CY)
            total = total + WD[0, rows]
            base = base + WD[1, rows]
        INV[f, i - 1] = reciprocal(total)
        BASE[f, i - 1] = base

    def sweep(f, i, now, later):
        tz = TZ[f, i - 1]
        centre = now[f, i, BODY, :]
        total = (
            BASE[f, i - 1]
            + TX[f, i - 1] * now[f, i - 1, BODY, :]
            + TX[f, i] * now[f, i + 1, BODY, :]
            + TY[f, i - 1, LO - 1 : HI - 1] * now[f, i, LO - 1 : HI - 1, :]
            + TY[f, i - 1, LO:HI] * now[f, i, LO + 1 : HI + 1, :]
            + tz * pltpu.roll(centre, NZ - 1, 1)
            + pltpu.roll(tz * centre, 1, 1)
        )
        later[f, i, BODY, :] = total * INV[f, i - 1]

    def far_first(n):
        return sorted(range(1, n), key=lambda d: -min(d, n - d))

    def x_pair(i_up, i_down, ref, both=True, f=0):
        pick_ = (lambda a: ref.at[:, a, BODY, :]) if both else (lambda a: ref.at[f, a, BODY, :])
        return [
            remote(i_up, pick_(CX), pick_(0), up),
            remote(i_down, pick_(1), pick_(CX + 1), down),
        ]

    over = [
        remote(KH_OVER, coe.at[0, 0], T0.at[0, pl.ds(1, CX), BODY, :], other),
        remote(KV_OVER, coe.at[0, 1], KVC.at[0], other),
    ]
    fields_over = [
        remote(FIELD_OVER + i - 1, F2.at[:, i, BODY, :], F2.at[:, i, BODY, :], other)
        for i in range(1, CX + 1)
    ]
    at_over = remote(AT_OVER, ats, atr, other)
    layers = range(1, CX + 1)

    @pl.when(sec == 0)
    def _():
        for c in loads0:
            c.start()
        pl.semaphore_wait(barrier, len(partners))
        halo_x = []
        for s, dev, src, dst in ((X_UP, up, CX - 1, 0), (X_DOWN, down, 0, CX + 1)):
            halo_x += [
                remote(s, unk.at[0, :, src], F0.at[:, dst, BODY, :], dev),
                remote(s + 1, coe.at[0, 0, src], T0.at[0, dst, BODY, :], dev),
                remote(s + 2, coe.at[0, 3, src], T0.at[1, dst, BODY, :], dev),
            ]
        for c in halo_x:
            c.start()
        for c in loads0:
            c.wait()
        for f in range(2):
            for i in layers:
                r = f * CX + i - 1
                ys0[r : r + 1] = edge(F0, f, i)
                ys0[r + 8 : r + 9] = edge(T0, f, i)
        halo_y = remote(Y_START, ys0, yr0, side)
        halo_y.start()
        for c in over:
            c.start()
        for f in range(2):
            for i in layers:
                z_faces(f, i, KVC[0, i - 1] if f == 0 else T0[1, i, BODY, :])
                y_faces(f, i)
            for a in range(1, CX):
                x_face(f, a)
        row_mask, col_hot, index, order, slot = wells()
        halo_y.wait()
        for f in range(2):
            for i in layers:
                r = f * CX + i - 1
                set_edges(F0, f, i, yr0[r : r + 1], False)
                set_edges(T0, f, i, yr0[r + 8 : r + 9], True)
                y_ends(f, i)
            for i in (2, 3):
                system(f, i, F0)
                sweep(f, i, F0, F1)
        for c in halo_x:
            c.wait()
        for f in range(2):
            for a in (0, CX):
                x_face(f, a)
            for i in (1, CX):
                system(f, i, F0)
                sweep(f, i, F0, F1)
        halo_x = x_pair(X2_UP, X2_DOWN, F1)
        for c in halo_x:
            c.start()
        for f in range(2):
            for i in layers:
                r = f * CX + i - 1
                ys1[r : r + 1] = edge(F1, f, i)
        halo_y = remote(Y_SECOND, ys1, yr1, side)
        halo_y.start()
        halo_y.wait()
        for f in range(2):
            for i in layers:
                r = f * CX + i - 1
                set_edges(F1, f, i, yr1[r : r + 1], False)
        for i in (2, 3):
            for f in range(2):
                sweep(f, i, F1, F2)
            fields_over[i - 1].start()
        for c in halo_x:
            c.wait()
        for i in (1, CX):
            for f in range(2):
                sweep(f, i, F1, F2)
            fields_over[i - 1].start()
        save = local(11, F2.at[:, pl.ds(1, CX), BODY, :], out.at[0])
        save.start()
        pressure = pick(F2[0, 1 : CX + 1, BODY, :].reshape(CX * CY, NZ), row_mask, col_hot)
        warmth = pick(F2[1, 1 : CX + 1, BODY, :].reshape(CX * CY, NZ), row_mask, col_hot)
        ats[...] = jnp.zeros_like(ats)
        ats[0:1] = pressure
        ats[1:2] = warmth
        at_over.start()
        q = index * (s_pp[...] - pressure)
        copies = rates_first((q, q * warmth), order, slot)
        copies = rates_second(copies)
        last = rates_last(copies)
        for c in over + fields_over + [at_over]:
            c.wait_send()
        save.wait()
        last.wait()

    @pl.when(sec == 1)
    def _():
        for c in loads1:
            c.start()
        pl.semaphore_wait(barrier, len(partners))
        for c in loads1:
            c.wait()
        for i in range(CX):
            kind = RK[i]
            ends = []
            masks = [kind == t for t in range(1, NROCK)]
            for k in range(3):
                e = jnp.full((CY, NZ), table[0, k], F32)
                for t in range(1, NROCK):
                    e = jnp.where(masks[t - 1], table[t, k], e)
                ends.append(e)
            water, gas = WG[0, i], WG[1, i]
            oil = 1.0 - water - gas
            MOB[0, i] = ends[0] * water * water * reciprocal(VM[1, i])
            MOB[1, i] = ends[1] * oil * oil * reciprocal(VM[2, i])
            MOB[2, i] = ends[2] * gas * gas * reciprocal(VM[3, i])
        row_mask, col_hot, index, order, slot = wells()
        lw, lo, lg = (pick(MOB[k].reshape(CX * CY, NZ), row_mask, col_hot) for k in range(3))

        over[0].wait_recv()
        halo_k = x_pair(K_UP, K_DOWN, T0, False)
        for c in halo_k:
            c.start()
        ys2[...] = jnp.zeros_like(ys2)
        for i in layers:
            ys2[i - 1 : i] = edge(T0, 0, i)
        halo_ky = remote(K_Y, ys2, yr2, side)
        halo_ky.start()
        for i in layers:
            y_faces(0, i)
        for a in range(1, CX):
            x_face(0, a)
        over[1].wait_recv()
        for i in layers:
            z_faces(0, i, KVC[0, i - 1])
        for c in halo_k:
            c.wait()
        for a in (0, CX):
            x_face(0, a)
        halo_ky.wait()
        for i in layers:
            set_edges(T0, 0, i, yr2[i - 1 : i], True)
            y_ends(0, i)

        for i in (2, 3, 1, 4):
            fields_over[i - 1].wait_recv()
            other_mob = MOB[1, i - 1] * jnp.exp(LINKED * (F2[1, i, BODY, :] - 1.0))
            part_all = reciprocal(MOB[0, i - 1] + other_mob + MOB[2, i - 1])
            SH[0, i, BODY, :] = MOB[0, i - 1] * part_all
            SH[1, i, BODY, :] = MOB[2, i - 1] * part_all
        halo_s = x_pair(S_UP, S_DOWN, SH) + x_pair(P_UP, P_DOWN, F2, False)
        for c in halo_s:
            c.start()
        ys3[...] = jnp.zeros_like(ys3)
        for i in layers:
            ys3[i - 1 : i] = edge(F2, 0, i)
            ys3[i + 3 : i + 4] = edge(SH, 0, i)
            ys3[i + 7 : i + 8] = edge(SH, 1, i)
        halo_sy = remote(S_Y, ys3, yr3, side)
        halo_sy.start()

        at_over.wait_recv()
        q = index * (s_pp[...] - atr[0:1])
        lo = lo * jnp.exp(LINKED * (atr[1:2] - 1.0))
        scaled = q * reciprocal(lw + lo + lg)
        copies = rates_first((scaled * lw, scaled * lg), order, slot)

        halo_sy.wait()
        for i in layers:
            set_edges(F2, 0, i, yr3[i - 1 : i], False)
            set_edges(SH, 0, i, yr3[i + 3 : i + 4], False)
            set_edges(SH, 1, i, yr3[i + 7 : i + 8], False)
        for c in halo_s:
            c.wait()

        def through(flow, shares):
            pos, neg = jnp.maximum(flow, 0.0), jnp.minimum(flow, 0.0)
            return [pos * a + neg * b for a, b in shares]

        for i in layers:
            p = F2[0, i, BODY, :]
            s = [SH[a, i, BODY, :] for a in range(2)]
            tz = TZ[0, i - 1]
            west = through(
                TX[0, i - 1] * (F2[0, i - 1, BODY, :] - p),
                [(SH[a, i - 1, BODY, :], s[a]) for a in range(2)],
            )
            east = through(
                TX[0, i] * (p - F2[0, i + 1, BODY, :]),
                [(s[a], SH[a, i + 1, BODY, :]) for a in range(2)],
            )
            south = through(
                TY[0, i - 1, LO - 1 : HI - 1] * (F2[0, i, LO - 1 : HI - 1, :] - p),
                [(SH[a, i, LO - 1 : HI - 1, :], s[a]) for a in range(2)],
            )
            north = through(
                TY[0, i - 1, LO:HI] * (p - F2[0, i, LO + 1 : HI + 1, :]),
                [(s[a], SH[a, i, LO + 1 : HI + 1, :]) for a in range(2)],
            )
            top = through(
                tz * (p - pltpu.roll(p, NZ - 1, 1)),
                [(s[a], pltpu.roll(s[a], NZ - 1, 1)) for a in range(2)],
            )
            rows = slice((i - 1) * CY, i * CY)
            rate = WD[1, rows] - WD[0, rows] * p
            inverse = reciprocal(VM[0, i - 1])
            for a in range(2):
                net = west[a] - east[a] + south[a] - north[a] + pltpu.roll(top[a], 1, 1) - top[a]
                WG[a, i - 1] = WG[a, i - 1] + (net + rate * s[a]) * inverse
        save = local(11, WG, out.at[0])
        save.start()
        copies = rates_second(copies)
        last = rates_last(copies)
        save.wait()
        last.wait()


def per_device(unk, coe, rock, table, loc, pw, wi, pp, own, slo):
    any_ = pl.BlockSpec(memory_space=pl.ANY)
    row = lambda a: a.reshape(1, PERFS)
    vm = lambda *s: pltpu.VMEM(s, F32)
    halo = (2, CX + 2, CY + 16, NZ)
    return pl.pallas_call(
        body,
        out_shape=(
            jax.ShapeDtypeStruct((1, 2, CX, CY, NZ), F32),
            jax.ShapeDtypeStruct((1, 2, 128), F32),
        ),
        in_specs=[any_] * 3 + [pl.BlockSpec(memory_space=pltpu.SMEM)] + [any_] * 6,
        out_specs=(any_, any_),
        scratch_shapes=[
            vm(*halo), vm(*halo), vm(*halo), vm(*halo), vm(*halo),
            vm(2, CX, CY, NZ),
            vm(2, CX, CY, NZ),
            vm(4, CX, CY, NZ),
            pltpu.VMEM((CX, CY, NZ), jnp.int32),
            vm(2, CX + 1, CY, NZ), vm(2, CX, CY + 16, NZ), vm(2, CX, CY, NZ),
            vm(2, CX, CY, NZ), vm(2, CX, CY, NZ),
            vm(2, CX * CY, NZ),
            vm(3, CX, CY, NZ),
            pltpu.VMEM((1, PERFS), jnp.int32), pltpu.VMEM((1, PERFS), jnp.int32),
            vm(1, PERFS), vm(1, PERFS),
            pltpu.VMEM((64, 128), jnp.int32), pltpu.VMEM((64, 128), jnp.int32),
            vm(16, NZ), vm(16, NZ), vm(8, NZ), vm(8, NZ), vm(8, NZ), vm(8, NZ),
            vm(16, NZ), vm(16, NZ),
            vm(8, PERFS), vm(8, PERFS),
            vm(RUN, 2, PAIRS, 128), vm(RUN, 2, PAIRS, 128),
            vm(PAIRS, 8, 128), vm(PAIRS, 8, 128), vm(2, 128),
            pltpu.SemaphoreType.DMA((N_SEM,)),
            pltpu.SemaphoreType.DMA((N_SEM,)),
            pltpu.SemaphoreType.DMA((N_LOCAL,)),
        ],
        compiler_params=pltpu.CompilerParams(
            collective_id=0, has_side_effects=True, vmem_limit_bytes=40 * 2**20
        ),
    )(
        unk, coe, rock, table, row(loc), row(pw), row(wi), row(pp),
        own.reshape(64, 128), slo.reshape(64, 128),
    )


def solution(mesh):
    in_specs = (
        P("sec", None, "gx", "gy", None),
        P("sec", None, "gx", "gy", None),
        P("gx", "gy", None),
        P(),
        P(("gx", "gy")),
        P(("gx", "gy")),
        P(("gx", "gy")),
        P(("gx", "gy")),
        P(),
        P(),
    )
    out_specs = (P("sec", None, "gx", "gy", None), P("sec", None, ("gx", "gy")))
    return jax.shard_map(
        per_device, mesh=mesh, in_specs=in_specs, out_specs=out_specs, check_vma=False
    )
```

```python
import functools

import jax
import jax.numpy as jnp
from jax import lax
from jax.experimental import pallas as pl
from jax.experimental.pallas import tpu as pltpu
from jax.sharding import PartitionSpec as P

MESH = pl.DeviceIdType.MESH
F32 = jnp.float32
BF16 = jnp.bfloat16
CX, CY, NZ = 4, 64, 256
PERFS = 256
NROCK = 8
RING = 64
RUN = 16
PAIRS = 8
LINKED = 1.5

LO, HI = 8, 8 + CY
BODY = pl.ds(LO, CY)

X_UP, X_DOWN = 0, 4
Y_START = 8
KH_OVER = 9
KV_CROSS, KV_ON = 10, 12
X2_UP, X2_DOWN = 14, 16
Y_SECOND = 18
MAIN_OVER = 19
REST_OVER = 20
AT_OVER = 26
K_UP, K_DOWN, K_Y = 27, 28, 29
S_UP, S_DOWN, S_Y = 30, 31, 32
P_UP, P_DOWN, P_Y = 33, 34, 35
R_FIRST = 36
R_SECOND = 52
N_SEM = 60
N_LOCAL = 16


def reciprocal(x):
    r = pl.reciprocal(x, approx=True)
    return r * (2.0 - x * r)


def harmonic(a, b):
    return (2.0 * a) * (b * reciprocal(a + b))


def split(x):
    high = x.astype(BF16)
    rest = x - high.astype(F32)
    mid = rest.astype(BF16)
    low = (rest - mid.astype(F32)).astype(BF16)
    return high, mid, low


def dot_nt(a, b):
    return lax.dot_general(a, b, (((1,), (1,)), ((), ())), preferred_element_type=F32)


def dot_nn(a, b):
    return lax.dot_general(a, b, (((1,), (0,)), ((), ())), preferred_element_type=F32)


def hot(index, rows):
    return lax.broadcasted_iota(jnp.int32, (rows, PERFS), 0) == index


def as_bf16(mask):
    return jnp.where(mask, 1.0, 0.0).astype(BF16)


def spread(row_hot, col_mask, value):
    total = None
    for piece in split(value):
        term = dot_nt(row_hot, jnp.where(col_mask, piece.astype(F32), 0.0).astype(BF16))
        total = term if total is None else total + term
    return total


def pick(field, row_mask, col_hot):
    total = None
    for piece in split(field):
        term = dot_nn(piece, col_hot)
        total = term if total is None else total + term
    return jnp.sum(jnp.where(row_mask, total, 0.0), axis=0, keepdims=True)


def body(
    unk, coe, rock, table, loc, pw, wi, pp, own, slo,
    out, rates,
    F0, F1, F2, T0, SH, KVC, RL, WG, VM, RK, TX, TY, TZ, INV, BASE, WD, MOB,
    s_loc, s_pw, s_wi, s_pp, s_own, s_slo,
    ys0, yr0, ys1, yr1, ys2, yr2, ys3, yr3, ys4, yr4, ats, atr,
    part, got1, part2, got2, rate_buf,
    send, recv, lsem,
):
    sec, gx, gy = (lax.axis_index(a) for a in ("sec", "gx", "gy"))
    up = (sec, lax.rem(gx + 1, RING), gy)
    down = (sec, lax.rem(gx + RING - 1, RING), gy)
    side = (sec, gx, 1 - gy)
    other = (1 - sec, gx, gy)
    cross = (1 - sec, gx, 1 - gy)
    zc, y = lax.rem(gx, RUN), gx // RUN
    pair = y * 2 + gy
    first = [(sec, y * RUN + lax.rem(zc + d, RUN), gy) for d in range(1, RUN)]
    second = []
    for d in range(1, PAIRS):
        q = lax.rem(pair + d, PAIRS)
        second.append((sec, (q // 2) * RUN + zc, lax.rem(q, 2)))

    barrier = pltpu.get_barrier_semaphore()
    partners = [up, down, side, other, cross] + first + second
    for dev in partners:
        pl.semaphore_signal(barrier, inc=1, device_id=dev, device_id_type=MESH)

    def local(i, src, dst):
        return pltpu.make_async_copy(src, dst, lsem.at[i])

    def remote(i, src, dst, dev):
        return pltpu.make_async_remote_copy(
            src_ref=src,
            dst_ref=dst,
            send_sem=send.at[i],
            recv_sem=recv.at[i],
            device_id=dev,
            device_id_type=MESH,
        )

    small = [
        local(0, loc, s_loc),
        local(1, pw, s_pw),
        local(2, wi, s_wi),
        local(3, pp, s_pp),
        local(4, own, s_own),
        local(5, slo, s_slo),
    ]
    for c in small:
        c.start()
    loads0 = [
        local(6, unk.at[0], F0.at[:, pl.ds(1, CX), BODY, :]),
        local(7, coe.at[0, 0], T0.at[0, pl.ds(1, CX), BODY, :]),
        local(8, coe.at[0, 3], T0.at[1, pl.ds(1, CX), BODY, :]),
        local(9, coe.at[0, pl.ds(1, 2)], KVC),
    ]
    loads1 = [local(6, unk.at[0], WG), local(7, coe.at[0], VM), local(8, rock, RK)]

    def wells():
        for c in small:
            c.wait()
        place = s_loc[...]
        row, col = lax.shift_right_logical(place, 8), jnp.bitwise_and(place, 255)
        row_mask, col_mask = hot(row, PERFS), hot(col, PERFS)
        row_hot, col_hot = as_bf16(row_mask), as_bf16(col_mask)
        live = s_pw[...] >= 0
        index = jnp.where(live, s_wi[...], 0.0)
        WD[0] = spread(row_hot, col_mask, index)
        WD[1] = spread(row_hot, col_mask, index * s_pp[...])
        well = jnp.maximum(s_pw[...], 0)
        w_row = hot(lax.shift_right_logical(well, 7), 64)
        w_col = as_bf16(hot(jnp.bitwise_and(well, 127), 128))

        def look(ref):
            found = dot_nn(ref[...].astype(F32).astype(BF16), w_col)
            return jnp.sum(jnp.where(w_row, found, 0.0), axis=0, keepdims=True).astype(jnp.int32)

        owner, slot = look(s_own), look(s_slo)
        o_gx, o_gy = lax.shift_right_logical(owner, 1), jnp.bitwise_and(owner, 1)
        order = (
            jnp.bitwise_and(o_gx, RUN - 1) * PAIRS + lax.shift_right_logical(o_gx, 4) * 2 + o_gy
        )
        return row_mask, col_hot, index, order, slot

    def rates_first(values, order, slot):
        own_mask, slot_hot = hot(order, RUN * PAIRS), as_bf16(hot(slot, 128))
        for a, value in enumerate(values):
            total = None
            for piece in split(value):
                lhs = jnp.where(own_mask, piece.astype(F32), 0.0).astype(BF16)
                term = dot_nt(lhs, slot_hot)
                total = term if total is None else total + term
            part[:, a] = total.reshape(RUN, PAIRS, 128)
        copies = [
            remote(R_FIRST + d, part.at[lax.rem(zc + d, RUN)], got1.at[d], first[d - 1])
            for d in far_first(RUN)
        ]
        for c in copies:
            c.start()
        return copies

    def rates_second(copies):
        for c in copies:
            c.wait()
        total = part[zc]
        for d in range(1, RUN):
            total = total + got1[d]
        part2[...] = jnp.zeros_like(part2)
        for a in range(2):
            for q in range(PAIRS):
                part2[q, a : a + 1] = total[a, q : q + 1]
        copies = [
            remote(R_SECOND + d, part2.at[lax.rem(pair + d, PAIRS)], got2.at[d], second[d - 1])
            for d in range(1, PAIRS)
        ]
        for c in copies:
            c.start()
        return copies

    def rates_last(copies):
        for c in copies:
            c.wait()
        total = part2[pair]
        for d in range(1, PAIRS):
            total = total + got2[d]
        rate_buf[...] = total[0:2]
        c = local(10, rate_buf, rates.at[0])
        c.start()
        return c

    def edge(ref, f, i):
        return jnp.where(gy == 0, ref[f, i, HI - 1 : HI, :], ref[f, i, LO : LO + 1, :])

    def set_edges(ref, f, i, row, zero):
        if zero:
            ref[f, i, HI : HI + 1, :] = jnp.where(gy == 0, row, 0.0)
            ref[f, i, LO - 1 : LO, :] = jnp.where(gy == 1, row, 0.0)
        else:
            ref[f, i, HI : HI + 1, :] = row
            ref[f, i, LO - 1 : LO, :] = row

    def x_face(f, a):
        face = harmonic(T0[f, a, BODY, :], T0[f, a + 1, BODY, :])
        if a == 0:
            face = jnp.where(gx == 0, 0.0, face)
        if a == CX:
            face = jnp.where(gx == RING - 1, 0.0, face)
        TX[f, a] = face

    def y_faces(f, i):
        TY[f, i - 1, LO : HI - 1] = harmonic(T0[f, i, LO : HI - 1, :], T0[f, i, LO + 1 : HI, :])

    def y_ends(f, i):
        for r in (LO - 1, HI - 1):
            TY[f, i - 1, r : r + 1] = harmonic(T0[f, i, r : r + 1, :], T0[f, i, r + 1 : r + 2, :])

    def z_faces(f, i, value):
        lane = lax.broadcasted_iota(jnp.int32, (CY, NZ), 1)
        face = harmonic(value, pltpu.roll(value, NZ - 1, 1))
        TZ[f, i - 1] = jnp.where(lane == NZ - 1, 0.0, face)

    def system(f, i, start):
        c = KVC[1, i - 1]
        tz = TZ[f, i - 1]
        total = (
            c + TX[f, i - 1] + TX[f, i] + TY[f, i - 1, LO - 1 : HI - 1] + TY[f, i - 1, LO:HI]
            + tz + pltpu.roll(tz, 1, 1)
        )
        base = c * start[f, i, BODY, :]
        if f == 0:
            rows = slice((i - 1) * CY, i * CY)
            total = total + WD[0, rows]
            base = base + WD[1, rows]
        INV[f, i - 1] = reciprocal(total)
        BASE[f, i - 1] = base

    def sweep(f, i, now, later):
        tz = TZ[f, i - 1]
        centre = now[f, i, BODY, :]
        total = (
            BASE[f, i - 1]
            + TX[f, i - 1] * now[f, i - 1, BODY, :]
            + TX[f, i] * now[f, i + 1, BODY, :]
            + TY[f, i - 1, LO - 1 : HI - 1] * now[f, i, LO - 1 : HI - 1, :]
            + TY[f, i - 1, LO:HI] * now[f, i, LO + 1 : HI + 1, :]
            + tz * pltpu.roll(centre, NZ - 1, 1)
            + pltpu.roll(tz * centre, 1, 1)
        )
        later[f, i, BODY, :] = total * INV[f, i - 1]

    def far_first(n):
        return sorted(range(1, n), key=lambda d: -min(d, n - d))

    def x_pair(i_up, i_down, ref, both=True, f=0):
        pick_ = (lambda a: ref.at[:, a, BODY, :]) if both else (lambda a: ref.at[f, a, BODY, :])
        return [
            remote(i_up, pick_(CX), pick_(0), up),
            remote(i_down, pick_(1), pick_(CX + 1), down),
        ]

    kh_over = remote(KH_OVER, coe.at[0, 0], T0.at[0, pl.ds(1, CX), BODY, :], other)
    halves = [pl.ds(0, 2), pl.ds(2, 2)]
    kv_cross = [remote(KV_CROSS + c, coe.at[0, 1, h], RL.at[h], cross) for c, h in enumerate(halves)]
    kv_on = [remote(KV_ON + c, RL.at[h], KVC.at[0, h], side) for c, h in enumerate(halves)]
    main_rows = pl.ds(pl.multiple_of(LO + 8 * gy, 8), CY - 8)
    edge_rows = pl.ds(pl.multiple_of(HI - 8 - (CY - 8) * gy, 8), 8)
    inner = F2.at[:, pl.ds(2, 2), main_rows, :]
    main_over = remote(MAIN_OVER, inner, inner, other)
    rest_over = []
    for f in range(2):
        views = [F2.at[f, 1, BODY, :], F2.at[f, CX, BODY, :], F2.at[f, pl.ds(2, 2), edge_rows, :]]
        rest_over.append(
            [remote(REST_OVER + 3 * f + n, v, v, other) for n, v in enumerate(views)]
        )
    at_over = remote(AT_OVER, ats, atr, other)
    layers = range(1, CX + 1)

    @pl.when(sec == 0)
    def _():
        for c in loads0:
            c.start()
        pl.semaphore_wait(barrier, len(partners))
        halo_x = []
        for f in range(2):
            group = []
            for s, dev, src, dst in ((X_UP, up, CX - 1, 0), (X_DOWN, down, 0, CX + 1)):
                group += [
                    remote(s + 2 * f, unk.at[0, f, src], F0.at[f, dst, BODY, :], dev),
                    remote(s + 2 * f + 1, coe.at[0, 3 * f, src], T0.at[f, dst, BODY, :], dev),
                ]
            for c in group:
                c.start()
            halo_x.append(group)
        for c in loads0:
            c.wait()
        for f in range(2):
            for i in layers:
                r = f * CX + i - 1
                ys0[r : r + 1] = edge(F0, f, i)
                ys0[r + 8 : r + 9] = edge(T0, f, i)
        halo_y = remote(Y_START, ys0, yr0, side)
        halo_y.start()
        kh_over.start()
        for c in kv_cross:
            c.start()
        for f in range(2):
            for i in layers:
                z_faces(f, i, KVC[0, i - 1] if f == 0 else T0[1, i, BODY, :])
                y_faces(f, i)
            for a in range(1, CX):
                x_face(f, a)
        row_mask, col_hot, index, order, slot = wells()
        halo_y.wait()
        for f in range(2):
            for i in layers:
                r = f * CX + i - 1
                set_edges(F0, f, i, yr0[r : r + 1], False)
                set_edges(T0, f, i, yr0[r + 8 : r + 9], True)
                y_ends(f, i)
            for i in (2, 3):
                system(f, i, F0)
                sweep(f, i, F0, F1)
                F1[f, i, HI : HI + 1, :] = jnp.zeros((1, NZ), F32)
                F1[f, i, LO - 1 : LO, :] = jnp.zeros((1, NZ), F32)
        halo_x2 = []
        for f in range(2):
            for c in halo_x[f]:
                c.wait()
            for a in (0, CX):
                x_face(f, a)
            for i in (1, CX):
                system(f, i, F0)
                sweep(f, i, F0, F1)
            halo_x2.append(x_pair(X2_UP + f, X2_DOWN + f, F1, False, f))
            for c in halo_x2[f]:
                c.start()
        for f in range(2):
            for i in layers:
                r = f * CX + i - 1
                ys1[r : r + 1] = edge(F1, f, i)
        halo_y = remote(Y_SECOND, ys1, yr1, side)
        halo_y.start()
        for f in range(2):
            for i in (2, 3):
                sweep(f, i, F1, F2)
        main_over.start()
        halo_y.wait()
        for at, r, t in ((0, HI - 1, HI - 1), (1, LO, LO - 1)):

            @pl.when(gy == at)
            def _(r=r, t=t):
                for f in range(2):
                    for i in (2, 3):
                        n = f * CX + i - 1
                        more = TY[f, i - 1, t : t + 1] * INV[f, i - 1, r - LO : r - LO + 1]
                        F2[f, i, r : r + 1, :] = F2[f, i, r : r + 1, :] + more * yr1[n : n + 1]

        for f in range(2):
            for i in (1, CX):
                n = f * CX + i - 1
                set_edges(F1, f, i, yr1[n : n + 1], False)
            for c in halo_x2[f]:
                c.wait()
            for i in (1, CX):
                sweep(f, i, F1, F2)
        pressure = pick(F2[0, 1 : CX + 1, BODY, :].reshape(CX * CY, NZ), row_mask, col_hot)
        warmth = pick(F2[1, 1 : CX + 1, BODY, :].reshape(CX * CY, NZ), row_mask, col_hot)
        ats[...] = jnp.zeros_like(ats)
        ats[0:1] = pressure
        ats[1:2] = warmth
        at_over.start()
        for f in (1, 0):
            for c in rest_over[f]:
                c.start()
        save = local(11, F2.at[:, pl.ds(1, CX), BODY, :], out.at[0])
        save.start()
        q = index * (s_pp[...] - pressure)
        copies = rates_first((q, q * warmth), order, slot)
        copies = rates_second(copies)
        last = rates_last(copies)
        for c in [kh_over, main_over, at_over] + kv_cross + rest_over[0] + rest_over[1]:
            c.wait_send()
        save.wait()
        last.wait()

    @pl.when(sec == 1)
    def _():
        for c in loads1:
            c.start()
        pl.semaphore_wait(barrier, len(partners))
        for c in loads1:
            c.wait()
        for i in range(CX):
            kind = RK[i]
            ends = []
            masks = [kind == t for t in range(1, NROCK)]
            for k in range(3):
                e = jnp.full((CY, NZ), table[k, 0], F32)
                for t in range(1, NROCK):
                    e = jnp.where(masks[t - 1], table[k, t], e)
                ends.append(e)
            water, gas = WG[0, i], WG[1, i]
            oil = 1.0 - water - gas
            MOB[0, i] = ends[0] * water * water * reciprocal(VM[1, i])
            MOB[1, i] = ends[1] * oil * oil * reciprocal(VM[2, i])
            MOB[2, i] = ends[2] * gas * gas * reciprocal(VM[3, i])
        kv_cross[0].wait_recv()
        kv_on[0].start()
        row_mask, col_hot, index, order, slot = wells()
        lw, lo, lg = (pick(MOB[k].reshape(CX * CY, NZ), row_mask, col_hot) for k in range(3))
        kv_cross[1].wait_recv()
        kv_on[1].start()

        kh_over.wait_recv()
        halo_k = x_pair(K_UP, K_DOWN, T0, False)
        for c in halo_k:
            c.start()
        ys2[...] = jnp.zeros_like(ys2)
        for i in layers:
            ys2[i - 1 : i] = edge(T0, 0, i)
        halo_ky = remote(K_Y, ys2, yr2, side)
        halo_ky.start()
        for i in layers:
            y_faces(0, i)
        for a in range(1, CX):
            x_face(0, a)
        for c in kv_on:
            c.wait()
        for i in layers:
            z_faces(0, i, KVC[0, i - 1])
        for c in halo_k:
            c.wait()
        for a in (0, CX):
            x_face(0, a)
        halo_ky.wait()
        for i in layers:
            set_edges(T0, 0, i, yr2[i - 1 : i], True)
            y_ends(0, i)

        main_over.wait_recv()
        at_over.wait_recv()
        q = index * (s_pp[...] - atr[0:1])
        lo = lo * jnp.exp(LINKED * (atr[1:2] - 1.0))
        scaled = q * reciprocal(lw + lo + lg)
        copies = rates_first((scaled * lw, scaled * lg), order, slot)
        for c in rest_over[1]:
            c.wait_recv()
        for i in (1, 4, 2, 3):
            other_mob = MOB[1, i - 1] * jnp.exp(LINKED * (F2[1, i, BODY, :] - 1.0))
            part_all = reciprocal(MOB[0, i - 1] + other_mob + MOB[2, i - 1])
            SH[0, i, BODY, :] = MOB[0, i - 1] * part_all
            SH[1, i, BODY, :] = MOB[2, i - 1] * part_all
        halo_s = x_pair(S_UP, S_DOWN, SH)
        for c in halo_s:
            c.start()
        for i in layers:
            ys3[i - 1 : i] = edge(SH, 0, i)
            ys3[i + 3 : i + 4] = edge(SH, 1, i)
        halo_sy = remote(S_Y, ys3, yr3, side)
        halo_sy.start()
        for c in rest_over[0]:
            c.wait_recv()
        halo_p = x_pair(P_UP, P_DOWN, F2, False)
        for c in halo_p:
            c.start()
        ys4[...] = jnp.zeros_like(ys4)
        for i in layers:
            ys4[i - 1 : i] = edge(F2, 0, i)
        halo_py = remote(P_Y, ys4, yr4, side)
        halo_py.start()
        copies = rates_second(copies)

        halo_sy.wait()
        halo_py.wait()
        for i in layers:
            set_edges(F2, 0, i, yr4[i - 1 : i], False)
            set_edges(SH, 0, i, yr3[i - 1 : i], False)
            set_edges(SH, 1, i, yr3[i + 3 : i + 4], False)
        for c in halo_s + halo_p:
            c.wait()

        def through(flow, shares):
            pos, neg = jnp.maximum(flow, 0.0), jnp.minimum(flow, 0.0)
            return [pos * a + neg * b for a, b in shares]

        for i in layers:
            p = F2[0, i, BODY, :]
            s = [SH[a, i, BODY, :] for a in range(2)]
            tz = TZ[0, i - 1]
            west = through(
                TX[0, i - 1] * (F2[0, i - 1, BODY, :] - p),
                [(SH[a, i - 1, BODY, :], s[a]) for a in range(2)],
            )
            east = through(
                TX[0, i] * (p - F2[0, i + 1, BODY, :]),
                [(s[a], SH[a, i + 1, BODY, :]) for a in range(2)],
            )
            south = through(
                TY[0, i - 1, LO - 1 : HI - 1] * (F2[0, i, LO - 1 : HI - 1, :] - p),
                [(SH[a, i, LO - 1 : HI - 1, :], s[a]) for a in range(2)],
            )
            north = through(
                TY[0, i - 1, LO:HI] * (p - F2[0, i, LO + 1 : HI + 1, :]),
                [(s[a], SH[a, i, LO + 1 : HI + 1, :]) for a in range(2)],
            )
            top = through(
                tz * (p - pltpu.roll(p, NZ - 1, 1)),
                [(s[a], pltpu.roll(s[a], NZ - 1, 1)) for a in range(2)],
            )
            rows = slice((i - 1) * CY, i * CY)
            rate = WD[1, rows] - WD[0, rows] * p
            inverse = reciprocal(VM[0, i - 1])
            for a in range(2):
                net = west[a] - east[a] + south[a] - north[a] + pltpu.roll(top[a], 1, 1) - top[a]
                WG[a, i - 1] = WG[a, i - 1] + (net + rate * s[a]) * inverse
        save = local(11, WG, out.at[0])
        save.start()
        last = rates_last(copies)
        save.wait()
        last.wait()


def per_device(unk, coe, rock, table, loc, pw, wi, pp, own, slo):
    any_ = pl.BlockSpec(memory_space=pl.ANY)
    row = lambda a: a.reshape(1, PERFS)
    vm = lambda *s: pltpu.VMEM(s, F32)
    halo = (2, CX + 2, CY + 16, NZ)
    return pl.pallas_call(
        body,
        out_shape=(
            jax.ShapeDtypeStruct((1, 2, CX, CY, NZ), F32),
            jax.ShapeDtypeStruct((1, 2, 128), F32),
        ),
        in_specs=[any_] * 3 + [pl.BlockSpec(memory_space=pltpu.SMEM)] + [any_] * 6,
        out_specs=(any_, any_),
        scratch_shapes=[
            vm(*halo), vm(*halo), vm(*halo), vm(*halo), vm(*halo),
            vm(2, CX, CY, NZ), vm(CX, CY, NZ),
            vm(2, CX, CY, NZ),
            vm(4, CX, CY, NZ),
            pltpu.VMEM((CX, CY, NZ), jnp.int32),
            vm(2, CX + 1, CY, NZ), vm(2, CX, CY + 16, NZ), vm(2, CX, CY, NZ),
            vm(2, CX, CY, NZ), vm(2, CX, CY, NZ),
            vm(2, CX * CY, NZ),
            vm(3, CX, CY, NZ),
            pltpu.VMEM((1, PERFS), jnp.int32), pltpu.VMEM((1, PERFS), jnp.int32),
            vm(1, PERFS), vm(1, PERFS),
            pltpu.VMEM((64, 128), jnp.int32), pltpu.VMEM((64, 128), jnp.int32),
            vm(16, NZ), vm(16, NZ), vm(8, NZ), vm(8, NZ), vm(8, NZ), vm(8, NZ),
            vm(8, NZ), vm(8, NZ), vm(8, NZ), vm(8, NZ),
            vm(8, PERFS), vm(8, PERFS),
            vm(RUN, 2, PAIRS, 128), vm(RUN, 2, PAIRS, 128),
            vm(PAIRS, 8, 128), vm(PAIRS, 8, 128), vm(2, 128),
            pltpu.SemaphoreType.DMA((N_SEM,)),
            pltpu.SemaphoreType.DMA((N_SEM,)),
            pltpu.SemaphoreType.DMA((N_LOCAL,)),
        ],
        compiler_params=pltpu.CompilerParams(
            collective_id=0, has_side_effects=True, vmem_limit_bytes=60 * 2**20
        ),
    )(
        unk, coe, rock, table.T, row(loc), row(pw), row(wi), row(pp),
        own.reshape(64, 128), slo.reshape(64, 128),
    )


def solution(mesh):
    in_specs = (
        P("sec", None, "gx", "gy", None),
        P("sec", None, "gx", "gy", None),
        P("gx", "gy", None),
        P(),
        P(("gx", "gy")),
        P(("gx", "gy")),
        P(("gx", "gy")),
        P(("gx", "gy")),
        P(),
        P(),
    )
    out_specs = (P("sec", None, "gx", "gy", None), P("sec", None, ("gx", "gy")))
    return jax.shard_map(
        per_device, mesh=mesh, in_specs=in_specs, out_specs=out_specs, check_vma=False
    )
```

```python
import functools

import jax
import jax.numpy as jnp
from jax import lax
from jax.experimental import pallas as pl
from jax.experimental.pallas import tpu as pltpu
from jax.sharding import PartitionSpec as P

MESH = pl.DeviceIdType.MESH
F32 = jnp.float32
BF16 = jnp.bfloat16
CX, CY, NZ = 4, 64, 256
PERFS = 256
NROCK = 8
RING = 64
RUN = 16
PAIRS = 8
LINKED = 1.5

LO, HI = 8, 8 + CY
BODY = pl.ds(LO, CY)

X_UP, X_DOWN = 0, 4
Y_START = 8
KH_OVER = 9
KV_CROSS, KV_ON, KV_OVER = 10, 11, 12
X2_UP, X2_DOWN = 14, 16
Y_SECOND = 18
MAIN_OVER = 19
REST_OVER = 20
AT_OVER = 26
K_UP, K_DOWN, K_Y = 27, 28, 29
S_UP, S_DOWN, S_Y = 30, 31, 32
P_UP, P_DOWN, P_Y = 33, 34, 35
R_FIRST = 36
R_SECOND = 52
N_SEM = 60
N_LOCAL = 16


def reciprocal(x):
    r = pl.reciprocal(x, approx=True)
    return r * (2.0 - x * r)


def harmonic(a, b):
    return (2.0 * a) * (b * reciprocal(a + b))


def split(x):
    high = x.astype(BF16)
    rest = x - high.astype(F32)
    mid = rest.astype(BF16)
    low = (rest - mid.astype(F32)).astype(BF16)
    return high, mid, low


def dot_nt(a, b):
    return lax.dot_general(a, b, (((1,), (1,)), ((), ())), preferred_element_type=F32)


def dot_nn(a, b):
    return lax.dot_general(a, b, (((1,), (0,)), ((), ())), preferred_element_type=F32)


def hot(index, rows):
    return lax.broadcasted_iota(jnp.int32, (rows, PERFS), 0) == index


def as_bf16(mask):
    return jnp.where(mask, 1.0, 0.0).astype(BF16)


def spread(row_hot, col_mask, value):
    total = None
    for piece in split(value):
        term = dot_nt(row_hot, jnp.where(col_mask, piece.astype(F32), 0.0).astype(BF16))
        total = term if total is None else total + term
    return total


def pick(field, row_mask, col_hot):
    total = None
    for piece in split(field):
        term = dot_nn(piece, col_hot)
        total = term if total is None else total + term
    return jnp.sum(jnp.where(row_mask, total, 0.0), axis=0, keepdims=True)


def body(
    unk, coe, rock, table, loc, pw, wi, pp, own, slo,
    out, rates,
    F0, F1, F2, T0, SH, KVC, RL, WG, VM, RK, TX, TY, TZ, INV, BASE, WD, MOB,
    s_loc, s_pw, s_wi, s_pp, s_own, s_slo,
    ys0, yr0, ys1, yr1, ys2, yr2, ys3, yr3, ys4, yr4, ats, atr,
    part, got1, part2, got2, rate_buf,
    send, recv, lsem,
):
    sec, gx, gy = (lax.axis_index(a) for a in ("sec", "gx", "gy"))
    up = (sec, lax.rem(gx + 1, RING), gy)
    down = (sec, lax.rem(gx + RING - 1, RING), gy)
    side = (sec, gx, 1 - gy)
    other = (1 - sec, gx, gy)
    cross = (1 - sec, gx, 1 - gy)
    zc, y = lax.rem(gx, RUN), gx // RUN
    pair = y * 2 + gy
    first = [(sec, y * RUN + lax.rem(zc + d, RUN), gy) for d in range(1, RUN)]
    second = []
    for d in range(1, PAIRS):
        q = lax.rem(pair + d, PAIRS)
        second.append((sec, (q // 2) * RUN + zc, lax.rem(q, 2)))

    barrier = pltpu.get_barrier_semaphore()
    partners = [up, down, side, other, cross] + first + second
    for dev in partners:
        pl.semaphore_signal(barrier, inc=1, device_id=dev, device_id_type=MESH)

    def local(i, src, dst):
        return pltpu.make_async_copy(src, dst, lsem.at[i])

    def remote(i, src, dst, dev):
        return pltpu.make_async_remote_copy(
            src_ref=src,
            dst_ref=dst,
            send_sem=send.at[i],
            recv_sem=recv.at[i],
            device_id=dev,
            device_id_type=MESH,
        )

    small = [
        local(0, loc, s_loc),
        local(1, pw, s_pw),
        local(2, wi, s_wi),
        local(3, pp, s_pp),
        local(4, own, s_own),
        local(5, slo, s_slo),
    ]
    for c in small:
        c.start()
    loads0 = [
        local(6, unk.at[0], F0.at[:, pl.ds(1, CX), BODY, :]),
        local(7, coe.at[0, 0], T0.at[0, pl.ds(1, CX), BODY, :]),
        local(8, coe.at[0, 3], T0.at[1, pl.ds(1, CX), BODY, :]),
        local(9, coe.at[0, pl.ds(1, 2)], KVC),
    ]
    loads1 = [local(6, unk.at[0], WG), local(7, coe.at[0], VM), local(8, rock, RK)]

    def wells():
        for c in small:
            c.wait()
        place = s_loc[...]
        row, col = lax.shift_right_logical(place, 8), jnp.bitwise_and(place, 255)
        row_mask, col_mask = hot(row, PERFS), hot(col, PERFS)
        row_hot, col_hot = as_bf16(row_mask), as_bf16(col_mask)
        live = s_pw[...] >= 0
        index = jnp.where(live, s_wi[...], 0.0)
        WD[0] = spread(row_hot, col_mask, index)
        WD[1] = spread(row_hot, col_mask, index * s_pp[...])
        well = jnp.maximum(s_pw[...], 0)
        w_row = hot(lax.shift_right_logical(well, 7), 64)
        w_col = as_bf16(hot(jnp.bitwise_and(well, 127), 128))

        def look(ref):
            found = dot_nn(ref[...].astype(F32).astype(BF16), w_col)
            return jnp.sum(jnp.where(w_row, found, 0.0), axis=0, keepdims=True).astype(jnp.int32)

        owner, slot = look(s_own), look(s_slo)
        o_gx, o_gy = lax.shift_right_logical(owner, 1), jnp.bitwise_and(owner, 1)
        order = (
            jnp.bitwise_and(o_gx, RUN - 1) * PAIRS + lax.shift_right_logical(o_gx, 4) * 2 + o_gy
        )
        return row_mask, col_hot, index, order, slot

    def rates_first(values, order, slot):
        own_mask, slot_hot = hot(order, RUN * PAIRS), as_bf16(hot(slot, 128))
        for a, value in enumerate(values):
            total = None
            for piece in split(value):
                lhs = jnp.where(own_mask, piece.astype(F32), 0.0).astype(BF16)
                term = dot_nt(lhs, slot_hot)
                total = term if total is None else total + term
            part[:, a] = total.reshape(RUN, PAIRS, 128)
        copies = [
            remote(R_FIRST + d, part.at[lax.rem(zc + d, RUN)], got1.at[d], first[d - 1])
            for d in far_first(RUN)
        ]
        for c in copies:
            c.start()
        return copies

    def rates_second(copies):
        for c in copies:
            c.wait()
        total = part[zc]
        for d in range(1, RUN):
            total = total + got1[d]
        part2[...] = jnp.zeros_like(part2)
        for a in range(2):
            for q in range(PAIRS):
                part2[q, a : a + 1] = total[a, q : q + 1]
        copies = [
            remote(R_SECOND + d, part2.at[lax.rem(pair + d, PAIRS)], got2.at[d], second[d - 1])
            for d in range(1, PAIRS)
        ]
        for c in copies:
            c.start()
        return copies

    def rates_last(copies):
        for c in copies:
            c.wait()
        total = part2[pair]
        for d in range(1, PAIRS):
            total = total + got2[d]
        rate_buf[...] = total[0:2]
        c = local(10, rate_buf, rates.at[0])
        c.start()
        return c

    def edge(ref, f, i):
        return jnp.where(gy == 0, ref[f, i, HI - 1 : HI, :], ref[f, i, LO : LO + 1, :])

    def set_edges(ref, f, i, row, zero):
        if zero:
            ref[f, i, HI : HI + 1, :] = jnp.where(gy == 0, row, 0.0)
            ref[f, i, LO - 1 : LO, :] = jnp.where(gy == 1, row, 0.0)
        else:
            ref[f, i, HI : HI + 1, :] = row
            ref[f, i, LO - 1 : LO, :] = row

    def x_face(f, a):
        face = harmonic(T0[f, a, BODY, :], T0[f, a + 1, BODY, :])
        if a == 0:
            face = jnp.where(gx == 0, 0.0, face)
        if a == CX:
            face = jnp.where(gx == RING - 1, 0.0, face)
        TX[f, a] = face

    def y_faces(f, i):
        TY[f, i - 1, LO : HI - 1] = harmonic(T0[f, i, LO : HI - 1, :], T0[f, i, LO + 1 : HI, :])

    def y_ends(f, i):
        for r in (LO - 1, HI - 1):
            TY[f, i - 1, r : r + 1] = harmonic(T0[f, i, r : r + 1, :], T0[f, i, r + 1 : r + 2, :])

    def z_faces(f, i, value):
        lane = lax.broadcasted_iota(jnp.int32, (CY, NZ), 1)
        face = harmonic(value, pltpu.roll(value, NZ - 1, 1))
        TZ[f, i - 1] = jnp.where(lane == NZ - 1, 0.0, face)

    def system(f, i, start):
        c = KVC[1, i - 1]
        tz = TZ[f, i - 1]
        total = (
            c + TX[f, i - 1] + TX[f, i] + TY[f, i - 1, LO - 1 : HI - 1] + TY[f, i - 1, LO:HI]
            + tz + pltpu.roll(tz, 1, 1)
        )
        base = c * start[f, i, BODY, :]
        if f == 0:
            rows = slice((i - 1) * CY, i * CY)
            total = total + WD[0, rows]
            base = base + WD[1, rows]
        INV[f, i - 1] = reciprocal(total)
        BASE[f, i - 1] = base

    def sweep(f, i, now, later):
        tz = TZ[f, i - 1]
        centre = now[f, i, BODY, :]
        total = (
            BASE[f, i - 1]
            + TX[f, i - 1] * now[f, i - 1, BODY, :]
            + TX[f, i] * now[f, i + 1, BODY, :]
            + TY[f, i - 1, LO - 1 : HI - 1] * now[f, i, LO - 1 : HI - 1, :]
            + TY[f, i - 1, LO:HI] * now[f, i, LO + 1 : HI + 1, :]
            + tz * pltpu.roll(centre, NZ - 1, 1)
            + pltpu.roll(tz * centre, 1, 1)
        )
        later[f, i, BODY, :] = total * INV[f, i - 1]

    def far_first(n):
        return sorted(range(1, n), key=lambda d: -min(d, n - d))

    def x_pair(i_up, i_down, ref, both=True, f=0):
        pick_ = (lambda a: ref.at[:, a, BODY, :]) if both else (lambda a: ref.at[f, a, BODY, :])
        return [
            remote(i_up, pick_(CX), pick_(0), up),
            remote(i_down, pick_(1), pick_(CX + 1), down),
        ]

    kh_over = remote(KH_OVER, coe.at[0, 0], T0.at[0, pl.ds(1, CX), BODY, :], other)
    halves = [pl.ds(0, 3), pl.ds(3, 1)]
    kv_cross = remote(KV_CROSS, coe.at[0, 1, halves[0]], RL, cross)
    kv_on = remote(KV_ON, RL, KVC.at[0, halves[0]], side)
    kv_over = remote(KV_OVER, coe.at[0, 1, halves[1]], KVC.at[0, halves[1]], other)
    main_rows = pl.ds(pl.multiple_of(LO + 8 * gy, 8), CY - 8)
    edge_rows = pl.ds(pl.multiple_of(HI - 8 - (CY - 8) * gy, 8), 8)
    inner = F2.at[:, pl.ds(2, 2), main_rows, :]
    main_over = remote(MAIN_OVER, inner, inner, other)
    rest_over = []
    for f in range(2):
        views = [F2.at[f, 1, BODY, :], F2.at[f, CX, BODY, :], F2.at[f, pl.ds(2, 2), edge_rows, :]]
        rest_over.append(
            [remote(REST_OVER + 3 * f + n, v, v, other) for n, v in enumerate(views)]
        )
    at_over = remote(AT_OVER, ats, atr, other)
    layers = range(1, CX + 1)

    @pl.when(sec == 0)
    def _():
        for c in loads0:
            c.start()
        pl.semaphore_wait(barrier, len(partners))
        halo_x = []
        for f in range(2):
            group = []
            for s, dev, src, dst in ((X_UP, up, CX - 1, 0), (X_DOWN, down, 0, CX + 1)):
                group += [
                    remote(s + 2 * f, unk.at[0, f, src], F0.at[f, dst, BODY, :], dev),
                    remote(s + 2 * f + 1, coe.at[0, 3 * f, src], T0.at[f, dst, BODY, :], dev),
                ]
            for c in group:
                c.start()
            halo_x.append(group)
        for c in loads0:
            c.wait()
        for f in range(2):
            for i in layers:
                r = f * CX + i - 1
                ys0[r : r + 1] = edge(F0, f, i)
                ys0[r + 8 : r + 9] = edge(T0, f, i)
        halo_y = remote(Y_START, ys0, yr0, side)
        halo_y.start()
        kh_over.start()
        kv_cross.start()
        for f in range(2):
            for i in layers:
                z_faces(f, i, KVC[0, i - 1] if f == 0 else T0[1, i, BODY, :])
                y_faces(f, i)
            for a in range(1, CX):
                x_face(f, a)
        row_mask, col_hot, index, order, slot = wells()
        halo_y.wait()
        for f in range(2):
            for i in layers:
                r = f * CX + i - 1
                set_edges(F0, f, i, yr0[r : r + 1], False)
                set_edges(T0, f, i, yr0[r + 8 : r + 9], True)
                y_ends(f, i)
            for i in (2, 3):
                system(f, i, F0)
                sweep(f, i, F0, F1)
                F1[f, i, HI : HI + 1, :] = jnp.zeros((1, NZ), F32)
                F1[f, i, LO - 1 : LO, :] = jnp.zeros((1, NZ), F32)
        halo_x2 = []
        for f in range(2):
            for c in halo_x[f]:
                c.wait()
            for a in (0, CX):
                x_face(f, a)
            for i in (1, CX):
                system(f, i, F0)
                sweep(f, i, F0, F1)
            halo_x2.append(x_pair(X2_UP + f, X2_DOWN + f, F1, False, f))
            for c in halo_x2[f]:
                c.start()
        for f in range(2):
            for i in layers:
                r = f * CX + i - 1
                ys1[r : r + 1] = edge(F1, f, i)
        halo_y = remote(Y_SECOND, ys1, yr1, side)
        halo_y.start()
        for f in range(2):
            for i in (2, 3):
                sweep(f, i, F1, F2)
        main_over.start()
        halo_y.wait()
        for at, r, t in ((0, HI - 1, HI - 1), (1, LO, LO - 1)):

            @pl.when(gy == at)
            def _(r=r, t=t):
                for f in range(2):
                    for i in (2, 3):
                        n = f * CX + i - 1
                        more = TY[f, i - 1, t : t + 1] * INV[f, i - 1, r - LO : r - LO + 1]
                        F2[f, i, r : r + 1, :] = F2[f, i, r : r + 1, :] + more * yr1[n : n + 1]

        for f in range(2):
            for i in (1, CX):
                n = f * CX + i - 1
                set_edges(F1, f, i, yr1[n : n + 1], False)
            for c in halo_x2[f]:
                c.wait()
            for i in (1, CX):
                sweep(f, i, F1, F2)
        pressure = pick(F2[0, 1 : CX + 1, BODY, :].reshape(CX * CY, NZ), row_mask, col_hot)
        warmth = pick(F2[1, 1 : CX + 1, BODY, :].reshape(CX * CY, NZ), row_mask, col_hot)
        ats[...] = jnp.zeros_like(ats)
        ats[0:1] = pressure
        ats[1:2] = warmth
        at_over.start()
        for f in (1, 0):
            for c in rest_over[f]:
                c.start()
        kv_over.start()
        save = local(11, F2.at[:, pl.ds(1, CX), BODY, :], out.at[0])
        save.start()
        q = index * (s_pp[...] - pressure)
        copies = rates_first((q, q * warmth), order, slot)
        copies = rates_second(copies)
        last = rates_last(copies)
        for c in [kh_over, kv_cross, kv_over, main_over, at_over] + rest_over[0] + rest_over[1]:
            c.wait_send()
        save.wait()
        last.wait()

    @pl.when(sec == 1)
    def _():
        for c in loads1:
            c.start()
        pl.semaphore_wait(barrier, len(partners))
        for c in loads1:
            c.wait()
        for i in range(CX):
            kind = RK[i]
            ends = []
            masks = [kind == t for t in range(1, NROCK)]
            for k in range(3):
                e = jnp.full((CY, NZ), table[k, 0], F32)
                for t in range(1, NROCK):
                    e = jnp.where(masks[t - 1], table[k, t], e)
                ends.append(e)
            water, gas = WG[0, i], WG[1, i]
            oil = 1.0 - water - gas
            MOB[0, i] = ends[0] * water * water * reciprocal(VM[1, i])
            MOB[1, i] = ends[1] * oil * oil * reciprocal(VM[2, i])
            MOB[2, i] = ends[2] * gas * gas * reciprocal(VM[3, i])
        kv_cross.wait_recv()
        kv_on.start()
        row_mask, col_hot, index, order, slot = wells()
        lw, lo, lg = (pick(MOB[k].reshape(CX * CY, NZ), row_mask, col_hot) for k in range(3))

        kh_over.wait_recv()
        halo_k = x_pair(K_UP, K_DOWN, T0, False)
        for c in halo_k:
            c.start()
        ys2[...] = jnp.zeros_like(ys2)
        for i in layers:
            ys2[i - 1 : i] = edge(T0, 0, i)
        halo_ky = remote(K_Y, ys2, yr2, side)
        halo_ky.start()
        for i in layers:
            y_faces(0, i)
        for a in range(1, CX):
            x_face(0, a)
        for c in halo_k:
            c.wait()
        for a in (0, CX):
            x_face(0, a)
        halo_ky.wait()
        for i in layers:
            set_edges(T0, 0, i, yr2[i - 1 : i], True)
            y_ends(0, i)

        main_over.wait_recv()
        at_over.wait_recv()
        q = index * (s_pp[...] - atr[0:1])
        lo = lo * jnp.exp(LINKED * (atr[1:2] - 1.0))
        scaled = q * reciprocal(lw + lo + lg)
        copies = rates_first((scaled * lw, scaled * lg), order, slot)
        for c in rest_over[1]:
            c.wait_recv()
        for i in (1, 4, 2, 3):
            other_mob = MOB[1, i - 1] * jnp.exp(LINKED * (F2[1, i, BODY, :] - 1.0))
            part_all = reciprocal(MOB[0, i - 1] + other_mob + MOB[2, i - 1])
            SH[0, i, BODY, :] = MOB[0, i - 1] * part_all
            SH[1, i, BODY, :] = MOB[2, i - 1] * part_all
        halo_s = x_pair(S_UP, S_DOWN, SH)
        for c in halo_s:
            c.start()
        for i in layers:
            ys3[i - 1 : i] = edge(SH, 0, i)
            ys3[i + 3 : i + 4] = edge(SH, 1, i)
        halo_sy = remote(S_Y, ys3, yr3, side)
        halo_sy.start()
        for c in rest_over[0]:
            c.wait_recv()
        halo_p = x_pair(P_UP, P_DOWN, F2, False)
        for c in halo_p:
            c.start()
        ys4[...] = jnp.zeros_like(ys4)
        for i in layers:
            ys4[i - 1 : i] = edge(F2, 0, i)
        halo_py = remote(P_Y, ys4, yr4, side)
        halo_py.start()
        copies = rates_second(copies)

        halo_sy.wait()
        halo_py.wait()
        for i in layers:
            set_edges(F2, 0, i, yr4[i - 1 : i], False)
            set_edges(SH, 0, i, yr3[i - 1 : i], False)
            set_edges(SH, 1, i, yr3[i + 3 : i + 4], False)
        for c in halo_s + halo_p:
            c.wait()
        kv_on.wait()
        kv_over.wait_recv()
        for i in layers:
            z_faces(0, i, KVC[0, i - 1])

        def through(flow, shares):
            pos, neg = jnp.maximum(flow, 0.0), jnp.minimum(flow, 0.0)
            return [pos * a + neg * b for a, b in shares]

        for i in layers:
            p = F2[0, i, BODY, :]
            s = [SH[a, i, BODY, :] for a in range(2)]
            tz = TZ[0, i - 1]
            west = through(
                TX[0, i - 1] * (F2[0, i - 1, BODY, :] - p),
                [(SH[a, i - 1, BODY, :], s[a]) for a in range(2)],
            )
            east = through(
                TX[0, i] * (p - F2[0, i + 1, BODY, :]),
                [(s[a], SH[a, i + 1, BODY, :]) for a in range(2)],
            )
            south = through(
                TY[0, i - 1, LO - 1 : HI - 1] * (F2[0, i, LO - 1 : HI - 1, :] - p),
                [(SH[a, i, LO - 1 : HI - 1, :], s[a]) for a in range(2)],
            )
            north = through(
                TY[0, i - 1, LO:HI] * (p - F2[0, i, LO + 1 : HI + 1, :]),
                [(s[a], SH[a, i, LO + 1 : HI + 1, :]) for a in range(2)],
            )
            top = through(
                tz * (p - pltpu.roll(p, NZ - 1, 1)),
                [(s[a], pltpu.roll(s[a], NZ - 1, 1)) for a in range(2)],
            )
            rows = slice((i - 1) * CY, i * CY)
            rate = WD[1, rows] - WD[0, rows] * p
            inverse = reciprocal(VM[0, i - 1])
            for a in range(2):
                net = west[a] - east[a] + south[a] - north[a] + pltpu.roll(top[a], 1, 1) - top[a]
                WG[a, i - 1] = WG[a, i - 1] + (net + rate * s[a]) * inverse
        save = local(11, WG, out.at[0])
        save.start()
        last = rates_last(copies)
        save.wait()
        last.wait()


def hand_over(unknowns, sums, out, rates, held, held_sums, take, give):
    parts = [(sums.at[0], held_sums, rates.at[0], 2 * CX)]
    for f in range(2):
        for i in range(CX):
            parts.append((unknowns.at[0, f, i], held.at[f, i], out.at[0, f, i], f * CX + i))
    inward = [pltpu.make_async_copy(a, b, take.at[n]) for a, b, _, n in parts]
    outward = [pltpu.make_async_copy(b, c, give.at[n]) for _, b, c, n in parts]
    for c in inward:
        c.start()
    for a, b in zip(inward, outward):
        a.wait()
        b.start()
    for c in outward:
        c.wait()


def per_device(unk, coe, rock, table, loc, pw, wi, pp, own, slo):
    any_ = pl.BlockSpec(memory_space=pl.ANY)
    row = lambda a: a.reshape(1, PERFS)
    vm = lambda *s: pltpu.VMEM(s, F32)
    halo = (2, CX + 2, CY + 16, NZ)
    unknowns, sums = pl.pallas_call(
        body,
        out_shape=(
            jax.ShapeDtypeStruct((1, 2, CX, CY, NZ), F32),
            jax.ShapeDtypeStruct((1, 2, 128), F32),
        ),
        in_specs=[any_] * 3 + [pl.BlockSpec(memory_space=pltpu.SMEM)] + [any_] * 6,
        out_specs=(any_, any_),
        scratch_shapes=[
            vm(*halo), vm(*halo), vm(*halo), vm(*halo), vm(*halo),
            vm(2, CX, CY, NZ), vm(3, CY, NZ),
            vm(2, CX, CY, NZ),
            vm(4, CX, CY, NZ),
            pltpu.VMEM((CX, CY, NZ), jnp.int32),
            vm(2, CX + 1, CY, NZ), vm(2, CX, CY + 16, NZ), vm(2, CX, CY, NZ),
            vm(2, CX, CY, NZ), vm(2, CX, CY, NZ),
            vm(2, CX * CY, NZ),
            vm(3, CX, CY, NZ),
            pltpu.VMEM((1, PERFS), jnp.int32), pltpu.VMEM((1, PERFS), jnp.int32),
            vm(1, PERFS), vm(1, PERFS),
            pltpu.VMEM((64, 128), jnp.int32), pltpu.VMEM((64, 128), jnp.int32),
            vm(16, NZ), vm(16, NZ), vm(8, NZ), vm(8, NZ), vm(8, NZ), vm(8, NZ),
            vm(8, NZ), vm(8, NZ), vm(8, NZ), vm(8, NZ),
            vm(8, PERFS), vm(8, PERFS),
            vm(RUN, 2, PAIRS, 128), vm(RUN, 2, PAIRS, 128),
            vm(PAIRS, 8, 128), vm(PAIRS, 8, 128), vm(2, 128),
            pltpu.SemaphoreType.DMA((N_SEM,)),
            pltpu.SemaphoreType.DMA((N_SEM,)),
            pltpu.SemaphoreType.DMA((N_LOCAL,)),
        ],
        compiler_params=pltpu.CompilerParams(
            collective_id=0, has_side_effects=True, vmem_limit_bytes=60 * 2**20
        ),
    )(
        unk, coe, rock, table.T, row(loc), row(pw), row(wi), row(pp),
        own.reshape(64, 128), slo.reshape(64, 128),
    )
    return pl.pallas_call(
        hand_over,
        out_shape=(
            jax.ShapeDtypeStruct(unknowns.shape, F32),
            jax.ShapeDtypeStruct(sums.shape, F32),
        ),
        in_specs=[any_, any_],
        out_specs=(any_, any_),
        scratch_shapes=[
            vm(2, CX, CY, NZ),
            vm(2, 128),
            pltpu.SemaphoreType.DMA((2 * CX + 1,)),
            pltpu.SemaphoreType.DMA((2 * CX + 1,)),
        ],
        compiler_params=pltpu.CompilerParams(vmem_limit_bytes=60 * 2**20),
    )(unknowns, sums)


def solution(mesh):
    in_specs = (
        P("sec", None, "gx", "gy", None),
        P("sec", None, "gx", "gy", None),
        P("gx", "gy", None),
        P(),
        P(("gx", "gy")),
        P(("gx", "gy")),
        P(("gx", "gy")),
        P(("gx", "gy")),
        P(),
        P(),
    )
    out_specs = (P("sec", None, "gx", "gy", None), P("sec", None, ("gx", "gy")))
    return jax.shard_map(
        per_device, mesh=mesh, in_specs=in_specs, out_specs=out_specs, check_vma=False
    )
```

```python
import functools

import jax
import jax.numpy as jnp
from jax import lax
from jax.experimental import pallas as pl
from jax.experimental.pallas import tpu as pltpu
from jax.sharding import PartitionSpec as P

MESH = pl.DeviceIdType.MESH
F32 = jnp.float32
BF16 = jnp.bfloat16
CX, CY, NZ = 4, 64, 256
PERFS = 256
NROCK = 8
RING = 64
RUN = 16
PAIRS = 8
LINKED = 1.5

LO, HI = 8, 8 + CY
BODY = pl.ds(LO, CY)

X_UP, X_DOWN = 0, 4
Y_START = 8
KH_OVER = 60
KV_CROSS, KV_ON, KV_OVER = 10, 11, 12
X2_UP, X2_DOWN = 14, 16
Y_SECOND = 18
REST_OVER = 20
AT_OVER = 26
K_UP, K_DOWN, K_Y = 27, 28, 29
S_UP, S_DOWN, S_Y = 30, 31, 32
P_UP, P_DOWN, P_Y = 33, 34, 35
R_FIRST = 36
R_SECOND = 52
MAIN_OVER = 65
N_SEM = 67
N_LOCAL = 16


def reciprocal(x):
    r = pl.reciprocal(x, approx=True)
    return r * (2.0 - x * r)


def harmonic(a, b):
    return (2.0 * a) * (b * reciprocal(a + b))


def split(x):
    high = x.astype(BF16)
    rest = x - high.astype(F32)
    mid = rest.astype(BF16)
    low = (rest - mid.astype(F32)).astype(BF16)
    return high, mid, low


def dot_nt(a, b):
    return lax.dot_general(a, b, (((1,), (1,)), ((), ())), preferred_element_type=F32)


def dot_nn(a, b):
    return lax.dot_general(a, b, (((1,), (0,)), ((), ())), preferred_element_type=F32)


def hot(index, rows):
    return lax.broadcasted_iota(jnp.int32, (rows, PERFS), 0) == index


def as_bf16(mask):
    return jnp.where(mask, 1.0, 0.0).astype(BF16)


def spread(row_hot, col_mask, value):
    total = None
    for piece in split(value):
        term = dot_nt(row_hot, jnp.where(col_mask, piece.astype(F32), 0.0).astype(BF16))
        total = term if total is None else total + term
    return total


def pick(field, row_mask, col_hot):
    total = None
    for piece in split(field):
        term = dot_nn(piece, col_hot)
        total = term if total is None else total + term
    return jnp.sum(jnp.where(row_mask, total, 0.0), axis=0, keepdims=True)


def body(
    unk, coe, rock, table, loc, pw, wi, pp, own, slo,
    out, rates,
    F0, F1, F2, T0, SH, KVC, RL, WG, VM, RK, TX, TY, TZ, INV, BASE, WD, MOB,
    s_loc, s_pw, s_wi, s_pp, s_own, s_slo,
    ys0, yr0, ys1, yr1, ys2, yr2, ys3, yr3, ys4, yr4, ats, atr,
    part, got1, part2, got2, rate_buf,
    send, recv, lsem,
):
    sec, gx, gy = (lax.axis_index(a) for a in ("sec", "gx", "gy"))
    up = (sec, lax.rem(gx + 1, RING), gy)
    down = (sec, lax.rem(gx + RING - 1, RING), gy)
    side = (sec, gx, 1 - gy)
    other = (1 - sec, gx, gy)
    cross = (1 - sec, gx, 1 - gy)
    zc, y = lax.rem(gx, RUN), gx // RUN
    core = lax.rem(gx, 2)
    mate = (sec, gx + 1 - 2 * core, gy)
    far = (sec, lax.rem(gx + RING - 1 + 2 * core, RING), gy)
    near_far, near_mate = 1 + (CX - 1) * core, CX - (CX - 1) * core
    halo_far, halo_mate = (CX + 1) * core, (CX + 1) * (1 - core)
    others = 2 - core
    pair = y * 2 + gy
    first = [(sec, y * RUN + lax.rem(zc + d, RUN), gy) for d in range(1, RUN)]
    second = []
    for d in range(1, PAIRS):
        q = lax.rem(pair + d, PAIRS)
        second.append((sec, (q // 2) * RUN + zc, lax.rem(q, 2)))

    barrier = pltpu.get_barrier_semaphore()
    partners = [up, down, side, other, cross] + first + second
    for dev in partners:
        pl.semaphore_signal(barrier, inc=1, device_id=dev, device_id_type=MESH)

    def local(i, src, dst):
        return pltpu.make_async_copy(src, dst, lsem.at[i])

    def remote(i, src, dst, dev):
        return pltpu.make_async_remote_copy(
            src_ref=src,
            dst_ref=dst,
            send_sem=send.at[i],
            recv_sem=recv.at[i],
            device_id=dev,
            device_id_type=MESH,
        )

    small = [
        local(0, loc, s_loc),
        local(1, pw, s_pw),
        local(2, wi, s_wi),
        local(3, pp, s_pp),
        local(4, own, s_own),
        local(5, slo, s_slo),
    ]
    for c in small:
        c.start()
    loads0 = [
        local(6, unk.at[0], F0.at[:, pl.ds(1, CX), BODY, :]),
        local(7, coe.at[0, 0], T0.at[0, pl.ds(1, CX), BODY, :]),
        local(8, coe.at[0, 3], T0.at[1, pl.ds(1, CX), BODY, :]),
        local(9, coe.at[0, pl.ds(1, 2)], KVC),
    ]
    loads1 = [local(6, unk.at[0], WG), local(7, coe.at[0], VM), local(8, rock, RK)]

    def wells():
        for c in small:
            c.wait()
        place = s_loc[...]
        row, col = lax.shift_right_logical(place, 8), jnp.bitwise_and(place, 255)
        row_mask, col_mask = hot(row, PERFS), hot(col, PERFS)
        row_hot, col_hot = as_bf16(row_mask), as_bf16(col_mask)
        live = s_pw[...] >= 0
        index = jnp.where(live, s_wi[...], 0.0)
        WD[0] = spread(row_hot, col_mask, index)
        WD[1] = spread(row_hot, col_mask, index * s_pp[...])
        well = jnp.maximum(s_pw[...], 0)
        w_row = hot(lax.shift_right_logical(well, 7), 64)
        w_col = as_bf16(hot(jnp.bitwise_and(well, 127), 128))

        def look(ref):
            found = dot_nn(ref[...].astype(F32).astype(BF16), w_col)
            return jnp.sum(jnp.where(w_row, found, 0.0), axis=0, keepdims=True).astype(jnp.int32)

        owner, slot = look(s_own), look(s_slo)
        o_gx, o_gy = lax.shift_right_logical(owner, 1), jnp.bitwise_and(owner, 1)
        order = (
            jnp.bitwise_and(o_gx, RUN - 1) * PAIRS + lax.shift_right_logical(o_gx, 4) * 2 + o_gy
        )
        return row_mask, col_hot, index, order, slot

    def rates_first(values, order, slot):
        own_mask, slot_hot = hot(order, RUN * PAIRS), as_bf16(hot(slot, 128))
        for a, value in enumerate(values):
            total = None
            for piece in split(value):
                lhs = jnp.where(own_mask, piece.astype(F32), 0.0).astype(BF16)
                term = dot_nt(lhs, slot_hot)
                total = term if total is None else total + term
            part[:, a] = total.reshape(RUN, PAIRS, 128)
        copies = [
            remote(R_FIRST + d, part.at[lax.rem(zc + d, RUN)], got1.at[d], first[d - 1])
            for d in far_first(RUN)
        ]
        for c in copies:
            c.start()
        return copies

    def rates_second(copies):
        for c in copies:
            c.wait()
        total = part[zc]
        for d in range(1, RUN):
            total = total + got1[d]
        part2[...] = jnp.zeros_like(part2)
        for a in range(2):
            for q in range(PAIRS):
                part2[q, a : a + 1] = total[a, q : q + 1]
        copies = [
            remote(R_SECOND + d, part2.at[lax.rem(pair + d, PAIRS)], got2.at[d], second[d - 1])
            for d in range(1, PAIRS)
        ]
        for c in copies:
            c.start()
        return copies

    def rates_last(copies):
        for c in copies:
            c.wait()
        total = part2[pair]
        for d in range(1, PAIRS):
            total = total + got2[d]
        rate_buf[...] = total[0:2]
        c = local(10, rate_buf, rates.at[0])
        c.start()
        return c

    def edge(ref, f, i):
        return jnp.where(gy == 0, ref[f, i, HI - 1 : HI, :], ref[f, i, LO : LO + 1, :])

    def set_edges(ref, f, i, row, zero):
        if zero:
            ref[f, i, HI : HI + 1, :] = jnp.where(gy == 0, row, 0.0)
            ref[f, i, LO - 1 : LO, :] = jnp.where(gy == 1, row, 0.0)
        else:
            ref[f, i, HI : HI + 1, :] = row
            ref[f, i, LO - 1 : LO, :] = row

    def x_face(f, a):
        outside = jnp.logical_or(
            jnp.logical_and(gx == 0, a == 0), jnp.logical_and(gx == RING - 1, a == CX)
        )
        face = harmonic(T0[f, a, BODY, :], T0[f, a + 1, BODY, :])
        TX[f, a] = jnp.where(outside, 0.0, face)

    def y_faces(f, i):
        TY[f, i - 1, LO : HI - 1] = harmonic(T0[f, i, LO : HI - 1, :], T0[f, i, LO + 1 : HI, :])

    def y_ends(f, i):
        for r in (LO - 1, HI - 1):
            TY[f, i - 1, r : r + 1] = harmonic(T0[f, i, r : r + 1, :], T0[f, i, r + 1 : r + 2, :])

    def z_faces(f, i, value):
        lane = lax.broadcasted_iota(jnp.int32, (CY, NZ), 1)
        face = harmonic(value, pltpu.roll(value, NZ - 1, 1))
        TZ[f, i - 1] = jnp.where(lane == NZ - 1, 0.0, face)

    def system(f, i, start):
        c = KVC[1, i - 1]
        tz = TZ[f, i - 1]
        total = (
            c + TX[f, i - 1] + TX[f, i] + TY[f, i - 1, LO - 1 : HI - 1] + TY[f, i - 1, LO:HI]
            + tz + pltpu.roll(tz, 1, 1)
        )
        base = c * start[f, i, BODY, :]
        if f == 0:
            rows = pl.ds((i - 1) * CY if isinstance(i, int) else pl.multiple_of((i - 1) * CY, CY), CY)
            total = total + WD[0, rows]
            base = base + WD[1, rows]
        INV[f, i - 1] = reciprocal(total)
        BASE[f, i - 1] = base

    def sweep(f, i, now, later):
        tz = TZ[f, i - 1]
        centre = now[f, i, BODY, :]
        total = (
            BASE[f, i - 1]
            + TX[f, i - 1] * now[f, i - 1, BODY, :]
            + TX[f, i] * now[f, i + 1, BODY, :]
            + TY[f, i - 1, LO - 1 : HI - 1] * now[f, i, LO - 1 : HI - 1, :]
            + TY[f, i - 1, LO:HI] * now[f, i, LO + 1 : HI + 1, :]
            + tz * pltpu.roll(centre, NZ - 1, 1)
            + pltpu.roll(tz * centre, 1, 1)
        )
        later[f, i, BODY, :] = total * INV[f, i - 1]

    def far_first(n):
        return sorted(range(1, n), key=lambda d: -min(d, n - d))

    def x_pair(i_up, i_down, ref, both=True, f=0):
        pick_ = (lambda a: ref.at[:, a, BODY, :]) if both else (lambda a: ref.at[f, a, BODY, :])
        return [
            remote(i_up, pick_(CX), pick_(0), up),
            remote(i_down, pick_(1), pick_(CX + 1), down),
        ]

    kh_over = [
        remote(KH_OVER + i, coe.at[0, 0, i - 1], T0.at[0, i, BODY, :], other) for i in (1, CX, 2)
    ]
    kh_last = remote(KH_OVER + 3, coe.at[0, 0, 2], T0.at[0, 3, BODY, :], other)
    kh_edges = remote(K_Y, yr0.at[pl.ds(8, 8)], yr2, other)
    halves = [pl.ds(0, 3), pl.ds(3, 1)]
    kv_cross = remote(KV_CROSS, coe.at[0, 1, halves[0]], RL, cross)
    kv_on = remote(KV_ON, RL, KVC.at[0, halves[0]], side)
    kv_over = remote(KV_OVER, coe.at[0, 1, halves[1]], KVC.at[0, halves[1]], other)
    main_rows = pl.ds(pl.multiple_of(LO + 8 * gy, 8), CY - 8)
    edge_rows = pl.ds(pl.multiple_of(HI - 8 - (CY - 8) * gy, 8), 8)
    inner = [F2.at[f, pl.ds(others, 3), main_rows, :] for f in range(2)]
    main_over = [remote(MAIN_OVER + f, v, v, other) for f, v in enumerate(inner)]
    rest_over = []
    for f in range(2):
        views = [F2.at[f, near_far, BODY, :], F2.at[f, pl.ds(others, 3), edge_rows, :]]
        rest_over.append(
            [remote(REST_OVER + 3 * f + n, v, v, other) for n, v in enumerate(views)]
        )
    at_over = remote(AT_OVER, ats, atr, other)
    layers = range(1, CX + 1)

    @pl.when(sec == 0)
    def _():
        for c in loads0:
            c.start()
        for c in loads0:
            c.wait()
        for f in range(2):
            for i in layers:
                r = f * CX + i - 1
                ys0[r : r + 1] = edge(F0, f, i)
                ys0[r + 8 : r + 9] = edge(T0, f, i)
        pl.semaphore_wait(barrier, len(partners))
        halo_y = remote(Y_START, ys0, yr0, side)
        halo_y.start()
        halo_far_x, halo_mate_x = [], []
        for f in range(2):
            for s, dev, src, dst, group in (
                (X_UP, far, near_far, halo_mate, halo_far_x),
                (X_DOWN, mate, near_mate, halo_far, halo_mate_x),
            ):
                pair_ = [
                    remote(s + 2 * f, unk.at[0, f, src - 1], F0.at[f, dst, BODY, :], dev),
                    remote(s + 2 * f + 1, coe.at[0, 3 * f, src - 1], T0.at[f, dst, BODY, :], dev),
                ]
                for c in pair_:
                    c.start()
                group.append(pair_)
        for c in kh_over:
            c.start()
        kv_cross.start()
        for f in range(2):
            for i in layers:
                z_faces(f, i, KVC[0, i - 1] if f == 0 else T0[1, i, BODY, :])
                y_faces(f, i)
            for a in range(1, CX):
                x_face(f, a)
        row_mask, col_hot, index, order, slot = wells()
        halo_y.wait()
        kh_edges.start()
        for f in range(2):
            for i in layers:
                r = f * CX + i - 1
                set_edges(F0, f, i, yr0[r : r + 1], False)
                set_edges(T0, f, i, yr0[r + 8 : r + 9], True)
                y_ends(f, i)
                F1[f, i, HI : HI + 1, :] = jnp.zeros((1, NZ), F32)
                F1[f, i, LO - 1 : LO, :] = jnp.zeros((1, NZ), F32)
            for i in (2, 3):
                system(f, i, F0)
                sweep(f, i, F0, F1)
        for f in range(2):
            for c in halo_mate_x[f]:
                c.wait()
            x_face(f, CX * (1 - core))
            system(f, near_mate, F0)
            sweep(f, near_mate, F0, F1)
        mate_x2 = remote(X2_DOWN, F1.at[:, near_mate, BODY, :], F1.at[:, halo_far, BODY, :], mate)
        mate_x2.start()
        far_x2 = []
        for f in (1, 0):
            for c in halo_far_x[f]:
                c.wait()
            x_face(f, CX * core)
            system(f, near_far, F0)
            sweep(f, near_far, F0, F1)
            c = remote(
                X2_UP + f, F1.at[f, near_far, BODY, :], F1.at[f, halo_mate, BODY, :], far
            )
            c.start()
            far_x2.append(c)
        for f in range(2):
            for i in layers:
                r = f * CX + i - 1
                ys1[r : r + 1] = edge(F1, f, i)
        halo_y = remote(Y_SECOND, ys1, yr1, side)
        halo_y.start()
        mate_x2.wait()
        for f in (1, 0):
            for k in range(3):
                sweep(f, others + k, F1, F2)
            if f == 1:
                main_over[1].start()
                kh_last.start()
        halo_y.wait()
        for at, r, t in ((0, HI - 1, HI - 1), (1, LO, LO - 1)):

            @pl.when(gy == at)
            def _(r=r, t=t):
                for f in range(2):
                    for k in range(3):
                        i = others + k
                        n = f * CX + i - 1
                        more = TY[f, i - 1, t : t + 1] * INV[f, i - 1, r - LO : r - LO + 1]
                        row = yr1[pl.ds(n, 1)]
                        F2[f, i, r : r + 1, :] = F2[f, i, r : r + 1, :] + more * row

        for f, c in zip((1, 0), far_x2):
            set_edges(F1, f, near_far, yr1[pl.ds(f * CX + near_far - 1, 1)], False)
            c.wait()
            sweep(f, near_far, F1, F2)
        pressure = pick(F2[0, 1 : CX + 1, BODY, :].reshape(CX * CY, NZ), row_mask, col_hot)
        warmth = pick(F2[1, 1 : CX + 1, BODY, :].reshape(CX * CY, NZ), row_mask, col_hot)
        ats[...] = jnp.zeros_like(ats)
        ats[0:1] = pressure
        ats[1:2] = warmth
        at_over.start()
        for c in rest_over[1] + rest_over[0]:
            c.start()
        main_over[0].start()
        kv_over.start()
        save = local(11, F2.at[:, pl.ds(1, CX), BODY, :], out.at[0])
        save.start()
        q = index * (s_pp[...] - pressure)
        copies = rates_first((q, q * warmth), order, slot)
        copies = rates_second(copies)
        last = rates_last(copies)
        for c in kh_over + main_over + [kh_last, kh_edges, kv_cross, kv_over, at_over] + rest_over[0] + rest_over[1]:
            c.wait_send()
        save.wait()
        last.wait()

    @pl.when(sec == 1)
    def _():
        for c in loads1:
            c.start()
        pl.semaphore_wait(barrier, len(partners))
        for c in loads1:
            c.wait()
        for i in range(CX):
            kind = RK[i]
            ends = []
            masks = [kind == t for t in range(1, NROCK)]
            for k in range(3):
                e = jnp.full((CY, NZ), table[k, 0], F32)
                for t in range(1, NROCK):
                    e = jnp.where(masks[t - 1], table[k, t], e)
                ends.append(e)
            water, gas = WG[0, i], WG[1, i]
            oil = 1.0 - water - gas
            MOB[0, i] = ends[0] * water * water * reciprocal(VM[1, i])
            MOB[1, i] = ends[1] * oil * oil * reciprocal(VM[2, i])
            MOB[2, i] = ends[2] * gas * gas * reciprocal(VM[3, i])
        kv_cross.wait_recv()
        kv_on.start()
        row_mask, col_hot, index, order, slot = wells()
        lw, lo, lg = (pick(MOB[k].reshape(CX * CY, NZ), row_mask, col_hot) for k in range(3))

        for c in kh_over:
            c.wait_recv()
        halo_k = x_pair(K_UP, K_DOWN, T0, False)
        for c in halo_k:
            c.start()
        for i in (1, CX, 2):
            y_faces(0, i)
        x_face(0, 1)
        kh_edges.wait_recv()
        for i in layers:
            set_edges(T0, 0, i, yr2[i - 1 : i], True)
        for i in (1, CX, 2):
            y_ends(0, i)
        kh_last.wait_recv()
        for a in (2, 3):
            x_face(0, a)
        y_faces(0, 3)
        y_ends(0, 3)
        for c in halo_k:
            c.wait()
        for a in (0, CX):
            x_face(0, a)

        at_over.wait_recv()
        q = index * (s_pp[...] - atr[0:1])
        lo = lo * jnp.exp(LINKED * (atr[1:2] - 1.0))
        scaled = q * reciprocal(lw + lo + lg)
        copies = rates_first((scaled * lw, scaled * lg), order, slot)
        for c in rest_over[1] + main_over[1:]:
            c.wait_recv()
        for i in (1, 4, 2, 3):
            other_mob = MOB[1, i - 1] * jnp.exp(LINKED * (F2[1, i, BODY, :] - 1.0))
            part_all = reciprocal(MOB[0, i - 1] + other_mob + MOB[2, i - 1])
            SH[0, i, BODY, :] = MOB[0, i - 1] * part_all
            SH[1, i, BODY, :] = MOB[2, i - 1] * part_all
        halo_s = x_pair(S_UP, S_DOWN, SH)
        for c in halo_s:
            c.start()
        for i in layers:
            ys3[i - 1 : i] = edge(SH, 0, i)
            ys3[i + 3 : i + 4] = edge(SH, 1, i)
        halo_sy = remote(S_Y, ys3, yr3, side)
        halo_sy.start()
        for c in rest_over[0]:
            c.wait_recv()
        far_p = remote(
            P_UP, F2.at[0, near_far, BODY, :], F2.at[0, halo_mate, BODY, :], far
        )
        far_p.start()
        ys4[...] = jnp.zeros_like(ys4)
        for at, r in ((0, HI - 1), (1, LO)):

            @pl.when(gy == at)
            def _(r=r):
                for i in layers:
                    ys4[i - 1 : i] = F2[0, i, r : r + 1, :]

        halo_py = remote(P_Y, ys4, yr4, side)
        halo_py.start()
        copies = rates_second(copies)

        halo_sy.wait()
        halo_py.wait()
        for i in layers:
            set_edges(F2, 0, i, yr4[i - 1 : i], False)
            set_edges(SH, 0, i, yr3[i - 1 : i], False)
            set_edges(SH, 1, i, yr3[i + 3 : i + 4], False)
        main_over[0].wait_recv()
        mate_p = remote(
            P_DOWN, F2.at[0, near_mate, BODY, :], F2.at[0, halo_far, BODY, :], mate
        )
        mate_p.start()
        for c in halo_s + [far_p]:
            c.wait()
        kv_on.wait()
        kv_over.wait_recv()
        for i in layers:
            z_faces(0, i, KVC[0, i - 1])
        mate_p.wait()

        def through(flow, shares):
            pos, neg = jnp.maximum(flow, 0.0), jnp.minimum(flow, 0.0)
            return [pos * a + neg * b for a, b in shares]

        for i in layers:
            p = F2[0, i, BODY, :]
            s = [SH[a, i, BODY, :] for a in range(2)]
            tz = TZ[0, i - 1]
            west = through(
                TX[0, i - 1] * (F2[0, i - 1, BODY, :] - p),
                [(SH[a, i - 1, BODY, :], s[a]) for a in range(2)],
            )
            east = through(
                TX[0, i] * (p - F2[0, i + 1, BODY, :]),
                [(s[a], SH[a, i + 1, BODY, :]) for a in range(2)],
            )
            south = through(
                TY[0, i - 1, LO - 1 : HI - 1] * (F2[0, i, LO - 1 : HI - 1, :] - p),
                [(SH[a, i, LO - 1 : HI - 1, :], s[a]) for a in range(2)],
            )
            north = through(
                TY[0, i - 1, LO:HI] * (p - F2[0, i, LO + 1 : HI + 1, :]),
                [(s[a], SH[a, i, LO + 1 : HI + 1, :]) for a in range(2)],
            )
            top = through(
                tz * (p - pltpu.roll(p, NZ - 1, 1)),
                [(s[a], pltpu.roll(s[a], NZ - 1, 1)) for a in range(2)],
            )
            rows = slice((i - 1) * CY, i * CY)
            rate = WD[1, rows] - WD[0, rows] * p
            inverse = reciprocal(VM[0, i - 1])
            for a in range(2):
                net = west[a] - east[a] + south[a] - north[a] + pltpu.roll(top[a], 1, 1) - top[a]
                WG[a, i - 1] = WG[a, i - 1] + (net + rate * s[a]) * inverse
        save = local(11, WG, out.at[0])
        save.start()
        last = rates_last(copies)
        save.wait()
        last.wait()


def hand_over(unknowns, sums, out, rates, held, held_sums, take, give):
    parts = [(sums.at[0], held_sums, rates.at[0], 2 * CX)]
    for f in range(2):
        for i in range(CX):
            parts.append((unknowns.at[0, f, i], held.at[f, i], out.at[0, f, i], f * CX + i))
    inward = [pltpu.make_async_copy(a, b, take.at[n]) for a, b, _, n in parts]
    outward = [pltpu.make_async_copy(b, c, give.at[n]) for _, b, c, n in parts]
    for c in inward:
        c.start()
    for a, b in zip(inward, outward):
        a.wait()
        b.start()
    for c in outward:
        c.wait()


def per_device(unk, coe, rock, table, loc, pw, wi, pp, own, slo):
    any_ = pl.BlockSpec(memory_space=pl.ANY)
    row = lambda a: a.reshape(1, PERFS)
    vm = lambda *s: pltpu.VMEM(s, F32)
    halo = (2, CX + 2, CY + 16, NZ)
    unknowns, sums = pl.pallas_call(
        body,
        out_shape=(
            jax.ShapeDtypeStruct((1, 2, CX, CY, NZ), F32),
            jax.ShapeDtypeStruct((1, 2, 128), F32),
        ),
        in_specs=[any_] * 3 + [pl.BlockSpec(memory_space=pltpu.SMEM)] + [any_] * 6,
        out_specs=(any_, any_),
        scratch_shapes=[
            vm(*halo), vm(*halo), vm(*halo), vm(*halo), vm(*halo),
            vm(2, CX, CY, NZ), vm(3, CY, NZ),
            vm(2, CX, CY, NZ),
            vm(4, CX, CY, NZ),
            pltpu.VMEM((CX, CY, NZ), jnp.int32),
            vm(2, CX + 1, CY, NZ), vm(2, CX, CY + 16, NZ), vm(2, CX, CY, NZ),
            vm(2, CX, CY, NZ), vm(2, CX, CY, NZ),
            vm(2, CX * CY, NZ),
            vm(3, CX, CY, NZ),
            pltpu.VMEM((1, PERFS), jnp.int32), pltpu.VMEM((1, PERFS), jnp.int32),
            vm(1, PERFS), vm(1, PERFS),
            pltpu.VMEM((64, 128), jnp.int32), pltpu.VMEM((64, 128), jnp.int32),
            vm(16, NZ), vm(16, NZ), vm(8, NZ), vm(8, NZ), vm(8, NZ), vm(8, NZ),
            vm(8, NZ), vm(8, NZ), vm(8, NZ), vm(8, NZ),
            vm(8, PERFS), vm(8, PERFS),
            vm(RUN, 2, PAIRS, 128), vm(RUN, 2, PAIRS, 128),
            vm(PAIRS, 8, 128), vm(PAIRS, 8, 128), vm(2, 128),
            pltpu.SemaphoreType.DMA((N_SEM,)),
            pltpu.SemaphoreType.DMA((N_SEM,)),
            pltpu.SemaphoreType.DMA((N_LOCAL,)),
        ],
        compiler_params=pltpu.CompilerParams(
            collective_id=0, has_side_effects=True, vmem_limit_bytes=60 * 2**20
        ),
    )(
        unk, coe, rock, table.T, row(loc), row(pw), row(wi), row(pp),
        own.reshape(64, 128), slo.reshape(64, 128),
    )
    return pl.pallas_call(
        hand_over,
        out_shape=(
            jax.ShapeDtypeStruct(unknowns.shape, F32),
            jax.ShapeDtypeStruct(sums.shape, F32),
        ),
        in_specs=[any_, any_],
        out_specs=(any_, any_),
        scratch_shapes=[
            vm(2, CX, CY, NZ),
            vm(2, 128),
            pltpu.SemaphoreType.DMA((2 * CX + 1,)),
            pltpu.SemaphoreType.DMA((2 * CX + 1,)),
        ],
        compiler_params=pltpu.CompilerParams(vmem_limit_bytes=60 * 2**20),
    )(unknowns, sums)


def solution(mesh):
    in_specs = (
        P("sec", None, "gx", "gy", None),
        P("sec", None, "gx", "gy", None),
        P("gx", "gy", None),
        P(),
        P(("gx", "gy")),
        P(("gx", "gy")),
        P(("gx", "gy")),
        P(("gx", "gy")),
        P(),
        P(),
    )
    out_specs = (P("sec", None, "gx", "gy", None), P("sec", None, ("gx", "gy")))
    return jax.shard_map(
        per_device, mesh=mesh, in_specs=in_specs, out_specs=out_specs, check_vma=False
    )
```

```python
import functools

import jax
import jax.numpy as jnp
from jax import lax
from jax.experimental import pallas as pl
from jax.experimental.pallas import tpu as pltpu
from jax.sharding import PartitionSpec as P

MESH = pl.DeviceIdType.MESH
F32 = jnp.float32
BF16 = jnp.bfloat16
CX, CY, NZ = 4, 64, 256
PERFS = 256
NROCK = 8
RING = 64
RUN = 16
PAIRS = 8
LINKED = 1.5

LO, HI = 8, 8 + CY
BODY = pl.ds(LO, CY)

X_UP, X_DOWN = 0, 4
Y_START = 8
KH_OVER = 60
KV_CROSS, KV_ON, KV_OVER = 10, 11, 12
X2_UP, X2_DOWN = 14, 16
Y_SECOND = 18
REST_OVER = 20
AT_OVER = 26
K_UP, K_DOWN, K_Y = 27, 28, 29
S_UP, S_DOWN, S_Y = 30, 31, 32
P_UP, P_DOWN, P_Y = 33, 34, 35
R_FIRST = 36
R_SECOND = 52
MAIN_OVER = 65
N_SEM = 67
N_LOCAL = 16


def reciprocal(x):
    r = pl.reciprocal(x, approx=True)
    return r * (2.0 - x * r)


def harmonic(a, b):
    return (2.0 * a) * (b * reciprocal(a + b))


def split(x):
    high = x.astype(BF16)
    rest = x - high.astype(F32)
    mid = rest.astype(BF16)
    low = (rest - mid.astype(F32)).astype(BF16)
    return high, mid, low


def dot_nt(a, b):
    return lax.dot_general(a, b, (((1,), (1,)), ((), ())), preferred_element_type=F32)


def dot_nn(a, b):
    return lax.dot_general(a, b, (((1,), (0,)), ((), ())), preferred_element_type=F32)


def hot(index, rows):
    return lax.broadcasted_iota(jnp.int32, (rows, PERFS), 0) == index


def as_bf16(mask):
    return jnp.where(mask, 1.0, 0.0).astype(BF16)


def spread(row_hot, col_mask, value):
    total = None
    for piece in split(value):
        term = dot_nt(row_hot, jnp.where(col_mask, piece.astype(F32), 0.0).astype(BF16))
        total = term if total is None else total + term
    return total


def pick(fields, row_mask, col_hot):
    found = dot_nn(jnp.concatenate([p for field in fields for p in split(field)], axis=0), col_hot)
    rows = []
    for k in range(len(fields)):
        a, b, c = (found[(3 * k + n) * PERFS : (3 * k + n + 1) * PERFS] for n in range(3))
        rows.append(jnp.sum(jnp.where(row_mask, a + b + c, 0.0), axis=0, keepdims=True))
    return rows


def body(
    unk, coe, rock, table, loc, pw, wi, pp, own, slo,
    out, rates,
    F0, F1, F2, T0, SH, KVC, RL, WG, VM, RK, TX, TY, TZ, INV, BASE, WD, MOB,
    s_loc, s_pw, s_wi, s_pp, s_own, s_slo,
    ys0, yr0, ys1, yr1, ys2, yr2, ys3, yr3, ys4, yr4, ats, atr,
    part, got1, part2, got2, rate_buf,
    send, recv, lsem,
):
    sec, gx, gy = (lax.axis_index(a) for a in ("sec", "gx", "gy"))
    up = (sec, lax.rem(gx + 1, RING), gy)
    down = (sec, lax.rem(gx + RING - 1, RING), gy)
    side = (sec, gx, 1 - gy)
    other = (1 - sec, gx, gy)
    cross = (1 - sec, gx, 1 - gy)
    zc, y = lax.rem(gx, RUN), gx // RUN
    core = lax.rem(gx, 2)
    mate = (sec, gx + 1 - 2 * core, gy)
    far = (sec, lax.rem(gx + RING - 1 + 2 * core, RING), gy)
    near_far, near_mate = 1 + (CX - 1) * core, CX - (CX - 1) * core
    halo_far, halo_mate = (CX + 1) * core, (CX + 1) * (1 - core)
    others = 2 - core
    pair = y * 2 + gy
    first = [(sec, y * RUN + lax.rem(zc + d, RUN), gy) for d in range(1, RUN)]
    second = []
    for d in range(1, PAIRS):
        q = lax.rem(pair + d, PAIRS)
        second.append((sec, (q // 2) * RUN + zc, lax.rem(q, 2)))

    barrier = pltpu.get_barrier_semaphore()
    partners = [up, down, side, other, cross] + first + second
    for dev in partners:
        pl.semaphore_signal(barrier, inc=1, device_id=dev, device_id_type=MESH)

    def local(i, src, dst):
        return pltpu.make_async_copy(src, dst, lsem.at[i])

    def remote(i, src, dst, dev):
        return pltpu.make_async_remote_copy(
            src_ref=src,
            dst_ref=dst,
            send_sem=send.at[i],
            recv_sem=recv.at[i],
            device_id=dev,
            device_id_type=MESH,
        )

    small = [
        local(0, loc, s_loc),
        local(1, pw, s_pw),
        local(2, wi, s_wi),
        local(3, pp, s_pp),
        local(4, own, s_own),
        local(5, slo, s_slo),
    ]
    for c in small:
        c.start()
    loads0 = [
        local(6, unk.at[0], F0.at[:, pl.ds(1, CX), BODY, :]),
        local(7, coe.at[0, 0], T0.at[0, pl.ds(1, CX), BODY, :]),
        local(8, coe.at[0, 3], T0.at[1, pl.ds(1, CX), BODY, :]),
        local(9, coe.at[0, pl.ds(1, 2)], KVC),
    ]
    loads1 = [local(6, unk.at[0], WG), local(7, coe.at[0], VM), local(8, rock, RK)]

    def wells():
        for c in small:
            c.wait()
        place = s_loc[...]
        row, col = lax.shift_right_logical(place, 8), jnp.bitwise_and(place, 255)
        row_mask, col_mask = hot(row, PERFS), hot(col, PERFS)
        row_hot, col_hot = as_bf16(row_mask), as_bf16(col_mask)
        live = s_pw[...] >= 0
        index = jnp.where(live, s_wi[...], 0.0)
        WD[0] = spread(row_hot, col_mask, index)
        WD[1] = spread(row_hot, col_mask, index * s_pp[...])
        well = jnp.maximum(s_pw[...], 0)
        w_row = hot(lax.shift_right_logical(well, 7), 64)
        w_col = as_bf16(hot(jnp.bitwise_and(well, 127), 128))

        def look(ref):
            found = dot_nn(ref[...].astype(F32).astype(BF16), w_col)
            return jnp.sum(jnp.where(w_row, found, 0.0), axis=0, keepdims=True).astype(jnp.int32)

        owner, slot = look(s_own), look(s_slo)
        o_gx, o_gy = lax.shift_right_logical(owner, 1), jnp.bitwise_and(owner, 1)
        order = (
            jnp.bitwise_and(o_gx, RUN - 1) * PAIRS + lax.shift_right_logical(o_gx, 4) * 2 + o_gy
        )
        return row_mask, col_hot, index, order, slot

    def rates_first(values, order, slot):
        own_mask, slot_hot = hot(order, RUN * PAIRS), as_bf16(hot(slot, 128))
        lhs = [
            jnp.where(own_mask, piece.astype(F32), 0.0).astype(BF16)
            for value in values
            for piece in split(value)
        ]
        found = dot_nt(jnp.concatenate(lhs, axis=0), slot_hot)
        size = RUN * PAIRS
        for a in range(2):
            u, v, w = (found[(3 * a + n) * size : (3 * a + n + 1) * size] for n in range(3))
            part[:, a] = (u + v + w).reshape(RUN, PAIRS, 128)
        copies = [
            remote(R_FIRST + d, part.at[lax.rem(zc + d, RUN)], got1.at[d], first[d - 1])
            for d in far_first(RUN)
        ]
        for c in copies:
            c.start()
        return copies

    def rates_second(copies):
        for c in copies:
            c.wait()
        total = part[zc]
        for d in range(1, RUN):
            total = total + got1[d]
        part2[...] = jnp.zeros_like(part2)
        for a in range(2):
            for q in range(PAIRS):
                part2[q, a : a + 1] = total[a, q : q + 1]
        copies = [
            remote(R_SECOND + d, part2.at[lax.rem(pair + d, PAIRS)], got2.at[d], second[d - 1])
            for d in range(1, PAIRS)
        ]
        for c in copies:
            c.start()
        return copies

    def rates_last(copies):
        for c in copies:
            c.wait()
        total = part2[pair]
        for d in range(1, PAIRS):
            total = total + got2[d]
        rate_buf[...] = total[0:2]
        c = local(10, rate_buf, rates.at[0])
        c.start()
        return c

    def edge(ref, f, i):
        return jnp.where(gy == 0, ref[f, i, HI - 1 : HI, :], ref[f, i, LO : LO + 1, :])

    def set_edges(ref, f, i, row, zero):
        if zero:
            ref[f, i, HI : HI + 1, :] = jnp.where(gy == 0, row, 0.0)
            ref[f, i, LO - 1 : LO, :] = jnp.where(gy == 1, row, 0.0)
        else:
            ref[f, i, HI : HI + 1, :] = row
            ref[f, i, LO - 1 : LO, :] = row

    def x_face(f, a):
        outside = jnp.logical_or(
            jnp.logical_and(gx == 0, a == 0), jnp.logical_and(gx == RING - 1, a == CX)
        )
        face = harmonic(T0[f, a, BODY, :], T0[f, a + 1, BODY, :])
        TX[f, a] = jnp.where(outside, 0.0, face)

    def y_faces(f, i):
        TY[f, i - 1, LO : HI - 1] = harmonic(T0[f, i, LO : HI - 1, :], T0[f, i, LO + 1 : HI, :])

    def y_ends(f, i):
        for r in (LO - 1, HI - 1):
            TY[f, i - 1, r : r + 1] = harmonic(T0[f, i, r : r + 1, :], T0[f, i, r + 1 : r + 2, :])

    def z_faces(f, i, value):
        lane = lax.broadcasted_iota(jnp.int32, (CY, NZ), 1)
        face = harmonic(value, pltpu.roll(value, NZ - 1, 1))
        TZ[f, i - 1] = jnp.where(lane == NZ - 1, 0.0, face)

    def system(f, i, start):
        c = KVC[1, i - 1]
        tz = TZ[f, i - 1]
        total = (
            c + TX[f, i - 1] + TX[f, i] + TY[f, i - 1, LO - 1 : HI - 1] + TY[f, i - 1, LO:HI]
            + tz + pltpu.roll(tz, 1, 1)
        )
        base = c * start[f, i, BODY, :]
        if f == 0:
            rows = pl.ds((i - 1) * CY if isinstance(i, int) else pl.multiple_of((i - 1) * CY, CY), CY)
            total = total + WD[0, rows]
            base = base + WD[1, rows]
        INV[f, i - 1] = reciprocal(total)
        BASE[f, i - 1] = base

    def sweep(f, i, now, later):
        tz = TZ[f, i - 1]
        centre = now[f, i, BODY, :]
        total = (
            BASE[f, i - 1]
            + TX[f, i - 1] * now[f, i - 1, BODY, :]
            + TX[f, i] * now[f, i + 1, BODY, :]
            + TY[f, i - 1, LO - 1 : HI - 1] * now[f, i, LO - 1 : HI - 1, :]
            + TY[f, i - 1, LO:HI] * now[f, i, LO + 1 : HI + 1, :]
            + tz * pltpu.roll(centre, NZ - 1, 1)
            + pltpu.roll(tz * centre, 1, 1)
        )
        later[f, i, BODY, :] = total * INV[f, i - 1]

    def far_first(n):
        return sorted(range(1, n), key=lambda d: -min(d, n - d))

    def x_pair(i_up, i_down, ref, both=True, f=0):
        pick_ = (lambda a: ref.at[:, a, BODY, :]) if both else (lambda a: ref.at[f, a, BODY, :])
        return [
            remote(i_up, pick_(CX), pick_(0), up),
            remote(i_down, pick_(1), pick_(CX + 1), down),
        ]

    kh_over = [
        remote(KH_OVER + i, coe.at[0, 0, i - 1], T0.at[0, i, BODY, :], other) for i in (1, CX, 2)
    ]
    kh_last = remote(KH_OVER + 3, coe.at[0, 0, 2], T0.at[0, 3, BODY, :], other)
    kh_edges = remote(K_Y, yr0.at[pl.ds(8, 8)], yr2, other)
    three = pl.ds(core, 3)
    kv_cross = remote(KV_CROSS, coe.at[0, 1, three], RL, cross)
    kv_on = remote(KV_ON, RL, KVC.at[0, three], side)
    kv_over = remote(KV_OVER, coe.at[0, 1, near_mate - 1], KVC.at[0, near_mate - 1], other)
    main_rows = pl.ds(pl.multiple_of(LO + 8 * gy, 8), CY - 8)
    edge_rows = pl.ds(pl.multiple_of(HI - 8 - (CY - 8) * gy, 8), 8)
    inner = [F2.at[f, pl.ds(others, 3), main_rows, :] for f in range(2)]
    main_over = [remote(MAIN_OVER + f, v, v, other) for f, v in enumerate(inner)]
    rest_over = []
    for f in range(2):
        views = [F2.at[f, near_far, BODY, :], F2.at[f, pl.ds(others, 3), edge_rows, :]]
        rest_over.append(
            [remote(REST_OVER + 3 * f + n, v, v, other) for n, v in enumerate(views)]
        )
    at_over = remote(AT_OVER, ats, atr, other)
    layers = range(1, CX + 1)

    @pl.when(sec == 0)
    def _():
        for c in loads0:
            c.start()
        for c in loads0:
            c.wait()
        for f in range(2):
            for i in layers:
                r = f * CX + i - 1
                ys0[r : r + 1] = edge(F0, f, i)
                ys0[r + 8 : r + 9] = edge(T0, f, i)
        pl.semaphore_wait(barrier, len(partners))
        halo_y = remote(Y_START, ys0, yr0, side)
        halo_y.start()
        halo_far_x, halo_mate_x = [], []
        for f in range(2):
            for s, dev, src, dst, group in (
                (X_UP, far, near_far, halo_mate, halo_far_x),
                (X_DOWN, mate, near_mate, halo_far, halo_mate_x),
            ):
                pair_ = [
                    remote(s + 2 * f, unk.at[0, f, src - 1], F0.at[f, dst, BODY, :], dev),
                    remote(s + 2 * f + 1, coe.at[0, 3 * f, src - 1], T0.at[f, dst, BODY, :], dev),
                ]
                for c in pair_:
                    c.start()
                group.append(pair_)
        for c in kh_over:
            c.start()
        kv_cross.start()
        for f in range(2):
            for i in layers:
                z_faces(f, i, KVC[0, i - 1] if f == 0 else T0[1, i, BODY, :])
                y_faces(f, i)
            for a in range(1, CX):
                x_face(f, a)
        row_mask, col_hot, index, order, slot = wells()
        halo_y.wait()
        kh_edges.start()
        for f in range(2):
            for i in layers:
                r = f * CX + i - 1
                set_edges(F0, f, i, yr0[r : r + 1], False)
                set_edges(T0, f, i, yr0[r + 8 : r + 9], True)
                y_ends(f, i)
                F1[f, i, HI : HI + 1, :] = jnp.zeros((1, NZ), F32)
                F1[f, i, LO - 1 : LO, :] = jnp.zeros((1, NZ), F32)
            for i in (2, 3):
                system(f, i, F0)
                sweep(f, i, F0, F1)
        for f in range(2):
            for c in halo_mate_x[f]:
                c.wait()
            x_face(f, CX * (1 - core))
            system(f, near_mate, F0)
            sweep(f, near_mate, F0, F1)
        mate_x2 = remote(X2_DOWN, F1.at[:, near_mate, BODY, :], F1.at[:, halo_far, BODY, :], mate)
        mate_x2.start()
        far_x2 = []
        for f in (1, 0):
            for c in halo_far_x[f]:
                c.wait()
            x_face(f, CX * core)
            system(f, near_far, F0)
            sweep(f, near_far, F0, F1)
            c = remote(
                X2_UP + f, F1.at[f, near_far, BODY, :], F1.at[f, halo_mate, BODY, :], far
            )
            c.start()
            far_x2.append(c)
        for f in range(2):
            for i in layers:
                r = f * CX + i - 1
                ys1[r : r + 1] = edge(F1, f, i)
        halo_y = remote(Y_SECOND, ys1, yr1, side)
        halo_y.start()
        mate_x2.wait()
        for f in (1, 0):
            for k in range(3):
                sweep(f, others + k, F1, F2)
            if f == 1:
                main_over[1].start()
                kh_last.start()
        halo_y.wait()
        for at, r, t in ((0, HI - 1, HI - 1), (1, LO, LO - 1)):

            @pl.when(gy == at)
            def _(r=r, t=t):
                for f in range(2):
                    for k in range(3):
                        i = others + k
                        n = f * CX + i - 1
                        more = TY[f, i - 1, t : t + 1] * INV[f, i - 1, r - LO : r - LO + 1]
                        row = yr1[pl.ds(n, 1)]
                        F2[f, i, r : r + 1, :] = F2[f, i, r : r + 1, :] + more * row

        for f, c in zip((1, 0), far_x2):
            set_edges(F1, f, near_far, yr1[pl.ds(f * CX + near_far - 1, 1)], False)
            c.wait()
            sweep(f, near_far, F1, F2)
        finals = [F2[f, 1 : CX + 1, BODY, :].reshape(CX * CY, NZ) for f in range(2)]
        pressure, warmth = pick(finals, row_mask, col_hot)
        ats[...] = jnp.zeros_like(ats)
        ats[0:1] = pressure
        ats[1:2] = warmth
        at_over.start()
        for c in rest_over[1] + rest_over[0]:
            c.start()
        main_over[0].start()
        save = local(11, F2.at[:, pl.ds(1, CX), BODY, :], out.at[0])
        save.start()
        q = index * (s_pp[...] - pressure)
        copies = rates_first((q, q * warmth), order, slot)
        copies = rates_second(copies)
        kv_over.start()
        last = rates_last(copies)
        for c in kh_over + main_over + [kh_last, kh_edges, kv_cross, kv_over, at_over] + rest_over[0] + rest_over[1]:
            c.wait_send()
        save.wait()
        last.wait()

    @pl.when(sec == 1)
    def _():
        for c in loads1:
            c.start()
        pl.semaphore_wait(barrier, len(partners))
        for c in loads1:
            c.wait()
        for i in range(CX):
            kind = RK[i]
            ends = []
            masks = [kind == t for t in range(1, NROCK)]
            for k in range(3):
                e = jnp.full((CY, NZ), table[k, 0], F32)
                for t in range(1, NROCK):
                    e = jnp.where(masks[t - 1], table[k, t], e)
                ends.append(e)
            water, gas = WG[0, i], WG[1, i]
            oil = 1.0 - water - gas
            MOB[0, i] = ends[0] * water * water * reciprocal(VM[1, i])
            MOB[1, i] = ends[1] * oil * oil * reciprocal(VM[2, i])
            MOB[2, i] = ends[2] * gas * gas * reciprocal(VM[3, i])
        kv_cross.wait_recv()
        kv_on.start()
        row_mask, col_hot, index, order, slot = wells()
        lw, lo, lg = pick([MOB[k].reshape(CX * CY, NZ) for k in range(3)], row_mask, col_hot)

        for c in kh_over:
            c.wait_recv()
        halo_k = x_pair(K_UP, K_DOWN, T0, False)
        for c in halo_k:
            c.start()
        for i in (1, CX, 2):
            y_faces(0, i)
        x_face(0, 1)
        kh_edges.wait_recv()
        for i in layers:
            set_edges(T0, 0, i, yr2[i - 1 : i], True)
        for i in (1, CX, 2):
            y_ends(0, i)
        kh_last.wait_recv()
        for a in (2, 3):
            x_face(0, a)
        y_faces(0, 3)
        y_ends(0, 3)
        for c in halo_k:
            c.wait()
        for a in (0, CX):
            x_face(0, a)

        at_over.wait_recv()
        q = index * (s_pp[...] - atr[0:1])
        lo = lo * jnp.exp(LINKED * (atr[1:2] - 1.0))
        scaled = q * reciprocal(lw + lo + lg)
        copies = rates_first((scaled * lw, scaled * lg), order, slot)
        for c in rest_over[1] + main_over[1:]:
            c.wait_recv()
        for i in (1, 4, 2, 3):
            other_mob = MOB[1, i - 1] * jnp.exp(LINKED * (F2[1, i, BODY, :] - 1.0))
            part_all = reciprocal(MOB[0, i - 1] + other_mob + MOB[2, i - 1])
            SH[0, i, BODY, :] = MOB[0, i - 1] * part_all
            SH[1, i, BODY, :] = MOB[2, i - 1] * part_all
        halo_s = x_pair(S_UP, S_DOWN, SH)
        for c in halo_s:
            c.start()
        for i in layers:
            ys3[i - 1 : i] = edge(SH, 0, i)
            ys3[i + 3 : i + 4] = edge(SH, 1, i)
        halo_sy = remote(S_Y, ys3, yr3, side)
        halo_sy.start()
        for c in rest_over[0]:
            c.wait_recv()
        far_p = remote(
            P_UP, F2.at[0, near_far, BODY, :], F2.at[0, halo_mate, BODY, :], far
        )
        far_p.start()
        ys4[...] = jnp.zeros_like(ys4)
        for at, r in ((0, HI - 1), (1, LO)):

            @pl.when(gy == at)
            def _(r=r):
                for i in layers:
                    ys4[i - 1 : i] = F2[0, i, r : r + 1, :]

        halo_py = remote(P_Y, ys4, yr4, side)
        halo_py.start()
        copies = rates_second(copies)

        halo_sy.wait()
        halo_py.wait()
        for i in layers:
            set_edges(F2, 0, i, yr4[i - 1 : i], False)
            set_edges(SH, 0, i, yr3[i - 1 : i], False)
            set_edges(SH, 1, i, yr3[i + 3 : i + 4], False)
        kv_on.wait()
        for k in range(3):
            z_faces(0, core + k + 1, KVC[0, core + k])
        main_over[0].wait_recv()
        mate_p = remote(
            P_DOWN, F2.at[0, near_mate, BODY, :], F2.at[0, halo_far, BODY, :], mate
        )
        mate_p.start()
        for c in halo_s + [far_p]:
            c.wait()

        def through(flow, shares):
            pos, neg = jnp.maximum(flow, 0.0), jnp.minimum(flow, 0.0)
            return [pos * a + neg * b for a, b in shares]

        saves = []
        for k in range(CX):
            i = near_far + k * (1 - 2 * core)
            if k == CX - 1:
                kv_over.wait_recv()
                z_faces(0, i, KVC[0, i - 1])
                mate_p.wait()
            p = F2[0, i, BODY, :]
            s = [SH[a, i, BODY, :] for a in range(2)]
            tz = TZ[0, i - 1]
            west = through(
                TX[0, i - 1] * (F2[0, i - 1, BODY, :] - p),
                [(SH[a, i - 1, BODY, :], s[a]) for a in range(2)],
            )
            east = through(
                TX[0, i] * (p - F2[0, i + 1, BODY, :]),
                [(s[a], SH[a, i + 1, BODY, :]) for a in range(2)],
            )
            south = through(
                TY[0, i - 1, LO - 1 : HI - 1] * (F2[0, i, LO - 1 : HI - 1, :] - p),
                [(SH[a, i, LO - 1 : HI - 1, :], s[a]) for a in range(2)],
            )
            north = through(
                TY[0, i - 1, LO:HI] * (p - F2[0, i, LO + 1 : HI + 1, :]),
                [(s[a], SH[a, i, LO + 1 : HI + 1, :]) for a in range(2)],
            )
            top = through(
                tz * (p - pltpu.roll(p, NZ - 1, 1)),
                [(s[a], pltpu.roll(s[a], NZ - 1, 1)) for a in range(2)],
            )
            rows = pl.ds(pl.multiple_of((i - 1) * CY, CY), CY)
            rate = WD[1, rows] - WD[0, rows] * p
            inverse = reciprocal(VM[0, i - 1])
            for a in range(2):
                net = west[a] - east[a] + south[a] - north[a] + pltpu.roll(top[a], 1, 1) - top[a]
                WG[a, i - 1] = WG[a, i - 1] + (net + rate * s[a]) * inverse
            saves.append(local(11 + k, WG.at[:, i - 1], out.at[0, :, i - 1]))
            saves[-1].start()
        last = rates_last(copies)
        for c in saves + [last]:
            c.wait()


def hand_over(unknowns, sums, out, rates, held, held_sums, take, give):
    parts = [(sums.at[0], held_sums, rates.at[0], 2 * CX)]
    for f in range(2):
        for i in range(CX):
            parts.append((unknowns.at[0, f, i], held.at[f, i], out.at[0, f, i], f * CX + i))
    inward = [pltpu.make_async_copy(a, b, take.at[n]) for a, b, _, n in parts]
    outward = [pltpu.make_async_copy(b, c, give.at[n]) for _, b, c, n in parts]
    for c in inward:
        c.start()
    for a, b in zip(inward, outward):
        a.wait()
        b.start()
    for c in outward:
        c.wait()


def per_device(unk, coe, rock, table, loc, pw, wi, pp, own, slo):
    any_ = pl.BlockSpec(memory_space=pl.ANY)
    row = lambda a: a.reshape(1, PERFS)
    vm = lambda *s: pltpu.VMEM(s, F32)
    halo = (2, CX + 2, CY + 16, NZ)
    unknowns, sums = pl.pallas_call(
        body,
        out_shape=(
            jax.ShapeDtypeStruct((1, 2, CX, CY, NZ), F32),
            jax.ShapeDtypeStruct((1, 2, 128), F32),
        ),
        in_specs=[any_] * 3 + [pl.BlockSpec(memory_space=pltpu.SMEM)] + [any_] * 6,
        out_specs=(any_, any_),
        scratch_shapes=[
            vm(*halo), vm(*halo), vm(*halo), vm(*halo), vm(*halo),
            vm(2, CX, CY, NZ), vm(3, CY, NZ),
            vm(2, CX, CY, NZ),
            vm(4, CX, CY, NZ),
            pltpu.VMEM((CX, CY, NZ), jnp.int32),
            vm(2, CX + 1, CY, NZ), vm(2, CX, CY + 16, NZ), vm(2, CX, CY, NZ),
            vm(2, CX, CY, NZ), vm(2, CX, CY, NZ),
            vm(2, CX * CY, NZ),
            vm(3, CX, CY, NZ),
            pltpu.VMEM((1, PERFS), jnp.int32), pltpu.VMEM((1, PERFS), jnp.int32),
            vm(1, PERFS), vm(1, PERFS),
            pltpu.VMEM((64, 128), jnp.int32), pltpu.VMEM((64, 128), jnp.int32),
            vm(16, NZ), vm(16, NZ), vm(8, NZ), vm(8, NZ), vm(8, NZ), vm(8, NZ),
            vm(8, NZ), vm(8, NZ), vm(8, NZ), vm(8, NZ),
            vm(8, PERFS), vm(8, PERFS),
            vm(RUN, 2, PAIRS, 128), vm(RUN, 2, PAIRS, 128),
            vm(PAIRS, 8, 128), vm(PAIRS, 8, 128), vm(2, 128),
            pltpu.SemaphoreType.DMA((N_SEM,)),
            pltpu.SemaphoreType.DMA((N_SEM,)),
            pltpu.SemaphoreType.DMA((N_LOCAL,)),
        ],
        compiler_params=pltpu.CompilerParams(
            collective_id=0, has_side_effects=True, vmem_limit_bytes=60 * 2**20
        ),
    )(
        unk, coe, rock, table.T, row(loc), row(pw), row(wi), row(pp),
        own.reshape(64, 128), slo.reshape(64, 128),
    )
    return pl.pallas_call(
        hand_over,
        out_shape=(
            jax.ShapeDtypeStruct(unknowns.shape, F32),
            jax.ShapeDtypeStruct(sums.shape, F32),
        ),
        in_specs=[any_, any_],
        out_specs=(any_, any_),
        scratch_shapes=[
            vm(2, CX, CY, NZ),
            vm(2, 128),
            pltpu.SemaphoreType.DMA((2 * CX + 1,)),
            pltpu.SemaphoreType.DMA((2 * CX + 1,)),
        ],
        compiler_params=pltpu.CompilerParams(vmem_limit_bytes=60 * 2**20),
    )(unknowns, sums)


def solution(mesh):
    in_specs = (
        P("sec", None, "gx", "gy", None),
        P("sec", None, "gx", "gy", None),
        P("gx", "gy", None),
        P(),
        P(("gx", "gy")),
        P(("gx", "gy")),
        P(("gx", "gy")),
        P(("gx", "gy")),
        P(),
        P(),
    )
    out_specs = (P("sec", None, "gx", "gy", None), P("sec", None, ("gx", "gy")))
    return jax.shard_map(
        per_device, mesh=mesh, in_specs=in_specs, out_specs=out_specs, check_vma=False
    )
```

```python
import functools

import jax
import jax.numpy as jnp
from jax import lax
from jax.experimental import pallas as pl
from jax.experimental.pallas import tpu as pltpu
from jax.sharding import PartitionSpec as P

MESH = pl.DeviceIdType.MESH
F32 = jnp.float32
BF16 = jnp.bfloat16
CX, CY, NZ = 4, 64, 256
PERFS = 256
NROCK = 8
RING = 64
RUN = 16
PAIRS = 8
LINKED = 1.5

LO, HI = 8, 8 + CY
BODY = pl.ds(LO, CY)

X_UP, X_DOWN = 0, 4
Y_START = 8
KH_OVER = 60
KV_CROSS, KV_ON, KV_OVER = 10, 11, 12
X2_UP, X2_DOWN = 14, 16
Y_SECOND = 18
REST_OVER = 20
AT_OVER = 26
K_UP, K_DOWN, K_Y = 27, 28, 29
S_UP, S_DOWN, S_Y = 30, 31, 32
P_UP, P_DOWN, P_Y = 33, 34, 35
R_FIRST = 36
R_SECOND = 52
MAIN_OVER = 65
N_SEM = 67
N_LOCAL = 16


def reciprocal(x):
    r = pl.reciprocal(x, approx=True)
    return r * (2.0 - x * r)


def harmonic(a, b):
    return (2.0 * a) * (b * reciprocal(a + b))


def split(x):
    high = x.astype(BF16)
    rest = x - high.astype(F32)
    mid = rest.astype(BF16)
    low = (rest - mid.astype(F32)).astype(BF16)
    return high, mid, low


def dot_nt(a, b):
    return lax.dot_general(a, b, (((1,), (1,)), ((), ())), preferred_element_type=F32)


def dot_nn(a, b):
    return lax.dot_general(a, b, (((1,), (0,)), ((), ())), preferred_element_type=F32)


def hot(index, rows):
    return lax.broadcasted_iota(jnp.int32, (rows, PERFS), 0) == index


def as_bf16(mask):
    return jnp.where(mask, 1.0, 0.0).astype(BF16)


def spread(row_hot, col_mask, value):
    total = None
    for piece in split(value):
        term = dot_nt(row_hot, jnp.where(col_mask, piece.astype(F32), 0.0).astype(BF16))
        total = term if total is None else total + term
    return total


def pick(fields, row_mask, col_hot):
    found = dot_nn(jnp.concatenate([p for field in fields for p in split(field)], axis=0), col_hot)
    rows = []
    for k in range(len(fields)):
        a, b, c = (found[(3 * k + n) * PERFS : (3 * k + n + 1) * PERFS] for n in range(3))
        rows.append(jnp.sum(jnp.where(row_mask, a + b + c, 0.0), axis=0, keepdims=True))
    return rows


def body(
    unk, coe, rock, table, loc, pw, wi, pp, own, slo,
    out, rates,
    F0, F1, F2, T0, SH, KVC, RL, WG, VM, RK, TX, TY, TZ, INV, BASE, WD, MOB,
    s_loc, s_pw, s_wi, s_pp, s_own, s_slo,
    ys0, yr0, ys1, yr1, ys2, yr2, ys3, yr3, ys4, yr4, ats, atr,
    part, got1, part2, got2, rate_buf,
    send, recv, lsem,
):
    sec, gx, gy = (lax.axis_index(a) for a in ("sec", "gx", "gy"))
    up = (sec, lax.rem(gx + 1, RING), gy)
    down = (sec, lax.rem(gx + RING - 1, RING), gy)
    side = (sec, gx, 1 - gy)
    other = (1 - sec, gx, gy)
    cross = (1 - sec, gx, 1 - gy)
    zc, y = lax.rem(gx, RUN), gx // RUN
    core = lax.rem(gx, 2)
    mate = (sec, gx + 1 - 2 * core, gy)
    far = (sec, lax.rem(gx + RING - 1 + 2 * core, RING), gy)
    near_far, near_mate = 1 + (CX - 1) * core, CX - (CX - 1) * core
    halo_far, halo_mate = (CX + 1) * core, (CX + 1) * (1 - core)
    others = 2 - core
    pair = y * 2 + gy
    first = [(sec, y * RUN + lax.rem(zc + d, RUN), gy) for d in range(1, RUN)]
    second = []
    for d in range(1, PAIRS):
        q = lax.rem(pair + d, PAIRS)
        second.append((sec, (q // 2) * RUN + zc, lax.rem(q, 2)))

    barrier = pltpu.get_barrier_semaphore()
    partners = [up, down, side, other, cross] + first + second
    for dev in partners:
        pl.semaphore_signal(barrier, inc=1, device_id=dev, device_id_type=MESH)

    def local(i, src, dst):
        return pltpu.make_async_copy(src, dst, lsem.at[i])

    def remote(i, src, dst, dev):
        return pltpu.make_async_remote_copy(
            src_ref=src,
            dst_ref=dst,
            send_sem=send.at[i],
            recv_sem=recv.at[i],
            device_id=dev,
            device_id_type=MESH,
        )

    small = [
        local(0, loc, s_loc),
        local(1, pw, s_pw),
        local(2, wi, s_wi),
        local(3, pp, s_pp),
        local(4, own, s_own),
        local(5, slo, s_slo),
    ]
    for c in small:
        c.start()
    loads0 = [
        local(6, unk.at[0], F0.at[:, pl.ds(1, CX), BODY, :]),
        local(7, coe.at[0, 0], T0.at[0, pl.ds(1, CX), BODY, :]),
        local(8, coe.at[0, 3], T0.at[1, pl.ds(1, CX), BODY, :]),
        local(9, coe.at[0, pl.ds(1, 2)], KVC),
    ]
    loads1 = [local(6, unk.at[0], WG), local(7, coe.at[0], VM), local(8, rock, RK)]

    def wells():
        for c in small:
            c.wait()
        place = s_loc[...]
        row, col = lax.shift_right_logical(place, 8), jnp.bitwise_and(place, 255)
        row_mask, col_mask = hot(row, PERFS), hot(col, PERFS)
        row_hot, col_hot = as_bf16(row_mask), as_bf16(col_mask)
        live = s_pw[...] >= 0
        index = jnp.where(live, s_wi[...], 0.0)
        WD[0] = spread(row_hot, col_mask, index)
        WD[1] = spread(row_hot, col_mask, index * s_pp[...])
        well = jnp.maximum(s_pw[...], 0)
        w_row = hot(lax.shift_right_logical(well, 7), 64)
        w_col = as_bf16(hot(jnp.bitwise_and(well, 127), 128))

        def look(ref):
            found = dot_nn(ref[...].astype(F32).astype(BF16), w_col)
            return jnp.sum(jnp.where(w_row, found, 0.0), axis=0, keepdims=True).astype(jnp.int32)

        owner, slot = look(s_own), look(s_slo)
        o_gx, o_gy = lax.shift_right_logical(owner, 1), jnp.bitwise_and(owner, 1)
        order = (
            jnp.bitwise_and(o_gx, RUN - 1) * PAIRS + lax.shift_right_logical(o_gx, 4) * 2 + o_gy
        )
        return row_mask, col_hot, index, order, slot

    def rates_first(values, order, slot):
        own_mask, slot_hot = hot(order, RUN * PAIRS), as_bf16(hot(slot, 128))
        lhs = [
            jnp.where(own_mask, piece.astype(F32), 0.0).astype(BF16)
            for value in values
            for piece in split(value)
        ]
        found = dot_nt(jnp.concatenate(lhs, axis=0), slot_hot)
        size = RUN * PAIRS
        for a in range(2):
            u, v, w = (found[(3 * a + n) * size : (3 * a + n + 1) * size] for n in range(3))
            part[:, a] = (u + v + w).reshape(RUN, PAIRS, 128)
        copies = [
            remote(R_FIRST + d, part.at[lax.rem(zc + d, RUN)], got1.at[d], first[d - 1])
            for d in far_first(RUN)
        ]
        for c in copies:
            c.start()
        return copies

    def rates_second(copies):
        for c in copies:
            c.wait()
        total = part[zc]
        for d in range(1, RUN):
            total = total + got1[d]
        part2[...] = jnp.zeros_like(part2)
        for a in range(2):
            for q in range(PAIRS):
                part2[q, a : a + 1] = total[a, q : q + 1]
        copies = [
            remote(R_SECOND + d, part2.at[lax.rem(pair + d, PAIRS)], got2.at[d], second[d - 1])
            for d in range(1, PAIRS)
        ]
        for c in copies:
            c.start()
        return copies

    def rates_last(copies):
        for c in copies:
            c.wait()
        total = part2[pair]
        for d in range(1, PAIRS):
            total = total + got2[d]
        rate_buf[...] = total[0:2]
        c = local(10, rate_buf, rates.at[0])
        c.start()
        return c

    def edge(ref, f, i):
        return jnp.where(gy == 0, ref[f, i, HI - 1 : HI, :], ref[f, i, LO : LO + 1, :])

    def set_edges(ref, f, i, row, zero):
        if zero:
            ref[f, i, HI : HI + 1, :] = jnp.where(gy == 0, row, 0.0)
            ref[f, i, LO - 1 : LO, :] = jnp.where(gy == 1, row, 0.0)
        else:
            ref[f, i, HI : HI + 1, :] = row
            ref[f, i, LO - 1 : LO, :] = row

    def x_face(f, a):
        outside = jnp.logical_or(
            jnp.logical_and(gx == 0, a == 0), jnp.logical_and(gx == RING - 1, a == CX)
        )
        face = harmonic(T0[f, a, BODY, :], T0[f, a + 1, BODY, :])
        TX[f, a] = jnp.where(outside, 0.0, face)

    def y_faces(f, i):
        TY[f, i - 1, LO : HI - 1] = harmonic(T0[f, i, LO : HI - 1, :], T0[f, i, LO + 1 : HI, :])

    def y_ends(f, i):
        for r in (LO - 1, HI - 1):
            TY[f, i - 1, r : r + 1] = harmonic(T0[f, i, r : r + 1, :], T0[f, i, r + 1 : r + 2, :])

    def z_faces(f, i, value):
        lane = lax.broadcasted_iota(jnp.int32, (CY, NZ), 1)
        face = harmonic(value, pltpu.roll(value, NZ - 1, 1))
        TZ[f, i - 1] = jnp.where(lane == NZ - 1, 0.0, face)

    def system(f, i, start):
        c = KVC[1, i - 1]
        tz = TZ[f, i - 1]
        total = (
            c + TX[f, i - 1] + TX[f, i] + TY[f, i - 1, LO - 1 : HI - 1] + TY[f, i - 1, LO:HI]
            + tz + pltpu.roll(tz, 1, 1)
        )
        base = c * start[f, i, BODY, :]
        if f == 0:
            rows = pl.ds((i - 1) * CY if isinstance(i, int) else pl.multiple_of((i - 1) * CY, CY), CY)
            total = total + WD[0, rows]
            base = base + WD[1, rows]
        INV[f, i - 1] = reciprocal(total)
        BASE[f, i - 1] = base

    def sweep(f, i, now, later):
        tz = TZ[f, i - 1]
        centre = now[f, i, BODY, :]
        total = (
            BASE[f, i - 1]
            + TX[f, i - 1] * now[f, i - 1, BODY, :]
            + TX[f, i] * now[f, i + 1, BODY, :]
            + TY[f, i - 1, LO - 1 : HI - 1] * now[f, i, LO - 1 : HI - 1, :]
            + TY[f, i - 1, LO:HI] * now[f, i, LO + 1 : HI + 1, :]
            + tz * pltpu.roll(centre, NZ - 1, 1)
            + pltpu.roll(tz * centre, 1, 1)
        )
        later[f, i, BODY, :] = total * INV[f, i - 1]

    def far_first(n):
        return sorted(range(1, n), key=lambda d: -min(d, n - d))

    def x_pair(i_up, i_down, ref, both=True, f=0):
        pick_ = (lambda a: ref.at[:, a, BODY, :]) if both else (lambda a: ref.at[f, a, BODY, :])
        return [
            remote(i_up, pick_(CX), pick_(0), up),
            remote(i_down, pick_(1), pick_(CX + 1), down),
        ]

    kh_over = [
        remote(KH_OVER + i, coe.at[0, 0, i - 1], T0.at[0, i, BODY, :], other) for i in (1, CX, 2)
    ]
    kh_last = remote(KH_OVER + 3, coe.at[0, 0, 2], T0.at[0, 3, BODY, :], other)
    kh_edges = remote(K_Y, yr0.at[pl.ds(8, 8)], yr2, other)
    three = pl.ds(core, 3)
    kv_cross = remote(KV_CROSS, coe.at[0, 1, three], RL, cross)
    kv_on = remote(KV_ON, RL, KVC.at[0, three], side)
    kv_over = remote(KV_OVER, coe.at[0, 1, near_mate - 1], KVC.at[0, near_mate - 1], other)
    main_rows = pl.ds(pl.multiple_of(LO + 8 * gy, 8), CY - 8)
    edge_rows = pl.ds(pl.multiple_of(HI - 8 - (CY - 8) * gy, 8), 8)
    inner = [F2.at[f, pl.ds(others, 3), main_rows, :] for f in range(2)]
    main_over = [remote(MAIN_OVER + f, v, v, other) for f, v in enumerate(inner)]
    rest_over = []
    for f in range(2):
        views = [F2.at[f, near_far, BODY, :], F2.at[f, pl.ds(others, 3), edge_rows, :]]
        rest_over.append(
            [remote(REST_OVER + 3 * f + n, v, v, other) for n, v in enumerate(views)]
        )
    at_over = remote(AT_OVER, ats, atr, other)
    layers = range(1, CX + 1)

    @pl.when(sec == 0)
    def _():
        for c in loads0:
            c.start()
        for c in loads0:
            c.wait()
        for f in range(2):
            for i in layers:
                r = f * CX + i - 1
                ys0[r : r + 1] = edge(F0, f, i)
                ys0[r + 8 : r + 9] = edge(T0, f, i)
        pl.semaphore_wait(barrier, len(partners))
        halo_y = remote(Y_START, ys0, yr0, side)
        halo_y.start()
        halo_far_x, halo_mate_x = [], []
        for f in range(2):
            for s, dev, src, dst, group in (
                (X_UP, far, near_far, halo_mate, halo_far_x),
                (X_DOWN, mate, near_mate, halo_far, halo_mate_x),
            ):
                pair_ = [
                    remote(s + 2 * f, unk.at[0, f, src - 1], F0.at[f, dst, BODY, :], dev),
                    remote(s + 2 * f + 1, coe.at[0, 3 * f, src - 1], T0.at[f, dst, BODY, :], dev),
                ]
                for c in pair_:
                    c.start()
                group.append(pair_)
        for c in kh_over:
            c.start()
        kv_cross.start()
        for f in range(2):
            for i in layers:
                z_faces(f, i, KVC[0, i - 1] if f == 0 else T0[1, i, BODY, :])
                y_faces(f, i)
            for a in range(1, CX):
                x_face(f, a)
        row_mask, col_hot, index, order, slot = wells()
        halo_y.wait()
        kh_edges.start()
        for f in range(2):
            for i in layers:
                r = f * CX + i - 1
                set_edges(F0, f, i, yr0[r : r + 1], False)
                set_edges(T0, f, i, yr0[r + 8 : r + 9], True)
                y_ends(f, i)
                F1[f, i, HI : HI + 1, :] = jnp.zeros((1, NZ), F32)
                F1[f, i, LO - 1 : LO, :] = jnp.zeros((1, NZ), F32)
            for i in (2, 3):
                system(f, i, F0)
                sweep(f, i, F0, F1)
        for f in range(2):
            for c in halo_mate_x[f]:
                c.wait()
            x_face(f, CX * (1 - core))
            system(f, near_mate, F0)
            sweep(f, near_mate, F0, F1)
        mate_x2 = remote(X2_DOWN, F1.at[:, near_mate, BODY, :], F1.at[:, halo_far, BODY, :], mate)
        mate_x2.start()
        far_x2 = []
        for f in (1, 0):
            for c in halo_far_x[f]:
                c.wait()
            x_face(f, CX * core)
            system(f, near_far, F0)
            sweep(f, near_far, F0, F1)
            c = remote(
                X2_UP + f, F1.at[f, near_far, BODY, :], F1.at[f, halo_mate, BODY, :], far
            )
            c.start()
            far_x2.append(c)
        for f in range(2):
            for i in layers:
                r = f * CX + i - 1
                ys1[r : r + 1] = edge(F1, f, i)
        halo_y = remote(Y_SECOND, ys1, yr1, side)
        halo_y.start()
        mate_x2.wait()
        for f in (1, 0):
            for k in range(3):
                sweep(f, others + k, F1, F2)
            if f == 1:
                main_over[1].start()
                kh_last.start()
        halo_y.wait()
        for at, r, t in ((0, HI - 1, HI - 1), (1, LO, LO - 1)):

            @pl.when(gy == at)
            def _(r=r, t=t):
                for f in range(2):
                    for k in range(3):
                        i = others + k
                        n = f * CX + i - 1
                        more = TY[f, i - 1, t : t + 1] * INV[f, i - 1, r - LO : r - LO + 1]
                        row = yr1[pl.ds(n, 1)]
                        F2[f, i, r : r + 1, :] = F2[f, i, r : r + 1, :] + more * row

        for f, c in zip((1, 0), far_x2):
            set_edges(F1, f, near_far, yr1[pl.ds(f * CX + near_far - 1, 1)], False)
            c.wait()
            sweep(f, near_far, F1, F2)
        finals = [F2[f, 1 : CX + 1, BODY, :].reshape(CX * CY, NZ) for f in range(2)]
        pressure, warmth = pick(finals, row_mask, col_hot)
        ats[...] = jnp.zeros_like(ats)
        ats[0:1] = pressure
        ats[1:2] = warmth
        at_over.start()
        for c in rest_over[1] + rest_over[0]:
            c.start()
        main_over[0].start()
        save = local(11, F2.at[:, pl.ds(1, CX), BODY, :], out.at[0])
        save.start()
        q = index * (s_pp[...] - pressure)
        copies = rates_first((q, q * warmth), order, slot)
        copies = rates_second(copies)
        kv_over.start()
        last = rates_last(copies)
        for c in kh_over + main_over + [kh_last, kh_edges, kv_cross, kv_over, at_over] + rest_over[0] + rest_over[1]:
            c.wait_send()
        save.wait()
        last.wait()

    @pl.when(sec == 1)
    def _():
        for c in loads1:
            c.start()
        pl.semaphore_wait(barrier, len(partners))
        for c in loads1:
            c.wait()
        for i in range(CX):
            kind = RK[i]
            ends = []
            masks = [kind == t for t in range(1, NROCK)]
            for k in range(3):
                e = jnp.full((CY, NZ), table[k, 0], F32)
                for t in range(1, NROCK):
                    e = jnp.where(masks[t - 1], table[k, t], e)
                ends.append(e)
            water, gas = WG[0, i], WG[1, i]
            oil = 1.0 - water - gas
            MOB[0, i] = ends[0] * water * water * reciprocal(VM[1, i])
            MOB[1, i] = ends[1] * oil * oil * reciprocal(VM[2, i])
            MOB[2, i] = ends[2] * gas * gas * reciprocal(VM[3, i])
        kv_cross.wait_recv()
        kv_on.start()
        row_mask, col_hot, index, order, slot = wells()
        lw, lo, lg = pick([MOB[k].reshape(CX * CY, NZ) for k in range(3)], row_mask, col_hot)

        for c in kh_over:
            c.wait_recv()
        halo_k = x_pair(K_UP, K_DOWN, T0, False)
        for c in halo_k:
            c.start()
        for i in (1, CX, 2):
            y_faces(0, i)
        x_face(0, 1)
        kh_edges.wait_recv()
        for i in layers:
            set_edges(T0, 0, i, yr2[i - 1 : i], True)
        for i in (1, CX, 2):
            y_ends(0, i)
        kh_last.wait_recv()
        for a in (2, 3):
            x_face(0, a)
        y_faces(0, 3)
        y_ends(0, 3)
        for c in halo_k:
            c.wait()
        for a in (0, CX):
            x_face(0, a)

        at_over.wait_recv()
        q = index * (s_pp[...] - atr[0:1])
        lo = lo * jnp.exp(LINKED * (atr[1:2] - 1.0))
        scaled = q * reciprocal(lw + lo + lg)
        copies = rates_first((scaled * lw, scaled * lg), order, slot)
        for c in rest_over[1] + main_over[1:]:
            c.wait_recv()
        for i in (1, 4, 2, 3):
            other_mob = MOB[1, i - 1] * jnp.exp(LINKED * (F2[1, i, BODY, :] - 1.0))
            part_all = reciprocal(MOB[0, i - 1] + other_mob + MOB[2, i - 1])
            SH[0, i, BODY, :] = MOB[0, i - 1] * part_all
            SH[1, i, BODY, :] = MOB[2, i - 1] * part_all
        halo_s = x_pair(S_UP, S_DOWN, SH)
        for c in halo_s:
            c.start()
        for i in layers:
            ys3[i - 1 : i] = edge(SH, 0, i)
            ys3[i + 3 : i + 4] = edge(SH, 1, i)
        halo_sy = remote(S_Y, ys3, yr3, side)
        halo_sy.start()
        for c in rest_over[0]:
            c.wait_recv()
        far_p = remote(
            P_UP, F2.at[0, near_far, BODY, :], F2.at[0, halo_mate, BODY, :], far
        )
        far_p.start()
        ys4[...] = jnp.zeros_like(ys4)
        for at, r in ((0, HI - 1), (1, LO)):

            @pl.when(gy == at)
            def _(r=r):
                for i in layers:
                    ys4[i - 1 : i] = F2[0, i, r : r + 1, :]

        halo_py = remote(P_Y, ys4, yr4, side)
        halo_py.start()
        copies = rates_second(copies)

        halo_sy.wait()
        halo_py.wait()
        for i in layers:
            set_edges(F2, 0, i, yr4[i - 1 : i], False)
            set_edges(SH, 0, i, yr3[i - 1 : i], False)
            set_edges(SH, 1, i, yr3[i + 3 : i + 4], False)
        kv_on.wait()
        for k in range(3):
            z_faces(0, core + k + 1, KVC[0, core + k])
        main_over[0].wait_recv()
        mate_p = remote(
            P_DOWN, F2.at[0, near_mate, BODY, :], F2.at[0, halo_far, BODY, :], mate
        )
        mate_p.start()
        for c in halo_s + [far_p]:
            c.wait()

        def through(flow, shares):
            pos, neg = jnp.maximum(flow, 0.0), jnp.minimum(flow, 0.0)
            return [pos * a + neg * b for a, b in shares]

        saves = []
        for k in range(CX):
            i = near_far + k * (1 - 2 * core)
            if k == CX - 1:
                kv_over.wait_recv()
                z_faces(0, i, KVC[0, i - 1])
                mate_p.wait()
            p = F2[0, i, BODY, :]
            s = [SH[a, i, BODY, :] for a in range(2)]
            tz = TZ[0, i - 1]
            west = through(
                TX[0, i - 1] * (F2[0, i - 1, BODY, :] - p),
                [(SH[a, i - 1, BODY, :], s[a]) for a in range(2)],
            )
            east = through(
                TX[0, i] * (p - F2[0, i + 1, BODY, :]),
                [(s[a], SH[a, i + 1, BODY, :]) for a in range(2)],
            )
            south = through(
                TY[0, i - 1, LO - 1 : HI - 1] * (F2[0, i, LO - 1 : HI - 1, :] - p),
                [(SH[a, i, LO - 1 : HI - 1, :], s[a]) for a in range(2)],
            )
            north = through(
                TY[0, i - 1, LO:HI] * (p - F2[0, i, LO + 1 : HI + 1, :]),
                [(s[a], SH[a, i, LO + 1 : HI + 1, :]) for a in range(2)],
            )
            top = through(
                tz * (p - pltpu.roll(p, NZ - 1, 1)),
                [(s[a], pltpu.roll(s[a], NZ - 1, 1)) for a in range(2)],
            )
            rows = pl.ds(pl.multiple_of((i - 1) * CY, CY), CY)
            rate = WD[1, rows] - WD[0, rows] * p
            inverse = reciprocal(VM[0, i - 1])
            for a in range(2):
                net = west[a] - east[a] + south[a] - north[a] + pltpu.roll(top[a], 1, 1) - top[a]
                WG[a, i - 1] = WG[a, i - 1] + (net + rate * s[a]) * inverse
            saves.append(local(11 + k, WG.at[:, i - 1], out.at[0, :, i - 1]))
            saves[-1].start()
        last = rates_last(copies)
        for c in saves + [last]:
            c.wait()


def hand_over(unknowns, sums, out, rates, held, held_sums, take, give):
    parts = [(sums.at[0], held_sums, rates.at[0], 2 * CX)]
    for f in range(2):
        parts.append((unknowns.at[0, f], held.at[f], out.at[0, f], f))
    inward = [pltpu.make_async_copy(a, b, take.at[n]) for a, b, _, n in parts]
    outward = [pltpu.make_async_copy(b, c, give.at[n]) for _, b, c, n in parts]
    for c in inward:
        c.start()
    for a, b in zip(inward, outward):
        a.wait()
        b.start()
    for c in outward:
        c.wait()


def per_device(unk, coe, rock, table, loc, pw, wi, pp, own, slo):
    any_ = pl.BlockSpec(memory_space=pl.ANY)
    row = lambda a: a.reshape(1, PERFS)
    vm = lambda *s: pltpu.VMEM(s, F32)
    halo = (2, CX + 2, CY + 16, NZ)
    unknowns, sums = pl.pallas_call(
        body,
        out_shape=(
            jax.ShapeDtypeStruct((1, 2, CX, CY, NZ), F32),
            jax.ShapeDtypeStruct((1, 2, 128), F32),
        ),
        in_specs=[any_] * 3 + [pl.BlockSpec(memory_space=pltpu.SMEM)] + [any_] * 6,
        out_specs=(any_, any_),
        scratch_shapes=[
            vm(*halo), vm(*halo), vm(*halo), vm(*halo), vm(*halo),
            vm(2, CX, CY, NZ), vm(3, CY, NZ),
            vm(2, CX, CY, NZ),
            vm(4, CX, CY, NZ),
            pltpu.VMEM((CX, CY, NZ), jnp.int32),
            vm(2, CX + 1, CY, NZ), vm(2, CX, CY + 16, NZ), vm(2, CX, CY, NZ),
            vm(2, CX, CY, NZ), vm(2, CX, CY, NZ),
            vm(2, CX * CY, NZ),
            vm(3, CX, CY, NZ),
            pltpu.VMEM((1, PERFS), jnp.int32), pltpu.VMEM((1, PERFS), jnp.int32),
            vm(1, PERFS), vm(1, PERFS),
            pltpu.VMEM((64, 128), jnp.int32), pltpu.VMEM((64, 128), jnp.int32),
            vm(16, NZ), vm(16, NZ), vm(8, NZ), vm(8, NZ), vm(8, NZ), vm(8, NZ),
            vm(8, NZ), vm(8, NZ), vm(8, NZ), vm(8, NZ),
            vm(8, PERFS), vm(8, PERFS),
            vm(RUN, 2, PAIRS, 128), vm(RUN, 2, PAIRS, 128),
            vm(PAIRS, 8, 128), vm(PAIRS, 8, 128), vm(2, 128),
            pltpu.SemaphoreType.DMA((N_SEM,)),
            pltpu.SemaphoreType.DMA((N_SEM,)),
            pltpu.SemaphoreType.DMA((N_LOCAL,)),
        ],
        compiler_params=pltpu.CompilerParams(
            collective_id=0, has_side_effects=True, vmem_limit_bytes=60 * 2**20
        ),
    )(
        unk, coe, rock, table.T, row(loc), row(pw), row(wi), row(pp),
        own.reshape(64, 128), slo.reshape(64, 128),
    )
    return pl.pallas_call(
        hand_over,
        out_shape=(
            jax.ShapeDtypeStruct(unknowns.shape, F32),
            jax.ShapeDtypeStruct(sums.shape, F32),
        ),
        in_specs=[any_, any_],
        out_specs=(any_, any_),
        scratch_shapes=[
            vm(2, CX, CY, NZ),
            vm(2, 128),
            pltpu.SemaphoreType.DMA((2 * CX + 1,)),
            pltpu.SemaphoreType.DMA((2 * CX + 1,)),
        ],
        compiler_params=pltpu.CompilerParams(vmem_limit_bytes=60 * 2**20),
    )(unknowns, sums)


def solution(mesh):
    in_specs = (
        P("sec", None, "gx", "gy", None),
        P("sec", None, "gx", "gy", None),
        P("gx", "gy", None),
        P(),
        P(("gx", "gy")),
        P(("gx", "gy")),
        P(("gx", "gy")),
        P(("gx", "gy")),
        P(),
        P(),
    )
    out_specs = (P("sec", None, "gx", "gy", None), P("sec", None, ("gx", "gy")))
    return jax.shard_map(
        per_device, mesh=mesh, in_specs=in_specs, out_specs=out_specs, check_vma=False
    )
```

```python
import functools

import jax
import jax.numpy as jnp
from jax import lax
from jax.experimental import pallas as pl
from jax.experimental.pallas import tpu as pltpu
from jax.sharding import PartitionSpec as P

MESH = pl.DeviceIdType.MESH
F32 = jnp.float32
BF16 = jnp.bfloat16
CX, CY, NZ = 4, 64, 256
PERFS = 256
NROCK = 8
RING = 64
RUN = 16
PAIRS = 8
LINKED = 1.5

LO, HI = 8, 8 + CY
BODY = pl.ds(LO, CY)

X_UP, X_DOWN = 0, 4
Y_START = 8
KH_OVER = 60
KV_CROSS, KV_ON, KV_OVER = 10, 11, 12
X2_UP, X2_DOWN = 14, 16
Y_SECOND = 18
REST_OVER = 20
AT_OVER = 26
K_UP, K_DOWN, K_Y = 27, 28, 29
S_UP, S_DOWN, S_Y = 30, 31, 32
P_UP, P_DOWN, P_Y = 33, 34, 35
R_FIRST = 36
R_SECOND = 52
MAIN_OVER = 65
N_SEM = 67
N_LOCAL = 16


def reciprocal(x):
    r = pl.reciprocal(x, approx=True)
    return r * (2.0 - x * r)


def harmonic(a, b):
    return (2.0 * a) * (b * reciprocal(a + b))


def split(x):
    high = x.astype(BF16)
    rest = x - high.astype(F32)
    mid = rest.astype(BF16)
    low = (rest - mid.astype(F32)).astype(BF16)
    return high, mid, low


def dot_nt(a, b):
    return lax.dot_general(a, b, (((1,), (1,)), ((), ())), preferred_element_type=F32)


def dot_nn(a, b):
    return lax.dot_general(a, b, (((1,), (0,)), ((), ())), preferred_element_type=F32)


def hot(index, rows):
    return lax.broadcasted_iota(jnp.int32, (rows, PERFS), 0) == index


def as_bf16(mask):
    return jnp.where(mask, 1.0, 0.0).astype(BF16)


def spread(row_hot, col_mask, value):
    total = None
    for piece in split(value):
        term = dot_nt(row_hot, jnp.where(col_mask, piece.astype(F32), 0.0).astype(BF16))
        total = term if total is None else total + term
    return total


def pick(fields, row_mask, col_hot):
    found = dot_nn(jnp.concatenate([p for field in fields for p in split(field)], axis=0), col_hot)
    rows = []
    for k in range(len(fields)):
        a, b, c = (found[(3 * k + n) * PERFS : (3 * k + n + 1) * PERFS] for n in range(3))
        rows.append(jnp.sum(jnp.where(row_mask, a + b + c, 0.0), axis=0, keepdims=True))
    return rows


def body(
    unk, coe, rock, table, loc, pw, wi, pp, own, slo,
    out, rates,
    F0, F1, F2, T0, SH, KVC, RL, WG, VM, RK, TX, TY, TZ, INV, BASE, WD, MOB,
    s_loc, s_pw, s_wi, s_pp, s_own, s_slo,
    ys0, yr0, ys1, yr1, ys2, yr2, ys3, yr3, ys4, yr4, ats, atr,
    part, got1, part2, got2, rate_buf,
    send, recv, lsem,
):
    sec, gx, gy = (lax.axis_index(a) for a in ("sec", "gx", "gy"))
    up = (sec, lax.rem(gx + 1, RING), gy)
    down = (sec, lax.rem(gx + RING - 1, RING), gy)
    side = (sec, gx, 1 - gy)
    other = (1 - sec, gx, gy)
    cross = (1 - sec, gx, 1 - gy)
    zc, y = lax.rem(gx, RUN), gx // RUN
    core = lax.rem(gx, 2)
    mate = (sec, gx + 1 - 2 * core, gy)
    far = (sec, lax.rem(gx + RING - 1 + 2 * core, RING), gy)
    near_far, near_mate = 1 + (CX - 1) * core, CX - (CX - 1) * core
    halo_far, halo_mate = (CX + 1) * core, (CX + 1) * (1 - core)
    others = 2 - core
    pair = y * 2 + gy
    first = [(sec, y * RUN + lax.rem(zc + d, RUN), gy) for d in range(1, RUN)]
    second = []
    for d in range(1, PAIRS):
        q = lax.rem(pair + d, PAIRS)
        second.append((sec, (q // 2) * RUN + zc, lax.rem(q, 2)))

    barrier = pltpu.get_barrier_semaphore()
    partners = [up, down, side, other, cross] + first + second
    for dev in partners:
        pl.semaphore_signal(barrier, inc=1, device_id=dev, device_id_type=MESH)

    def local(i, src, dst):
        return pltpu.make_async_copy(src, dst, lsem.at[i])

    def remote(i, src, dst, dev):
        return pltpu.make_async_remote_copy(
            src_ref=src,
            dst_ref=dst,
            send_sem=send.at[i],
            recv_sem=recv.at[i],
            device_id=dev,
            device_id_type=MESH,
        )

    small = [
        local(0, loc, s_loc),
        local(1, pw, s_pw),
        local(2, wi, s_wi),
        local(3, pp, s_pp),
        local(4, own, s_own),
        local(5, slo, s_slo),
    ]
    for c in small:
        c.start()
    loads0 = [
        local(6, unk.at[0], F0.at[:, pl.ds(1, CX), BODY, :]),
        local(7, coe.at[0, 0], T0.at[0, pl.ds(1, CX), BODY, :]),
        local(8, coe.at[0, 3], T0.at[1, pl.ds(1, CX), BODY, :]),
        local(9, coe.at[0, pl.ds(1, 2)], KVC),
    ]
    loads1 = [local(6, unk.at[0], WG), local(7, coe.at[0], VM), local(8, rock, RK)]

    def wells():
        for c in small:
            c.wait()
        place = s_loc[...]
        row, col = lax.shift_right_logical(place, 8), jnp.bitwise_and(place, 255)
        row_mask, col_mask = hot(row, PERFS), hot(col, PERFS)
        row_hot, col_hot = as_bf16(row_mask), as_bf16(col_mask)
        live = s_pw[...] >= 0
        index = jnp.where(live, s_wi[...], 0.0)
        WD[0] = spread(row_hot, col_mask, index)
        WD[1] = spread(row_hot, col_mask, index * s_pp[...])
        well = jnp.maximum(s_pw[...], 0)
        w_row = hot(lax.shift_right_logical(well, 7), 64)
        w_col = as_bf16(hot(jnp.bitwise_and(well, 127), 128))

        def look(ref):
            found = dot_nn(ref[...].astype(F32).astype(BF16), w_col)
            return jnp.sum(jnp.where(w_row, found, 0.0), axis=0, keepdims=True).astype(jnp.int32)

        owner, slot = look(s_own), look(s_slo)
        o_gx, o_gy = lax.shift_right_logical(owner, 1), jnp.bitwise_and(owner, 1)
        order = (
            jnp.bitwise_and(o_gx, RUN - 1) * PAIRS + lax.shift_right_logical(o_gx, 4) * 2 + o_gy
        )
        return row_mask, col_hot, index, order, slot

    def rates_first(values, order, slot):
        own_mask, slot_hot = hot(order, RUN * PAIRS), as_bf16(hot(slot, 128))
        lhs = [
            jnp.where(own_mask, piece.astype(F32), 0.0).astype(BF16)
            for value in values
            for piece in split(value)
        ]
        found = dot_nt(jnp.concatenate(lhs, axis=0), slot_hot)
        size = RUN * PAIRS
        for a in range(2):
            u, v, w = (found[(3 * a + n) * size : (3 * a + n + 1) * size] for n in range(3))
            part[:, a] = (u + v + w).reshape(RUN, PAIRS, 128)
        copies = [
            remote(R_FIRST + d, part.at[lax.rem(zc + d, RUN)], got1.at[d], first[d - 1])
            for d in far_first(RUN)
        ]
        for c in copies:
            c.start()
        return copies

    def rates_second(copies):
        for c in copies:
            c.wait()
        total = part[zc]
        for d in range(1, RUN):
            total = total + got1[d]
        part2[...] = jnp.zeros_like(part2)
        for a in range(2):
            for q in range(PAIRS):
                part2[q, a : a + 1] = total[a, q : q + 1]
        copies = [
            remote(R_SECOND + d, part2.at[lax.rem(pair + d, PAIRS)], got2.at[d], second[d - 1])
            for d in range(1, PAIRS)
        ]
        for c in copies:
            c.start()
        return copies

    def rates_last(copies):
        for c in copies:
            c.wait()
        total = part2[pair]
        for d in range(1, PAIRS):
            total = total + got2[d]
        rate_buf[...] = total[0:2]
        c = local(10, rate_buf, rates.at[0])
        c.start()
        return c

    def edge(ref, f, i):
        return jnp.where(gy == 0, ref[f, i, HI - 1 : HI, :], ref[f, i, LO : LO + 1, :])

    def set_edges(ref, f, i, row, zero):
        if zero:
            ref[f, i, HI : HI + 1, :] = jnp.where(gy == 0, row, 0.0)
            ref[f, i, LO - 1 : LO, :] = jnp.where(gy == 1, row, 0.0)
        else:
            ref[f, i, HI : HI + 1, :] = row
            ref[f, i, LO - 1 : LO, :] = row

    def x_face(f, a):
        outside = jnp.logical_or(
            jnp.logical_and(gx == 0, a == 0), jnp.logical_and(gx == RING - 1, a == CX)
        )
        face = harmonic(T0[f, a, BODY, :], T0[f, a + 1, BODY, :])
        TX[f, a] = jnp.where(outside, 0.0, face)

    def y_faces(f, i):
        TY[f, i - 1, LO : HI - 1] = harmonic(T0[f, i, LO : HI - 1, :], T0[f, i, LO + 1 : HI, :])

    def y_ends(f, i):
        for r in (LO - 1, HI - 1):
            TY[f, i - 1, r : r + 1] = harmonic(T0[f, i, r : r + 1, :], T0[f, i, r + 1 : r + 2, :])

    def z_faces(f, i, value):
        lane = lax.broadcasted_iota(jnp.int32, (CY, NZ), 1)
        face = harmonic(value, pltpu.roll(value, NZ - 1, 1))
        TZ[f, i - 1] = jnp.where(lane == NZ - 1, 0.0, face)

    def system(f, i, start):
        c = KVC[1, i - 1]
        tz = TZ[f, i - 1]
        total = (
            c + TX[f, i - 1] + TX[f, i] + TY[f, i - 1, LO - 1 : HI - 1] + TY[f, i - 1, LO:HI]
            + tz + pltpu.roll(tz, 1, 1)
        )
        base = c * start[f, i, BODY, :]
        if f == 0:
            rows = pl.ds((i - 1) * CY if isinstance(i, int) else pl.multiple_of((i - 1) * CY, CY), CY)
            total = total + WD[0, rows]
            base = base + WD[1, rows]
        INV[f, i - 1] = reciprocal(total)
        BASE[f, i - 1] = base

    def sweep(f, i, now, later):
        tz = TZ[f, i - 1]
        centre = now[f, i, BODY, :]
        total = (
            BASE[f, i - 1]
            + TX[f, i - 1] * now[f, i - 1, BODY, :]
            + TX[f, i] * now[f, i + 1, BODY, :]
            + TY[f, i - 1, LO - 1 : HI - 1] * now[f, i, LO - 1 : HI - 1, :]
            + TY[f, i - 1, LO:HI] * now[f, i, LO + 1 : HI + 1, :]
            + tz * pltpu.roll(centre, NZ - 1, 1)
            + pltpu.roll(tz * centre, 1, 1)
        )
        later[f, i, BODY, :] = total * INV[f, i - 1]

    def far_first(n):
        return sorted(range(1, n), key=lambda d: -min(d, n - d))

    def x_pair(i_up, i_down, ref, both=True, f=0):
        pick_ = (lambda a: ref.at[:, a, BODY, :]) if both else (lambda a: ref.at[f, a, BODY, :])
        return [
            remote(i_up, pick_(CX), pick_(0), up),
            remote(i_down, pick_(1), pick_(CX + 1), down),
        ]

    kh_over = [
        remote(KH_OVER + i, coe.at[0, 0, i - 1], T0.at[0, i, BODY, :], other) for i in (1, CX, 2)
    ]
    kh_last = remote(KH_OVER + 3, coe.at[0, 0, 2], T0.at[0, 3, BODY, :], other)
    kh_edges = remote(K_Y, yr0.at[pl.ds(8, 8)], yr2, other)
    three = pl.ds(core, 3)
    kv_cross = remote(KV_CROSS, coe.at[0, 1, three], RL, cross)
    kv_on = remote(KV_ON, RL, KVC.at[0, three], side)
    kv_over = remote(KV_OVER, coe.at[0, 1, near_mate - 1], KVC.at[0, near_mate - 1], other)
    main_rows = pl.ds(pl.multiple_of(LO + 8 * gy, 8), CY - 8)
    edge_rows = pl.ds(pl.multiple_of(HI - 8 - (CY - 8) * gy, 8), 8)
    inner = [F2.at[f, pl.ds(others, 3), main_rows, :] for f in range(2)]
    main_over = [remote(MAIN_OVER + f, v, v, other) for f, v in enumerate(inner)]
    rest_over = []
    for f in range(2):
        views = [F2.at[f, near_far, BODY, :], F2.at[f, pl.ds(others, 3), edge_rows, :]]
        rest_over.append(
            [remote(REST_OVER + 3 * f + n, v, v, other) for n, v in enumerate(views)]
        )
    at_over = remote(AT_OVER, ats, atr, other)
    layers = range(1, CX + 1)

    @pl.when(sec == 0)
    def _():
        for c in loads0:
            c.start()
        for c in loads0:
            c.wait()
        for f in range(2):
            for i in layers:
                r = f * CX + i - 1
                ys0[r : r + 1] = edge(F0, f, i)
                ys0[r + 8 : r + 9] = edge(T0, f, i)
        pl.semaphore_wait(barrier, len(partners))
        halo_y = remote(Y_START, ys0, yr0, side)
        halo_y.start()
        halo_far_x, halo_mate_x = [], []
        for s, dev, src, dst, group in (
            (X_UP, far, near_far, halo_mate, halo_far_x),
            (X_DOWN, mate, near_mate, halo_far, halo_mate_x),
        ):
            for f in range(2):
                pair_ = [
                    remote(s + 2 * f, unk.at[0, f, src - 1], F0.at[f, dst, BODY, :], dev),
                    remote(s + 2 * f + 1, coe.at[0, 3 * f, src - 1], T0.at[f, dst, BODY, :], dev),
                ]
                for c in pair_:
                    c.start()
                group.append(pair_)
        for c in kh_over:
            c.start()
        kv_cross.start()
        for f in range(2):
            for i in layers:
                z_faces(f, i, KVC[0, i - 1] if f == 0 else T0[1, i, BODY, :])
                y_faces(f, i)
            for a in range(1, CX):
                x_face(f, a)
        row_mask, col_hot, index, order, slot = wells()
        halo_y.wait()
        kh_edges.start()
        for f in range(2):
            for i in layers:
                r = f * CX + i - 1
                set_edges(F0, f, i, yr0[r : r + 1], False)
                set_edges(T0, f, i, yr0[r + 8 : r + 9], True)
                y_ends(f, i)
                F1[f, i, HI : HI + 1, :] = jnp.zeros((1, NZ), F32)
                F1[f, i, LO - 1 : LO, :] = jnp.zeros((1, NZ), F32)
            for i in (2, 3):
                system(f, i, F0)
                sweep(f, i, F0, F1)
        for f in range(2):
            for c in halo_mate_x[f]:
                c.wait()
            x_face(f, CX * (1 - core))
            system(f, near_mate, F0)
            sweep(f, near_mate, F0, F1)
        mate_x2 = remote(X2_DOWN, F1.at[:, near_mate, BODY, :], F1.at[:, halo_far, BODY, :], mate)
        mate_x2.start()
        far_x2 = []
        for f in (0, 1):
            for c in halo_far_x[f]:
                c.wait()
            x_face(f, CX * core)
            system(f, near_far, F0)
            sweep(f, near_far, F0, F1)
            c = remote(
                X2_UP + f, F1.at[f, near_far, BODY, :], F1.at[f, halo_mate, BODY, :], far
            )
            c.start()
            far_x2.append(c)
        for f in range(2):
            for i in layers:
                r = f * CX + i - 1
                ys1[r : r + 1] = edge(F1, f, i)
        halo_y = remote(Y_SECOND, ys1, yr1, side)
        halo_y.start()
        mate_x2.wait()
        for f in (1, 0):
            for k in range(3):
                sweep(f, others + k, F1, F2)
            if f == 1:
                main_over[1].start()
                kh_last.start()
        halo_y.wait()
        for at, r, t in ((0, HI - 1, HI - 1), (1, LO, LO - 1)):

            @pl.when(gy == at)
            def _(r=r, t=t):
                for f in range(2):
                    for k in range(3):
                        i = others + k
                        n = f * CX + i - 1
                        more = TY[f, i - 1, t : t + 1] * INV[f, i - 1, r - LO : r - LO + 1]
                        row = yr1[pl.ds(n, 1)]
                        F2[f, i, r : r + 1, :] = F2[f, i, r : r + 1, :] + more * row

        for f, c in zip((0, 1), far_x2):
            set_edges(F1, f, near_far, yr1[pl.ds(f * CX + near_far - 1, 1)], False)
            c.wait()
            sweep(f, near_far, F1, F2)
        finals = [F2[f, 1 : CX + 1, BODY, :].reshape(CX * CY, NZ) for f in range(2)]
        pressure, warmth = pick(finals, row_mask, col_hot)
        ats[...] = jnp.zeros_like(ats)
        ats[0:1] = pressure
        ats[1:2] = warmth
        at_over.start()
        for c in rest_over[1] + rest_over[0]:
            c.start()
        main_over[0].start()
        save = local(11, F2.at[:, pl.ds(1, CX), BODY, :], out.at[0])
        save.start()
        q = index * (s_pp[...] - pressure)
        copies = rates_first((q, q * warmth), order, slot)
        copies = rates_second(copies)
        kv_over.start()
        last = rates_last(copies)
        for c in kh_over + main_over + [kh_last, kh_edges, kv_cross, kv_over, at_over] + rest_over[0] + rest_over[1]:
            c.wait_send()
        save.wait()
        last.wait()

    @pl.when(sec == 1)
    def _():
        for c in loads1:
            c.start()
        pl.semaphore_wait(barrier, len(partners))
        for c in loads1:
            c.wait()
        for i in range(CX):
            kind = RK[i]
            ends = []
            masks = [kind == t for t in range(1, NROCK)]
            for k in range(3):
                e = jnp.full((CY, NZ), table[k, 0], F32)
                for t in range(1, NROCK):
                    e = jnp.where(masks[t - 1], table[k, t], e)
                ends.append(e)
            water, gas = WG[0, i], WG[1, i]
            oil = 1.0 - water - gas
            MOB[0, i] = ends[0] * water * water * reciprocal(VM[1, i])
            MOB[1, i] = ends[1] * oil * oil * reciprocal(VM[2, i])
            MOB[2, i] = ends[2] * gas * gas * reciprocal(VM[3, i])
        kv_cross.wait_recv()
        kv_on.start()
        row_mask, col_hot, index, order, slot = wells()
        lw, lo, lg = pick([MOB[k].reshape(CX * CY, NZ) for k in range(3)], row_mask, col_hot)

        for c in kh_over:
            c.wait_recv()
        halo_k = x_pair(K_UP, K_DOWN, T0, False)
        for c in halo_k:
            c.start()
        for i in (1, CX, 2):
            y_faces(0, i)
        x_face(0, 1)
        kh_edges.wait_recv()
        for i in layers:
            set_edges(T0, 0, i, yr2[i - 1 : i], True)
        for i in (1, CX, 2):
            y_ends(0, i)
        kh_last.wait_recv()
        for a in (2, 3):
            x_face(0, a)
        y_faces(0, 3)
        y_ends(0, 3)
        for c in halo_k:
            c.wait()
        for a in (0, CX):
            x_face(0, a)

        at_over.wait_recv()
        q = index * (s_pp[...] - atr[0:1])
        lo = lo * jnp.exp(LINKED * (atr[1:2] - 1.0))
        scaled = q * reciprocal(lw + lo + lg)
        copies = rates_first((scaled * lw, scaled * lg), order, slot)
        for c in rest_over[1] + main_over[1:]:
            c.wait_recv()
        for i in (1, 4, 2, 3):
            other_mob = MOB[1, i - 1] * jnp.exp(LINKED * (F2[1, i, BODY, :] - 1.0))
            part_all = reciprocal(MOB[0, i - 1] + other_mob + MOB[2, i - 1])
            SH[0, i, BODY, :] = MOB[0, i - 1] * part_all
            SH[1, i, BODY, :] = MOB[2, i - 1] * part_all
        halo_s = x_pair(S_UP, S_DOWN, SH)
        for c in halo_s:
            c.start()
        for i in layers:
            ys3[i - 1 : i] = edge(SH, 0, i)
            ys3[i + 3 : i + 4] = edge(SH, 1, i)
        halo_sy = remote(S_Y, ys3, yr3, side)
        halo_sy.start()
        for c in rest_over[0]:
            c.wait_recv()
        far_p = remote(
            P_UP, F2.at[0, near_far, BODY, :], F2.at[0, halo_mate, BODY, :], far
        )
        far_p.start()
        ys4[...] = jnp.zeros_like(ys4)
        for at, r in ((0, HI - 1), (1, LO)):

            @pl.when(gy == at)
            def _(r=r):
                for i in layers:
                    ys4[i - 1 : i] = F2[0, i, r : r + 1, :]

        halo_py = remote(P_Y, ys4, yr4, side)
        halo_py.start()
        copies = rates_second(copies)

        halo_sy.wait()
        halo_py.wait()
        for i in layers:
            set_edges(F2, 0, i, yr4[i - 1 : i], False)
            set_edges(SH, 0, i, yr3[i - 1 : i], False)
            set_edges(SH, 1, i, yr3[i + 3 : i + 4], False)
        kv_on.wait()
        for k in range(3):
            z_faces(0, core + k + 1, KVC[0, core + k])
        main_over[0].wait_recv()
        mate_p = remote(
            P_DOWN, F2.at[0, near_mate, BODY, :], F2.at[0, halo_far, BODY, :], mate
        )
        mate_p.start()
        for c in halo_s + [far_p]:
            c.wait()

        def through(flow, shares):
            pos, neg = jnp.maximum(flow, 0.0), jnp.minimum(flow, 0.0)
            return [pos * a + neg * b for a, b in shares]

        saves = []
        for k in range(CX):
            i = near_far + k * (1 - 2 * core)
            if k == CX - 1:
                kv_over.wait_recv()
                z_faces(0, i, KVC[0, i - 1])
                mate_p.wait()
            p = F2[0, i, BODY, :]
            s = [SH[a, i, BODY, :] for a in range(2)]
            tz = TZ[0, i - 1]
            west = through(
                TX[0, i - 1] * (F2[0, i - 1, BODY, :] - p),
                [(SH[a, i - 1, BODY, :], s[a]) for a in range(2)],
            )
            east = through(
                TX[0, i] * (p - F2[0, i + 1, BODY, :]),
                [(s[a], SH[a, i + 1, BODY, :]) for a in range(2)],
            )
            south = through(
                TY[0, i - 1, LO - 1 : HI - 1] * (F2[0, i, LO - 1 : HI - 1, :] - p),
                [(SH[a, i, LO - 1 : HI - 1, :], s[a]) for a in range(2)],
            )
            north = through(
                TY[0, i - 1, LO:HI] * (p - F2[0, i, LO + 1 : HI + 1, :]),
                [(s[a], SH[a, i, LO + 1 : HI + 1, :]) for a in range(2)],
            )
            top = through(
                tz * (p - pltpu.roll(p, NZ - 1, 1)),
                [(s[a], pltpu.roll(s[a], NZ - 1, 1)) for a in range(2)],
            )
            rows = pl.ds(pl.multiple_of((i - 1) * CY, CY), CY)
            rate = WD[1, rows] - WD[0, rows] * p
            inverse = reciprocal(VM[0, i - 1])
            for a in range(2):
                net = west[a] - east[a] + south[a] - north[a] + pltpu.roll(top[a], 1, 1) - top[a]
                WG[a, i - 1] = WG[a, i - 1] + (net + rate * s[a]) * inverse
            saves.append(local(11 + k, WG.at[:, i - 1], out.at[0, :, i - 1]))
            saves[-1].start()
        last = rates_last(copies)
        for c in saves + [last]:
            c.wait()


def hand_over(unknowns, sums, out, rates, held, held_sums, take, give):
    parts = [(sums.at[0], held_sums, rates.at[0], 2 * CX)]
    for f in range(2):
        parts.append((unknowns.at[0, f], held.at[f], out.at[0, f], f))
    inward = [pltpu.make_async_copy(a, b, take.at[n]) for a, b, _, n in parts]
    outward = [pltpu.make_async_copy(b, c, give.at[n]) for _, b, c, n in parts]
    for c in inward:
        c.start()
    for a, b in zip(inward, outward):
        a.wait()
        b.start()
    for c in outward:
        c.wait()


def per_device(unk, coe, rock, table, loc, pw, wi, pp, own, slo):
    any_ = pl.BlockSpec(memory_space=pl.ANY)
    row = lambda a: a.reshape(1, PERFS)
    vm = lambda *s: pltpu.VMEM(s, F32)
    halo = (2, CX + 2, CY + 16, NZ)
    unknowns, sums = pl.pallas_call(
        body,
        out_shape=(
            jax.ShapeDtypeStruct((1, 2, CX, CY, NZ), F32),
            jax.ShapeDtypeStruct((1, 2, 128), F32),
        ),
        in_specs=[any_] * 3 + [pl.BlockSpec(memory_space=pltpu.SMEM)] + [any_] * 6,
        out_specs=(any_, any_),
        scratch_shapes=[
            vm(*halo), vm(*halo), vm(*halo), vm(*halo), vm(*halo),
            vm(2, CX, CY, NZ), vm(3, CY, NZ),
            vm(2, CX, CY, NZ),
            vm(4, CX, CY, NZ),
            pltpu.VMEM((CX, CY, NZ), jnp.int32),
            vm(2, CX + 1, CY, NZ), vm(2, CX, CY + 16, NZ), vm(2, CX, CY, NZ),
            vm(2, CX, CY, NZ), vm(2, CX, CY, NZ),
            vm(2, CX * CY, NZ),
            vm(3, CX, CY, NZ),
            pltpu.VMEM((1, PERFS), jnp.int32), pltpu.VMEM((1, PERFS), jnp.int32),
            vm(1, PERFS), vm(1, PERFS),
            pltpu.VMEM((64, 128), jnp.int32), pltpu.VMEM((64, 128), jnp.int32),
            vm(16, NZ), vm(16, NZ), vm(8, NZ), vm(8, NZ), vm(8, NZ), vm(8, NZ),
            vm(8, NZ), vm(8, NZ), vm(8, NZ), vm(8, NZ),
            vm(8, PERFS), vm(8, PERFS),
            vm(RUN, 2, PAIRS, 128), vm(RUN, 2, PAIRS, 128),
            vm(PAIRS, 8, 128), vm(PAIRS, 8, 128), vm(2, 128),
            pltpu.SemaphoreType.DMA((N_SEM,)),
            pltpu.SemaphoreType.DMA((N_SEM,)),
            pltpu.SemaphoreType.DMA((N_LOCAL,)),
        ],
        compiler_params=pltpu.CompilerParams(
            collective_id=0, has_side_effects=True, vmem_limit_bytes=60 * 2**20
        ),
    )(
        unk, coe, rock, table.T, row(loc), row(pw), row(wi), row(pp),
        own.reshape(64, 128), slo.reshape(64, 128),
    )
    return pl.pallas_call(
        hand_over,
        out_shape=(
            jax.ShapeDtypeStruct(unknowns.shape, F32),
            jax.ShapeDtypeStruct(sums.shape, F32),
        ),
        in_specs=[any_, any_],
        out_specs=(any_, any_),
        scratch_shapes=[
            vm(2, CX, CY, NZ),
            vm(2, 128),
            pltpu.SemaphoreType.DMA((2 * CX + 1,)),
            pltpu.SemaphoreType.DMA((2 * CX + 1,)),
        ],
        compiler_params=pltpu.CompilerParams(vmem_limit_bytes=60 * 2**20),
    )(unknowns, sums)


def solution(mesh):
    in_specs = (
        P("sec", None, "gx", "gy", None),
        P("sec", None, "gx", "gy", None),
        P("gx", "gy", None),
        P(),
        P(("gx", "gy")),
        P(("gx", "gy")),
        P(("gx", "gy")),
        P(("gx", "gy")),
        P(),
        P(),
    )
    out_specs = (P("sec", None, "gx", "gy", None), P("sec", None, ("gx", "gy")))
    return jax.shard_map(
        per_device, mesh=mesh, in_specs=in_specs, out_specs=out_specs, check_vma=False
    )
```
